128 devices in a mesh: dp: 32 (over z, x_lo, y), ctx: 4 (over x_hi, core).
Axes of the slice: x: 4 (x_hi: 2, x_lo: 2; x = x_hi * 2 + x_lo), y: 4, z: 4, core: 2. Of those that a mesh axis runs over, the one named last changes fastest.
Arguments:
- tokens: bfloat16 [16384, 2048], P(('dp', 'ctx')), may hold values from -24 to 24
- cotangent: bfloat16 [16384, 2048], P(('dp', 'ctx')), may hold values from -6 to 6
- lengths: int32 [32, 2], P('dp'), may hold values from 1 to 448, 512 in all within a row
- span_ids: int32 [32, 8], P('dp'), may hold values from 0 to 7, each once within a row
- query_weight: float32 [2048, 2048], P(('dp', 'ctx')), may hold values from -0.125 to 0.125
- key_matrix: float32 [2048, 1024], P(('dp', 'ctx')), may hold values from -0.125 to 0.125
- value_matrix: float32 [2048, 1024], P(('dp', 'ctx')), may hold values from -0.125 to 0.125
- out_weight: float32 [2048, 2048], P(('dp', 'ctx')), may hold values from -1.5 to 1.5
- gate_weight: float32 [2048, 6144], P(('dp', 'ctx')), may hold values from -0.125 to 0.125
- up_weight: float32 [2048, 6144], P(('dp', 'ctx')), may hold values from -0.125 to 0.125
- down_weight: float32 [6144, 2048], P(('dp', 'ctx')), may hold values from -0.078125 to 0.078125
- norm_gains: float32 [4352], P(('dp', 'ctx')), may hold values from 0.5 to 1.5
- query_first: float32 [2048, 2048], P(('dp', 'ctx')), may hold values from -80 to 80
- key_first_moment: float32 [2048, 1024], P(('dp', 'ctx')), may hold values from -80 to 80
- value_first_moment: float32 [2048, 1024], P(('dp', 'ctx')), may hold values from -160 to 160
- out_first: float32 [2048, 2048], P(('dp', 'ctx')), may hold values from -6 to 6
- gate_first: float32 [2048, 6144], P(('dp', 'ctx')), may hold values from -24 to 24
- up_first: float32 [2048, 6144], P(('dp', 'ctx')), may hold values from -24 to 24
- down_first: float32 [6144, 2048], P(('dp', 'ctx')), may hold values from -48 to 48
- gains_first: float32 [4352], P(('dp', 'ctx')), may hold values from -128 to 128
- query_second: float32 [2048, 2048], P(('dp', 'ctx')), may hold values from 861.7984 to 3447.1936
- key_second_moment: float32 [2048, 1024], P(('dp', 'ctx')), may hold values from 861.7984 to 3447.1936
- value_second_moment: float32 [2048, 1024], P(('dp', 'ctx')), may hold values from 3447.1936 to 13788.774
- out_second: float32 [2048, 2048], P(('dp', 'ctx')), may hold values from 19.33312 to 77.49632
- gate_second: float32 [2048, 6144], P(('dp', 'ctx')), may hold values from 77.49632 to 309.6576
- up_second: float32 [2048, 6144], P(('dp', 'ctx')), may hold values from 77.49632 to 309.6576
- down_second: float32 [6144, 2048], P(('dp', 'ctx')), may hold values from 309.6576 to 1240.2688
- gains_second: float32 [4352], P(('dp', 'ctx')), may hold values from 1933.312 to 7749.632
Outputs:
- block_output: bfloat16 [16384, 2048], P(('dp', 'ctx'))
- input_grad: float32 [16384, 2048], P(('dp', 'ctx'))
- new_query_weight: float32 [2048, 2048], P(('dp', 'ctx'))
- new_query_first: float32 [2048, 2048], P(('dp', 'ctx'))
- new_query_second: float32 [2048, 2048], P(('dp', 'ctx'))
- new_key_weight: float32 [2048, 1024], P(('dp', 'ctx'))
- new_key_first: float32 [2048, 1024], P(('dp', 'ctx'))
- new_key_second: float32 [2048, 1024], P(('dp', 'ctx'))
- new_value_weight: float32 [2048, 1024], P(('dp', 'ctx'))
- new_value_first: float32 [2048, 1024], P(('dp', 'ctx'))
- new_value_second: float32 [2048, 1024], P(('dp', 'ctx'))
- new_out_weight: float32 [2048, 2048], P(('dp', 'ctx'))
- new_out_first: float32 [2048, 2048], P(('dp', 'ctx'))
- new_out_second: float32 [2048, 2048], P(('dp', 'ctx'))
- new_gate_weight: float32 [2048, 6144], P(('dp', 'ctx'))
- new_gate_first: float32 [2048, 6144], P(('dp', 'ctx'))
- new_gate_second: float32 [2048, 6144], P(('dp', 'ctx'))
- new_up_weight: float32 [2048, 6144], P(('dp', 'ctx'))
- new_up_first: float32 [2048, 6144], P(('dp', 'ctx'))
- new_up_second: float32 [2048, 6144], P(('dp', 'ctx'))
- new_down_weight: float32 [6144, 2048], P(('dp', 'ctx'))
- new_down_first: float32 [6144, 2048], P(('dp', 'ctx'))
- new_down_second: float32 [6144, 2048], P(('dp', 'ctx'))
- new_gains: float32 [4352], P(('dp', 'ctx'))
- new_gains_first: float32 [4352], P(('dp', 'ctx'))
- new_gains_second: float32 [4352], P(('dp', 'ctx'))
The draws below stay inside these ranges and needn't reach their ends.
Inputs may be any that keep to these rules, and one draw needn't show every extreme that they name: Row g holds the lengths of the 2 sequences of data group g, laid end to end in this order over its 512 slots; they sum to 512. `span_ids`: entry 2 c + j of row g is the block of 64 slots held by block j of device c of data group g; each row names every block once.
All inputs are finite; a program needn't handle non-finite values.
Results may differ from the reference program's by a relative error of at most 0.02.
Values may be sent and summed in bfloat16 or wider, within the bound.
No kernel may reach another device: no remote copies, remote signals or barrier semaphores. Data moves between devices by JAX's collectives and lax.ppermute only.
A program may use at most 512 MiB of HBM per device.

```python
import math
import jax
import jax.numpy as jnp
import numpy as np
from jax import lax

MODEL_WIDTH = 2048
QUERY_HEADS = 16
KEY_VALUE_HEADS = 8
HEAD_SIZE = 128
FF = 6144
TOK_DEV = 128
SEQS = 2
STEP = 10
TOKEN_COUNT = 16384
GAINS = 4352
N_DP = 32
N_CTX = 4


def spiked(values, key, source, target, shards_of, factor):
    def block_of(dim):
        return (jnp.arange(values.shape[dim]) // (values.shape[dim] // shards_of)).reshape((-1,) + (1,) * (values.ndim - 1 - dim))

    one_side = jax.random.permutation(key, shards_of)[block_of(target)]
    other_side = (block_of(target) + shards_of // 2) % shards_of
    return jnp.where((block_of(source) == one_side) | (block_of(source) == other_side), factor * values, values)


def block_levels(stream_key, extent, pieces, least, largest):
    level, own = 1.0, jax.random.fold_in(stream_key, 6)
    for axis_at, shards_of in pieces:
        heights = jnp.exp(jax.random.uniform(jax.random.fold_in(own, axis_at), (shards_of,), jnp.float32, least / len(pieces), largest / len(pieces)))
        level = level * jnp.repeat(heights, extent[axis_at] // shards_of).reshape([-1 if axis == axis_at else 1 for axis in range(len(extent))])
    return level


def profile(amount, total, reach, lean):
    loads = [(1 << 20) // math.isqrt(rank ** lean) + 1 for rank in range(2, amount + 1)]
    surplus, counts = total - reach - (amount - 1), [1] * (amount - 1)
    while surplus > 0:
        free = [i for i in range(amount - 1) if counts[i] < reach]
        whole, left = sum([loads[i] for i in free]), surplus
        for i in free:
            addition = min(reach - counts[i], max(1, left * loads[i] // whole), surplus)
            counts[i] = counts[i] + addition
            surplus = surplus - addition
    return np.array([reach] + counts)


def ragged_sizes(stream_key, amount, total, limit, skew):
    if amount == 2:
        one = jax.random.randint(stream_key, (), max(1, total - limit), min(limit, total - 1) + 1)
        return jnp.stack([one, total - one])
    sizes = jnp.asarray(profile(amount, total, limit, skew), jnp.int32)
    pairs = (amount - 1) // 2
    source_of, sink = sizes[1:1 + 2 * pairs:2], sizes[2:2 + 2 * pairs:2]
    room = jnp.minimum(source_of - 1, limit - sink)
    moved = jax.random.randint(jax.random.fold_in(stream_key, 1), (pairs,), 0, 1 << 20) % (room + 1)
    sizes = sizes.at[1:1 + 2 * pairs:2].set(source_of - moved).at[2:2 + 2 * pairs:2].set(sink + moved)
    return sizes[jax.random.permutation(jax.random.fold_in(stream_key, 2), amount)]


def centred(key, shape, spread, reach, shards=(), held_as=jnp.bfloat16):
    factor_of = block_levels(key, shape, shards, -0.22, 0.18) if shards else 1.0
    values = jax.random.normal(key, shape, jnp.float32) * spread * factor_of
    return jnp.minimum(jnp.maximum(values, -reach), reach).astype(held_as)


def heavy_noise(stream_key, dims, scale, most, pieces, heavy, kind=jnp.bfloat16):
    drawn = scale * jax.random.normal(stream_key, dims, jnp.float32)
    if pieces:
        drawn = drawn * block_levels(stream_key, dims, pieces, -0.22, 0.18)
    return jnp.clip(spiked(drawn, jax.random.fold_in(stream_key, 3), *heavy), -most, most).astype(kind)


def setup_inputs(seed: int = 0) -> dict:
    seeds = jax.random.split(jax.random.key(seed), 29)
    return {
        "tokens": heavy_noise(seeds[0], (TOKEN_COUNT, MODEL_WIDTH), 1.0, 24.0, ((0, 128),), (0, 1, 128, 5.5)),
        "cotangent": centred(seeds[1], (TOKEN_COUNT, MODEL_WIDTH), 1.0, 6.0, ((0, 128),)),
        "lengths": jax.vmap(lambda own: ragged_sizes(own, SEQS, TOK_DEV * N_CTX, TOK_DEV * N_CTX - TOK_DEV * N_CTX // 8, 2))(jax.random.split(seeds[2], N_DP)).reshape((N_DP, SEQS)).astype(jnp.int32),
        "span_ids": jax.vmap(lambda own: jax.random.permutation(own, 2 * N_CTX))(jax.random.split(seeds[3], N_DP)).reshape((N_DP, 2 * N_CTX)).astype(jnp.int32),
        "query_weight": centred(seeds[4], (MODEL_WIDTH, QUERY_HEADS * HEAD_SIZE), MODEL_WIDTH ** -0.5, 0.125, ((0, 128),), jnp.float32),
        "key_matrix": centred(seeds[5], (MODEL_WIDTH, KEY_VALUE_HEADS * HEAD_SIZE), MODEL_WIDTH ** -0.5, 0.125, ((0, 128),), jnp.float32),
        "value_matrix": centred(seeds[6], (MODEL_WIDTH, KEY_VALUE_HEADS * HEAD_SIZE), MODEL_WIDTH ** -0.5, 0.125, ((0, 128),), jnp.float32),
        "out_weight": centred(seeds[7], (QUERY_HEADS * HEAD_SIZE, MODEL_WIDTH), (QUERY_HEADS * HEAD_SIZE // TOK_DEV) ** -0.5, 1.5, ((0, 128),), jnp.float32),
        "gate_weight": centred(seeds[8], (MODEL_WIDTH, FF), MODEL_WIDTH ** -0.5, 0.125, ((0, 128),), jnp.float32),
        "up_weight": centred(seeds[9], (MODEL_WIDTH, FF), MODEL_WIDTH ** -0.5, 0.125, ((0, 128),), jnp.float32),
        "down_weight": centred(seeds[10], (FF, MODEL_WIDTH), FF ** -0.5, 0.078125, ((0, 128),), jnp.float32),
        "norm_gains": jnp.clip(1.0 + 0.1 * jax.random.normal(seeds[11], (GAINS,), jnp.float32), 0.5, 1.5),
        "query_first": centred(seeds[12], (MODEL_WIDTH, QUERY_HEADS * HEAD_SIZE), (0.111 * TOKEN_COUNT ** 0.5), 80.0, ((0, 128),), jnp.float32),
        "key_first_moment": centred(seeds[13], (MODEL_WIDTH, KEY_VALUE_HEADS * HEAD_SIZE), (0.111 * TOKEN_COUNT ** 0.5), 80.0, ((0, 128),), jnp.float32),
        "value_first_moment": centred(seeds[14], (MODEL_WIDTH, KEY_VALUE_HEADS * HEAD_SIZE), (0.222 * TOKEN_COUNT ** 0.5), 160.0, ((0, 128),), jnp.float32),
        "out_first": centred(seeds[15], (QUERY_HEADS * HEAD_SIZE, MODEL_WIDTH), (0.0167 * TOKEN_COUNT ** 0.5), 6.0, ((0, 128),), jnp.float32),
        "gate_first": centred(seeds[16], (MODEL_WIDTH, FF), (0.0333 * TOKEN_COUNT ** 0.5), 24.0, ((0, 128),), jnp.float32),
        "up_first": centred(seeds[17], (MODEL_WIDTH, FF), (0.0333 * TOKEN_COUNT ** 0.5), 24.0, ((0, 128),), jnp.float32),
        "down_first": centred(seeds[18], (FF, MODEL_WIDTH), (0.0667 * TOKEN_COUNT ** 0.5), 48.0, ((0, 128),), jnp.float32),
        "gains_first": centred(seeds[19], (GAINS,), (0.167 * TOKEN_COUNT ** 0.5), 128.0, ((0, 128),), jnp.float32),
        "query_second": jnp.clip(jnp.exp(math.log(3447.1936) - 1.3862944 * jax.random.uniform(seeds[20], (MODEL_WIDTH, QUERY_HEADS * HEAD_SIZE), jnp.float32) ** block_levels(seeds[20], (MODEL_WIDTH, QUERY_HEADS * HEAD_SIZE), ((0, 128),), -0.2, 0.2)), 861.7984, 3447.1936),
        "key_second_moment": jnp.clip(jnp.exp(math.log(3447.1936) - 1.3862944 * jax.random.uniform(seeds[21], (MODEL_WIDTH, KEY_VALUE_HEADS * HEAD_SIZE), jnp.float32) ** block_levels(seeds[21], (MODEL_WIDTH, KEY_VALUE_HEADS * HEAD_SIZE), ((0, 128),), -0.2, 0.2)), 861.7984, 3447.1936),
        "value_second_moment": jnp.clip(jnp.exp(math.log(13788.774) - 1.3862944 * jax.random.uniform(seeds[22], (MODEL_WIDTH, KEY_VALUE_HEADS * HEAD_SIZE), jnp.float32) ** block_levels(seeds[22], (MODEL_WIDTH, KEY_VALUE_HEADS * HEAD_SIZE), ((0, 128),), -0.2, 0.2)), 3447.1936, 13788.774),
        "out_second": jnp.clip(jnp.exp(math.log(77.49632) - 1.3884108 * jax.random.uniform(seeds[23], (QUERY_HEADS * HEAD_SIZE, MODEL_WIDTH), jnp.float32) ** block_levels(seeds[23], (QUERY_HEADS * HEAD_SIZE, MODEL_WIDTH), ((0, 128),), -0.2, 0.2)), 19.33312, 77.49632),
        "gate_second": jnp.clip(jnp.exp(math.log(309.6576) - 1.38523666 * jax.random.uniform(seeds[24], (MODEL_WIDTH, FF), jnp.float32) ** block_levels(seeds[24], (MODEL_WIDTH, FF), ((0, 128),), -0.2, 0.2)), 77.49632, 309.6576),
        "up_second": jnp.clip(jnp.exp(math.log(309.6576) - 1.38523666 * jax.random.uniform(seeds[25], (MODEL_WIDTH, FF), jnp.float32) ** block_levels(seeds[25], (MODEL_WIDTH, FF), ((0, 128),), -0.2, 0.2)), 77.49632, 309.6576),
        "down_second": jnp.clip(jnp.exp(math.log(1240.2688) - 1.3876163 * jax.random.uniform(seeds[26], (FF, MODEL_WIDTH), jnp.float32) ** block_levels(seeds[26], (FF, MODEL_WIDTH), ((0, 128),), -0.2, 0.2)), 309.6576, 1240.2688),
        "gains_second": jnp.clip(jnp.exp(math.log(7749.632) - 1.3884107 * jax.random.uniform(seeds[27], (GAINS,), jnp.float32) ** block_levels(seeds[27], (GAINS,), ((0, 128),), -0.2, 0.2)), 1933.312, 7749.632),
    }


EPS = 1e-06
THETA = 1000000.0
BETA_ONE = 0.9
BETA_TWO = 0.95
ADAM_EPS = 1e-08
DECAY = 0.1
HIGH = lax.Precision.HIGHEST

@jax.custom_vjp
def reduced_precision(v):
    return lax.optimization_barrier(v.astype(jnp.bfloat16)).astype(jnp.float32)

@jax.custom_vjp
def low_back(v):
    return v

def low_keep(v):
    return (reduced_precision(v), None)

def low_pass(kept, grad):
    return (grad,)

def back_keep(v):
    return (v, None)

def back_low(kept, grad):
    return (reduced_precision(grad),)
reduced_precision.defvjp(low_keep, low_pass)
low_back.defvjp(back_keep, back_low)

def root_mean_scale(value_vectors, gain):
    return value_vectors * lax.rsqrt(lax.optimization_barrier(jnp.mean(value_vectors * value_vectors, axis=-1, keepdims=True)) + EPS) * gain

def apply_rotation(vector, cosine_table, sine_table):
    half = vector.shape[-1] // 2
    first = vector[..., :half]
    second = vector[..., half:]
    return jnp.concatenate([first * cosine_table - second * sine_table, second * cosine_table + first * sine_table], axis=-1)

def layout(lengths_row, span_row, span):
    offsets = jnp.arange(span, dtype=jnp.int32)
    slots = (span_row[:, None].astype(jnp.int32) * span + offsets[None, :]).reshape(-1).astype(jnp.int32)
    ends = jnp.cumsum(lengths_row).astype(jnp.int32)
    passed = slots[:, None] >= ends[None, :]
    sequence = lax.optimization_barrier(jnp.sum(passed.astype(jnp.int32), axis=1)).astype(jnp.int32)
    position = (slots - lax.optimization_barrier(jnp.sum(jnp.where(passed, lengths_row[None, :], 0), axis=1))).astype(jnp.int32)
    return (slots, sequence, position)

def group_forward(x_rows, lengths_row, span_row, weights):
    wq, wk, wv, wo, wg, wu, wd, gain_one, gain_two, gain_query, key_norm_gain = weights
    token_tally = x_rows.shape[0]
    span = token_tally // span_row.shape[0]
    slots, sequence, position = layout(lengths_row, span_row, span)
    normalized_input = reduced_precision(root_mean_scale(x_rows, gain_one))
    q_lin = low_back(jnp.dot(normalized_input, wq, precision=HIGH))
    key_linear = low_back(jnp.dot(normalized_input, wk, precision=HIGH))
    gathered_values = low_back(reduced_precision(jnp.dot(normalized_input, wv, precision=HIGH)))
    half = HEAD_SIZE // 2
    freq = THETA ** (-(2.0 * jnp.arange(half, dtype=jnp.float32)) / HEAD_SIZE)
    angle = position.astype(jnp.float32)[:, None] * freq[None, :]
    cosine_table = jnp.cos(angle)[:, None, :]
    sine_table = jnp.sin(angle)[:, None, :]
    query_rotated = reduced_precision(apply_rotation(root_mean_scale(q_lin.reshape(token_tally, QUERY_HEADS, HEAD_SIZE), gain_query), cosine_table, sine_table))
    key_rotated = reduced_precision(apply_rotation(root_mean_scale(key_linear.reshape(token_tally, KEY_VALUE_HEADS, HEAD_SIZE), key_norm_gain), cosine_table, sine_table))
    value_vectors = gathered_values.reshape(token_tally, KEY_VALUE_HEADS, HEAD_SIZE)
    query_grouped = query_rotated.reshape(token_tally, KEY_VALUE_HEADS, QUERY_HEADS // KEY_VALUE_HEADS, HEAD_SIZE)
    scores = low_back(jnp.einsum('qgrd,kgd->grqk', query_grouped, key_rotated, precision=HIGH) * HEAD_SIZE ** (-0.5))
    allowed = (sequence[:, None] == sequence[None, :]) & (slots[None, :] <= slots[:, None])
    scores = jnp.where(allowed[None, None], scores, -1e+30)
    top = lax.optimization_barrier(jnp.max(scores, axis=-1, keepdims=True))
    expo = jnp.exp(scores - top)
    probs = expo / lax.optimization_barrier(jnp.sum(expo, axis=-1, keepdims=True))
    mixed = jnp.einsum('grqk,kgd->qgrd', reduced_precision(probs), value_vectors, precision=HIGH).reshape(token_tally, QUERY_HEADS * HEAD_SIZE)
    mixed = low_back(reduced_precision(mixed))
    hidden_two = x_rows + low_back(jnp.dot(mixed, wo, precision=HIGH))
    normed_two = reduced_precision(root_mean_scale(hidden_two, gain_two))
    gate = low_back(jnp.dot(normed_two, wg, precision=HIGH))
    upward = low_back(jnp.dot(normed_two, wu, precision=HIGH))
    hidden = reduced_precision(jax.nn.silu(gate) * upward)
    return hidden_two + low_back(jnp.dot(hidden, wd, precision=HIGH))

def forward(x_all, params, lengths, span_ids):
    wq, wk, wv, wo, wg, wu, wd, gains = params
    rounded = tuple((reduced_precision(weight) for weight in (wq, wk, wv, wo, wg, wu, wd)))
    gains_low = reduced_precision(gains)
    weights = rounded + (gains_low[:MODEL_WIDTH], gains_low[MODEL_WIDTH:2 * MODEL_WIDTH], gains_low[2 * MODEL_WIDTH:2 * MODEL_WIDTH + HEAD_SIZE], gains_low[2 * MODEL_WIDTH + HEAD_SIZE:])
    groups = x_all.reshape(N_DP, -1, MODEL_WIDTH)

    def one_group(item):
        return group_forward(item[0], item[1], item[2], weights)
    result = lax.map(jax.checkpoint(one_group), (groups, lengths, span_ids))
    return result.reshape(x_all.shape)

def adam(weight, grad, first, second, rate, decay):
    first_new = BETA_ONE * first + (1.0 - BETA_ONE) * grad
    second_new = BETA_TWO * second + (1.0 - BETA_TWO) * grad * grad
    first_hat = first_new / (1.0 - BETA_ONE ** STEP)
    second_hat = second_new / (1.0 - BETA_TWO ** STEP)
    weight_new = weight - rate * (first_hat / (jnp.sqrt(second_hat) + ADAM_EPS) + decay * weight)
    return (weight_new, first_new, second_new)

def reference(tokens, cotangent, lengths, span_ids, query_weight, key_matrix, value_matrix, out_weight, gate_weight, up_weight, down_weight, norm_gains, query_first, key_first_moment, value_first_moment, out_first, gate_first, up_first, down_first, gains_first, query_second, key_second_moment, value_second_moment, out_second, gate_second, up_second, down_second, gains_second):
    params = (query_weight, key_matrix, value_matrix, out_weight, gate_weight, up_weight, down_weight, norm_gains)
    x_all = tokens.astype(jnp.float32)

    def run(xs, ps):
        return forward(xs, ps, lengths, span_ids)
    output, pull = jax.vjp(run, x_all, params)
    input_grad, grads = pull(cotangent.astype(jnp.float32))
    firsts = (query_first, key_first_moment, value_first_moment, out_first, gate_first, up_first, down_first, gains_first)
    seconds = (query_second, key_second_moment, value_second_moment, out_second, gate_second, up_second, down_second, gains_second)
    rates = (MODEL_WIDTH ** (-0.5), MODEL_WIDTH ** (-0.5), MODEL_WIDTH ** (-0.5), (TOK_DEV / (QUERY_HEADS * HEAD_SIZE)) ** 0.5, MODEL_WIDTH ** (-0.5), MODEL_WIDTH ** (-0.5), FF ** (-0.5), 0.5)
    decays = (DECAY, DECAY, DECAY, DECAY, DECAY, DECAY, DECAY, 0.0)
    res = [adam(params[i], grads[i], firsts[i], seconds[i], rates[i], decays[i]) for i in range(8)]
    return (output.astype(jnp.bfloat16), input_grad, res[0][0], res[0][1], res[0][2], res[1][0], res[1][1], res[1][2], res[2][0], res[2][1], res[2][2], res[3][0], res[3][1], res[3][2], res[4][0], res[4][1], res[4][2], res[5][0], res[5][1], res[5][2], res[6][0], res[6][1], res[6][2], res[7][0], res[7][1], res[7][2])
```

```python
import jax
import jax.numpy as jnp
from jax import lax
from jax.sharding import Mesh
from jax.sharding import PartitionSpec as P

MODEL_WIDTH = 2048
QUERY_HEADS = 16
KEY_VALUE_HEADS = 8
HEAD_SIZE = 128
FF = 6144
TOK_DEV = 128
STEP = 10

EPS = 1e-06
THETA = 1000000.0
BETA_ONE = 0.9
BETA_TWO = 0.95
ADAM_EPS = 1e-08
DECAY = 0.1

AXES = ("z", "xl", "y", "xh", "c")
SIZES = (4, 2, 4, 2, 2)
RING = ("xl", "xh", "c")
PLANE = ("z", "y")
CHIPS = ("xl", "xh")
SHARE = 8
OFFSETS = (0, 2, 1, 3)
BF = jnp.bfloat16
F32 = jnp.float32


def chip_number(x):
    return (x % 2) * 2 + x // 2


def from_chip(value, offset):
    pairs = [(chip_number((x + offset) % 4), chip_number(x)) for x in range(4)]
    return lax.ppermute(value, CHIPS, pairs)


def from_core(value):
    return lax.ppermute(value, "c", [(0, 1), (1, 0)])


def row_route():
    pairs = []
    for z in range(4):
        for xl in range(2):
            for y in range(4):
                for xh in range(2):
                    for c in range(2):
                        own = (((z * 2 + xl) * 4 + y) * 2 + xh) * 2 + c
                        part = 2 * z + xl
                        to = (((y * 2 + part // 4) * 4 + (xh * 2 + c)) * 2 + (part // 2) % 2) * 2 + part % 2
                        pairs.append((own, to))
    return pairs


def gather_rows(block):
    near = {0: block}
    for offset in OFFSETS[1:]:
        near[offset] = from_chip(block, offset)
    far = {offset: from_core(near[offset]) for offset in OFFSETS}
    return jnp.concatenate([near[o] for o in OFFSETS] + [far[o] for o in OFFSETS], axis=0)


def scatter_rows(near, far):
    rows = near.shape[0] // 4
    arrived = from_core(far.astype(BF))
    both = near + arrived.astype(F32)
    total = both[:rows]
    for index in range(1, 4):
        piece = both[index * rows : (index + 1) * rows].astype(BF)
        total = total + from_chip(piece, -OFFSETS[index]).astype(F32)
    return total


def inverse_rms(values):
    return lax.rsqrt(jnp.mean(values * values, axis=-1, keepdims=True) + EPS)


def rms(values, gain):
    return values * inverse_rms(values) * gain


def norm_back(values, gain, grad):
    scale = inverse_rms(values)
    normalized = values * scale
    inner = grad * gain
    back = scale * inner - normalized * scale * jnp.mean(inner * normalized, axis=-1, keepdims=True)
    return back, grad * normalized


def rotate(vector, cosine, sine):
    half = vector.shape[-1] // 2
    first = vector[..., :half]
    second = vector[..., half:]
    return jnp.concatenate([first * cosine - second * sine, second * cosine + first * sine], axis=-1)


def dot(left, right):
    return jnp.dot(left, right, preferred_element_type=F32)


def dot_last(left, right):
    return lax.dot_general(left, right, (((1,), (1,)), ((), ())), preferred_element_type=F32)


def dot_first(left, right):
    return lax.dot_general(left, right, (((0,), (0,)), ((), ())), preferred_element_type=F32)


def adam(weight, grad, first, second, rate, decay):
    first_new = BETA_ONE * first + (1.0 - BETA_ONE) * grad
    second_new = BETA_TWO * second + (1.0 - BETA_TWO) * grad * grad
    first_hat = first_new / (1.0 - BETA_ONE**STEP)
    second_hat = second_new / (1.0 - BETA_TWO**STEP)
    weight_new = weight - rate * (first_hat / (jnp.sqrt(second_hat) + ADAM_EPS) + decay * weight)
    return (weight_new, first_new, second_new)


def pieces(value, width):
    rows, columns = value.shape
    return value.reshape(rows, columns // width, width).transpose(1, 0, 2).reshape(-1, width)


def join(value, count):
    lead, width = value.shape[:-2], value.shape[-1]
    value = value.reshape(lead + (count, -1, width))
    return jnp.swapaxes(value, -3, -2).reshape(lead + (-1, count * width))


def plane_to_rows(value):
    width = value.shape[-1]
    value = value.reshape(4, 4, 2, -1, width)
    return value.transpose(0, 2, 1, 3, 4).reshape(-1, width)


def rows_to_plane(value):
    width = value.shape[-1]
    value = value.reshape(4, 2, 4, -1, width)
    return value.transpose(0, 2, 1, 3, 4).reshape(16, -1, width)


def group_first(value):
    tail = value.shape[1:]
    value = value.reshape((2, 2, -1) + tail)
    return jnp.swapaxes(value, 0, 1).reshape((2, -1) + tail)


def rows_first(value):
    tail = value.shape[2:]
    value = value.reshape((2, 2, -1) + tail)
    return jnp.swapaxes(value, 0, 1).reshape((-1,) + tail)


def layout(lengths, span_ids):
    span = TOK_DEV // 2
    table = jnp.concatenate([lengths[0], span_ids[0]])
    other = lax.ppermute(table, "xl", [(0, 1), (1, 0)])
    both = jnp.stack([table, other])
    sizes, spans = both[:, :2], both[:, 2:]
    chip = lax.axis_index("xh") * 2 + lax.axis_index("xl")
    core = lax.axis_index("c")
    offset = jnp.arange(2)[:, None, None] + 2 * jnp.arange(2)[None, None, :]
    place = ((chip + offset) % 4) // 2 * 2 + (core + jnp.arange(2)[None, :, None]) % 2
    block = (2 * place[..., None] + jnp.arange(2)).reshape(2, 8)
    owner = jnp.sum(jnp.where(block[:, :, None] == jnp.arange(8), spans[:, None, :], 0), axis=-1)
    slots = (owner[:, :, None] * span + jnp.arange(span)).reshape(2, -1)
    ends = jnp.cumsum(sizes, axis=1)
    passed = slots[:, :, None] >= ends[:, None, :]
    sequence = jnp.sum(passed.astype(jnp.int32), axis=-1)
    position = slots - jnp.sum(jnp.where(passed, sizes[:, None, :], 0), axis=-1)
    return slots, sequence, position


def local(
    tokens,
    cotangent,
    lengths,
    span_ids,
    query_weight,
    key_matrix,
    value_matrix,
    out_weight,
    gate_weight,
    up_weight,
    down_weight,
    norm_gains,
    query_first,
    key_first_moment,
    value_first_moment,
    out_first,
    gate_first,
    up_first,
    down_first,
    gains_first,
    query_second,
    key_second_moment,
    value_second_moment,
    out_second,
    gate_second,
    up_second,
    down_second,
    gains_second,
):
    width = MODEL_WIDTH
    heads = QUERY_HEADS // SHARE
    query_cols = heads * HEAD_SIZE
    cell = query_cols + 2 * HEAD_SIZE
    hidden_cols = FF // SHARE
    row = query_weight.shape[0]
    gain_row = norm_gains.shape[0]
    half_rows = 4 * TOK_DEV
    scale = HEAD_SIZE ** (-0.5)

    def by_share(weight):
        return weight.astype(BF).reshape(row, SHARE, -1).transpose(1, 0, 2)

    head_low = jnp.concatenate([by_share(query_weight), by_share(key_matrix), by_share(value_matrix)], axis=2)
    mlp_low = jnp.concatenate([by_share(gate_weight), by_share(up_weight)], axis=2)
    gains_low = jnp.zeros((SHARE, row, HEAD_SIZE), BF).at[:, 0, :gain_row].set(norm_gains.astype(BF)[None])
    columns = lax.all_to_all(
        jnp.concatenate([head_low, mlp_low, gains_low], axis=2), RING, 0, 0, tiled=True
    )
    lines = lax.ppermute(
        jnp.concatenate([out_weight.astype(BF), down_weight.astype(BF)], axis=0), AXES, row_route()
    )
    out_lines, down_lines = lines[:row], lines[row:]
    mlp_end = cell + 2 * hidden_cols
    head_block = columns[:, :, :cell].reshape(SHARE * row, cell)
    mlp_block = columns[:, :, cell:mlp_end].reshape(SHARE * row, 2 * hidden_cols)
    gain_block = jnp.zeros((row, cell), BF).at[0, : SHARE * gain_row].set(
        columns[:, 0, mlp_end : mlp_end + gain_row].reshape(-1)
    )
    early = lax.all_gather(
        jnp.concatenate([head_block, pieces(out_lines, cell), gain_block], axis=0), PLANE, axis=0
    )
    late_block = jnp.concatenate([pieces(mlp_block, cell), pieces(down_lines, cell)], axis=0)
    late_block, early = lax.optimization_barrier((late_block, early))
    late = lax.all_gather(late_block, PLANE, axis=0)

    inputs = gather_rows(tokens)
    upstream = gather_rows(cotangent)

    out_parts = width // cell
    mlp_parts = 2 * hidden_cols // cell
    head_end = SHARE * row
    out_end = head_end + out_parts * row
    head_weight = plane_to_rows(early[:, :head_end])
    out_slice = join(early[:, head_end:out_end], out_parts).reshape(-1, width)
    gains = early[:, out_end, : SHARE * gain_row].astype(F32)
    gains = gains.reshape(4, 4, 2, -1).transpose(0, 2, 1, 3).reshape(-1)
    gain_one = gains[:width]
    gain_two = gains[width : 2 * width]
    gain_query = gains[2 * width : 2 * width + HEAD_SIZE]
    gain_key = gains[2 * width + HEAD_SIZE :]
    mlp_height = mlp_parts * SHARE * row
    mlp_weight = plane_to_rows(join(late[:, :mlp_height], mlp_parts))
    down_slice = join(late[:, mlp_height:], out_parts).reshape(-1, width)

    slots, sequence, position = layout(lengths, span_ids)
    half = HEAD_SIZE // 2
    freq = THETA ** (-(2.0 * jnp.arange(half, dtype=F32)) / HEAD_SIZE)
    angle = position.astype(F32)[:, :, None] * freq
    cosine = jnp.cos(angle)[:, :, None, :]
    sine = jnp.sin(angle)[:, :, None, :]
    allowed = (sequence[:, :, None] == sequence[:, None, :]) & (slots[:, None, :] <= slots[:, :, None])

    inputs_wide = inputs.astype(F32)
    normed_one = rms(inputs_wide, gain_one).astype(BF)
    linear = dot(normed_one, head_weight)
    query_linear = group_first(linear[:, :query_cols]).reshape(2, -1, heads, HEAD_SIZE)
    key_linear = group_first(linear[:, query_cols : query_cols + HEAD_SIZE])[:, :, None, :]
    values = group_first(linear[:, query_cols + HEAD_SIZE :].astype(BF))
    query_rotated = rotate(rms(query_linear, gain_query), cosine, sine).astype(BF)
    key_rotated = rotate(rms(key_linear, gain_key), cosine, sine).astype(BF)[:, :, 0]
    scores = jnp.einsum("gqrd,gkd->grqk", query_rotated, key_rotated, preferred_element_type=F32) * scale
    scores = jnp.where(allowed[:, None], scores, -1e30)
    top = jnp.max(scores, axis=-1, keepdims=True)
    expo = jnp.exp(scores - top)
    probs = expo / jnp.sum(expo, axis=-1, keepdims=True)
    probs_low = probs.astype(BF)
    mixed = rows_first(
        jnp.einsum("grqk,gkd->gqrd", probs_low, values, preferred_element_type=F32).astype(BF)
    ).reshape(-1, query_cols)
    branch = scatter_rows(dot(mixed[:half_rows], out_slice), dot(mixed[half_rows:], out_slice))
    hidden_two = tokens.astype(F32) + branch
    normed_two = gather_rows(rms(hidden_two, gain_two).astype(BF))
    both = dot(normed_two, mlp_weight)
    gate, up = both[:, :hidden_cols], both[:, hidden_cols:]
    sigma = jax.nn.sigmoid(gate)
    active = gate * sigma
    hidden = (active * up).astype(BF)

    grad_hidden = dot_last(upstream, down_slice)
    grad_gate = (grad_hidden * up * sigma * (1.0 + gate * (1.0 - sigma))).astype(BF)
    grad_up = (grad_hidden * active).astype(BF)
    grad_both = jnp.concatenate([grad_gate, grad_up], axis=1)
    grad_normed_two = scatter_rows(
        dot_last(grad_both[:half_rows], mlp_weight), dot_last(grad_both[half_rows:], mlp_weight)
    )
    down_grad = dot_first(hidden, upstream).astype(BF)
    mlp_grad = dot_first(normed_two, grad_both).astype(BF)
    down_grad = down_grad.reshape(16, -1, width)
    mlp_grad = rows_to_plane(mlp_grad)
    late_grad = lax.psum_scatter(
        jnp.concatenate([split_join(mlp_grad, cell), split_join(down_grad, cell)], axis=1).reshape(-1, cell),
        PLANE,
        scatter_dimension=0,
        tiled=True,
    )
    back_two, gain_two_terms = norm_back(hidden_two, gain_two, grad_normed_two)
    grad_hidden_two = cotangent.astype(F32) + back_two
    grad_branch = gather_rows(grad_hidden_two.astype(BF))

    grad_mixed = group_first(dot_last(grad_branch, out_slice).astype(BF)).reshape(2, -1, heads, HEAD_SIZE)
    out_grad = dot_first(mixed, grad_branch).astype(BF)
    grad_prob = jnp.einsum("gqrd,gkd->grqk", grad_mixed, values, preferred_element_type=F32)
    inner = jnp.sum(probs * grad_prob, axis=-1, keepdims=True)
    grad_score = (probs * (grad_prob - inner)).astype(BF)
    grad_query_rotated = (
        jnp.einsum("grqk,gkd->gqrd", grad_score, key_rotated, preferred_element_type=F32) * scale
    )
    grad_key_rotated = (
        jnp.einsum("grqk,gqrd->gkd", grad_score, query_rotated, preferred_element_type=F32) * scale
    )
    grad_values = jnp.einsum("grqk,gqrd->gkd", probs_low, grad_mixed, preferred_element_type=F32)
    back_query, query_terms = norm_back(query_linear, gain_query, rotate(grad_query_rotated, cosine, -sine))
    back_key, key_terms = norm_back(
        key_linear, gain_key, rotate(grad_key_rotated[:, :, None, :], cosine, -sine)
    )
    grad_heads = rows_first(
        jnp.concatenate(
            [
                back_query.reshape(2, -1, query_cols).astype(BF),
                back_key[:, :, 0].astype(BF),
                grad_values.astype(BF),
            ],
            axis=-1,
        )
    )
    grad_normed_near = dot_last(grad_heads[:half_rows], head_weight)
    grad_normed_far = dot_last(grad_heads[half_rows:], head_weight)
    grad_normed = scatter_rows(grad_normed_near, grad_normed_far)
    normalized = inputs_wide * inverse_rms(inputs_wide)
    gain_one_grad = jnp.sum(grad_normed_near * normalized[:half_rows], axis=0) + jnp.sum(
        grad_normed_far * normalized[half_rows:], axis=0
    )
    back_one, _ = norm_back(tokens.astype(F32), gain_one, grad_normed)
    input_grad = grad_hidden_two + back_one

    gain_terms = jnp.concatenate(
        [
            gain_one_grad,
            jnp.sum(gain_two_terms, axis=0),
            jnp.sum(query_terms, axis=(0, 1, 2)),
            jnp.sum(key_terms, axis=(0, 1, 2)),
        ]
    )
    gain_terms = gain_terms.reshape(4, 2, 4, -1).transpose(0, 2, 1, 3).reshape(16, SHARE * gain_row)
    gain_rows = jnp.zeros((16, row, cell), BF).at[:, 0, : SHARE * gain_row].set(gain_terms.astype(BF))
    head_grad = rows_to_plane(dot_first(normed_one, grad_heads).astype(BF))
    out_grad = out_grad.reshape(16, -1, width)
    early_grad = lax.psum_scatter(
        jnp.concatenate([head_grad, split_join(out_grad, cell), gain_rows], axis=1).reshape(-1, cell),
        PLANE,
        scatter_dimension=0,
        tiled=True,
    )
    mlp_back = lax.all_to_all(
        join(late_grad[:mlp_height], mlp_parts).reshape(SHARE, row, -1), RING, 0, 0, tiled=True
    )
    home = [(to, own) for own, to in row_route()]
    down_back = lax.ppermute(join(late_grad[mlp_height:], out_parts), AXES, home)
    gain_back = jnp.zeros((SHARE, row, HEAD_SIZE), BF).at[:, 0, :gain_row].set(
        early_grad[out_end, : SHARE * gain_row].reshape(SHARE, gain_row)
    )
    head_back = lax.all_to_all(
        jnp.concatenate([early_grad[:head_end].reshape(SHARE, row, cell), gain_back], axis=2),
        RING,
        0,
        0,
        tiled=True,
    )
    out_back = lax.ppermute(join(early_grad[head_end:out_end], out_parts), AXES, home)

    down_out = scatter_rows(dot(hidden[:half_rows], down_slice), dot(hidden[half_rows:], down_slice))
    block_output = (hidden_two + down_out).astype(BF)

    def whole(value):
        return value.astype(F32).transpose(1, 0, 2).reshape(row, -1)

    grads = (
        whole(head_back[:, :, :query_cols]),
        whole(head_back[:, :, query_cols : query_cols + HEAD_SIZE]),
        whole(head_back[:, :, query_cols + HEAD_SIZE : cell]),
        out_back.astype(F32),
        whole(mlp_back[:, :, :hidden_cols]),
        whole(mlp_back[:, :, hidden_cols:]),
        down_back.astype(F32),
        jnp.sum(head_back[:, 0, cell : cell + gain_row].astype(F32), axis=0),
    )
    params = (
        query_weight,
        key_matrix,
        value_matrix,
        out_weight,
        gate_weight,
        up_weight,
        down_weight,
        norm_gains,
    )
    firsts = (
        query_first,
        key_first_moment,
        value_first_moment,
        out_first,
        gate_first,
        up_first,
        down_first,
        gains_first,
    )
    seconds = (
        query_second,
        key_second_moment,
        value_second_moment,
        out_second,
        gate_second,
        up_second,
        down_second,
        gains_second,
    )
    rates = (
        MODEL_WIDTH ** (-0.5),
        MODEL_WIDTH ** (-0.5),
        MODEL_WIDTH ** (-0.5),
        (TOK_DEV / (QUERY_HEADS * HEAD_SIZE)) ** 0.5,
        MODEL_WIDTH ** (-0.5),
        MODEL_WIDTH ** (-0.5),
        FF ** (-0.5),
        0.5,
    )
    decays = (DECAY, DECAY, DECAY, DECAY, DECAY, DECAY, DECAY, 0.0)
    results = [block_output, input_grad]
    for i in range(8):
        results.extend(adam(params[i], grads[i], firsts[i], seconds[i], rates[i], decays[i]))
    return tuple(results)


def split_join(value, width):
    rows, columns = value.shape[1:]
    value = value.reshape(16, rows, columns // width, width)
    return jnp.swapaxes(value, 1, 2).reshape(16, -1, width)


def solution(mesh):
    fine = Mesh(mesh.devices.reshape(SIZES), AXES)
    matrix, vector, grouped = P(AXES, None), P(AXES), P(("z", "xl", "y"), None)
    states = (matrix,) * 7 + (vector,)
    return jax.shard_map(
        local,
        mesh=fine,
        in_specs=(matrix, matrix, grouped, grouped) + states * 3,
        out_specs=(matrix, matrix) + (matrix,) * 21 + (vector,) * 3,
        check_vma=False,
    )
```

```python
import jax
import jax.numpy as jnp
from jax import lax
from jax.experimental import pallas as pl
from jax.experimental.pallas import tpu as pltpu
from jax.sharding import Mesh
from jax.sharding import PartitionSpec as P

MODEL_WIDTH = 2048
QUERY_HEADS = 16
KEY_VALUE_HEADS = 8
HEAD_SIZE = 128
FF = 6144
TOK_DEV = 128
STEP = 10

EPS = 1e-06
THETA = 1000000.0
BETA_ONE = 0.9
BETA_TWO = 0.95
ADAM_EPS = 1e-08
DECAY = 0.1

AXES = ("z", "xl", "y", "xh", "c")
SIZES = (4, 2, 4, 2, 2)
RING = ("xl", "xh", "c")
PLANE = ("z", "y")
CHIPS = ("xl", "xh")
SHARE = 8
OFFSETS = (0, 2, 1, 3)
BF = jnp.bfloat16
F32 = jnp.float32


def chip_number(x):
    return (x % 2) * 2 + x // 2


def from_chip(value, offset):
    pairs = [(chip_number((x + offset) % 4), chip_number(x)) for x in range(4)]
    return lax.ppermute(value, CHIPS, pairs)


def from_core(value):
    return lax.ppermute(value, "c", [(0, 1), (1, 0)])


def row_route():
    pairs = []
    for z in range(4):
        for xl in range(2):
            for y in range(4):
                for xh in range(2):
                    for c in range(2):
                        own = (((z * 2 + xl) * 4 + y) * 2 + xh) * 2 + c
                        part = 2 * z + xl
                        to = (((y * 2 + part // 4) * 4 + (xh * 2 + c)) * 2 + (part // 2) % 2) * 2 + part % 2
                        pairs.append((own, to))
    return pairs


def gather_rows(block):
    near = [block] + [from_chip(block, offset) for offset in OFFSETS[1:]]
    return near + [from_core(value) for value in near]


def row_blocks():
    return [group * 4 + core * 2 + chip for core in range(2) for group in range(2) for chip in range(2)]


def dot(left, right):
    return jnp.dot(left, right, preferred_element_type=F32)


def dot_last(left, right):
    return lax.dot_general(left, right, (((1,), (1,)), ((), ())), preferred_element_type=F32)


def dot_first(left, right):
    return lax.dot_general(left, right, (((0,), (0,)), ((), ())), preferred_element_type=F32)


def inverse_rms(values):
    return lax.rsqrt(jnp.mean(values * values, axis=-1, keepdims=True) + EPS)


def call(body, outs, args, after=(), scratch=(), vmem=48, flops=0, name=None):
    size = sum(a.size * a.dtype.itemsize for a in args) + sum(
        o.size * jnp.dtype(o.dtype).itemsize for o in outs
    )
    count = len(args)

    def run(*refs):
        body(*refs[:count], *refs[count + len(after) :])

    return pl.pallas_call(
        run,
        out_shape=tuple(outs),
        in_specs=[pl.BlockSpec(memory_space=pltpu.VMEM)] * count + [pl.BlockSpec(memory_space=pl.ANY)] * len(after),
        out_specs=tuple(pl.BlockSpec(memory_space=pltpu.VMEM) for _ in outs),
        scratch_shapes=list(scratch),
        compiler_params=pltpu.CompilerParams(vmem_limit_bytes=vmem * 2**20),
        cost_estimate=pl.CostEstimate(flops=flops, bytes_accessed=size, transcendentals=0),
        name=name,
    )(*args, *after)


def shape(dims, dtype=BF):
    return jax.ShapeDtypeStruct(tuple(dims), dtype)


class Sizes:
    def __init__(self):
        self.width = MODEL_WIDTH
        self.heads = QUERY_HEADS // SHARE
        self.query = self.heads * HEAD_SIZE
        self.cell = self.query + 2 * HEAD_SIZE
        self.hidden = FF // SHARE
        self.row = MODEL_WIDTH // 128
        self.down_row = FF // 128
        self.out_parts = self.width // self.cell
        self.mlp_parts = 2 * self.hidden // self.cell
        self.ring_rows = SHARE * self.row
        self.mlp_rows = self.mlp_parts * self.row
        self.out_rows = self.out_parts * self.row
        self.down_rows = self.out_parts * self.down_row
        self.early = self.ring_rows + self.out_rows + self.row
        self.late = SHARE * self.mlp_rows + self.down_rows
        self.gains = (2 * MODEL_WIDTH + 2 * HEAD_SIZE) // 128
        self.block = TOK_DEV
        self.rows = 8 * TOK_DEV
        self.group = 4 * TOK_DEV
        self.half = 2 * TOK_DEV


def pack_weights(s):
    def body(query, key, value, out, gate, up, down, gains, columns, lines):
        for j in range(SHARE):
            q, h = s.query, HEAD_SIZE
            columns[j, : s.row, :q] = query[:, j * q : (j + 1) * q].astype(BF)
            columns[j, : s.row, q : q + h] = key[:, j * h : (j + 1) * h].astype(BF)
            columns[j, : s.row, q + h :] = value[:, j * h : (j + 1) * h].astype(BF)
            for source, start in ((gate, 0), (up, s.hidden)):
                done = 0
                while done < s.hidden:
                    at = start + done
                    part, inside = at // s.cell, at % s.cell
                    size = min(s.cell - inside, s.hidden - done)
                    columns[j, s.row * (1 + part) : s.row * (2 + part), inside : inside + size] = source[
                        :, j * s.hidden + done : j * s.hidden + done + size
                    ].astype(BF)
                    done += size
            columns[j, s.row + s.mlp_rows :, :] = jnp.zeros((s.row, s.cell), BF)
            columns[j, s.row + s.mlp_rows :, :HEAD_SIZE] = gains[...].astype(BF)
        for p in range(s.out_parts):
            lines[p * s.row : (p + 1) * s.row] = out[:, p * s.cell : (p + 1) * s.cell].astype(BF)
            at = s.out_rows + p * s.down_row
            lines[at : at + s.down_row] = down[:, p * s.cell : (p + 1) * s.cell].astype(BF)

    return body


def place_weights(s):
    def body(columns, lines, early, late, table):
        gain_at = s.row + s.mlp_rows
        table[...] = jnp.zeros_like(table)
        for j in range(SHARE):
            early[j * s.row : (j + 1) * s.row] = columns[j, : s.row]
            late[j * s.mlp_rows : (j + 1) * s.mlp_rows] = columns[j, s.row : gain_at]
            table[j : j + 1] = columns[j, gain_at : gain_at + s.row].astype(F32)[:1]
        early[s.ring_rows : s.ring_rows + s.out_rows] = lines[: s.out_rows]
        early[s.ring_rows + s.out_rows :] = table[...].astype(BF)
        late[SHARE * s.mlp_rows :] = lines[s.out_rows :]

    return body


def fill_head_weight(s, early, target):
    part = 4 * s.row
    for z in range(4):
        for xl in range(2):
            for y in range(4):
                at = ((z * 2 + xl) * 4 + y) * part
                target[at : at + part] = early[z * 4 + y, xl * part : (xl + 1) * part]


def fill_out_weight(s, early, target):
    for f in range(16):
        for p in range(s.out_parts):
            at = s.ring_rows + p * s.row
            target[f * s.row : (f + 1) * s.row, p * s.cell : (p + 1) * s.cell] = early[f, at : at + s.row]


def turn(value):
    return pltpu.roll(value, HEAD_SIZE // 2, 1)


def head_forward(s):
    scale = HEAD_SIZE ** (-0.5)

    def body(*refs):
        blocks = refs[:8]
        early, bias, cosine, sine, gain_one, gain_query, gain_key = refs[8:15]
        normed, linear, query, key, value, probs, mixed, near, far = refs[15:24]
        weight, out_weight = refs[24:]
        for ref, at in zip(blocks, row_blocks()):
            wide = ref[...].astype(F32)
            normed[at * s.block : (at + 1) * s.block] = (wide * inverse_rms(wide) * gain_one[...]).astype(BF)
        fill_head_weight(s, early, weight)
        fill_out_weight(s, early, out_weight)
        q, h = s.query, HEAD_SIZE
        for group in range(2):
            rows = pl.ds(group * s.group, s.group)
            lin = dot(normed[rows], weight[...])
            linear[rows] = lin[:, : q + h]
            value[rows] = lin[:, q + h :].astype(BF)
            cos, sin = cosine[rows], sine[rows]

            def turned(part, gain):
                part = part * inverse_rms(part) * gain[...]
                return (part * cos + turn(part) * sin).astype(BF)

            key[rows] = turned(lin[:, q : q + h], gain_key)
            for r in range(s.heads):
                query[rows, r * h : (r + 1) * h] = turned(lin[:, r * h : (r + 1) * h], gain_query)
            for r in range(s.heads):
                score = dot_last(query[rows, r * h : (r + 1) * h], key[rows]) * scale + bias[group]
                expo = jnp.exp(score - jnp.max(score, axis=-1, keepdims=True))
                prob = expo / jnp.sum(expo, axis=-1, keepdims=True)
                probs[group * s.heads + r] = prob
                mixed[rows, r * h : (r + 1) * h] = dot(prob.astype(BF), value[rows]).astype(BF)
        for group in range(2):
            into = pl.ds(group * s.half, s.half)
            far[into] = dot(mixed[pl.ds(group * s.group + s.half, s.half)], out_weight[...]).astype(BF)
            near[into] = dot(mixed[pl.ds(group * s.group, s.half)], out_weight[...]).astype(BF)

    return body


def ring_add(s):
    def body(near, arrived, own, *others):
        own[...] = near[: s.block].astype(F32) + arrived[: s.block].astype(F32)
        for i, other in enumerate(others):
            rows = pl.ds((i + 1) * s.block, s.block)
            other[...] = (near[rows].astype(F32) + arrived[rows].astype(F32)).astype(BF)

    return body


def total_of(own, parts):
    total = own[...]
    for part in parts:
        total = total + part[...].astype(F32)
    return total


def branch_end(s):
    def body(own, first, second, third, tokens, gain_two, hidden_two, normed):
        value = tokens[...].astype(F32) + total_of(own, (first, second, third))
        hidden_two[...] = value
        normed[...] = (value * inverse_rms(value) * gain_two[...]).astype(BF)

    return body


def norm_back(values, gain, grad):
    scale = inverse_rms(values)
    normalized = values * scale
    inner = grad * gain
    back = scale * inner - normalized * scale * jnp.mean(inner * normalized, axis=-1, keepdims=True)
    return back, grad * normalized


def mlp_weights(s):
    def body(*refs):
        late = refs[0]
        blocks = refs[1:9]
        weight, down, upstream, grad_hidden = refs[9:]
        for f in range(16):
            z, y = divmod(f, 4)
            for j in range(SHARE):
                xl, part = divmod(j, 4)
                at = (((z * 2 + xl) * 4 + y) * 4 + part) * s.row
                for p in range(s.mlp_parts):
                    start = j * s.mlp_rows + p * s.row
                    weight[at : at + s.row, p * s.cell : (p + 1) * s.cell] = late[f, start : start + s.row]
            for p in range(s.out_parts):
                start = SHARE * s.mlp_rows + p * s.down_row
                down[f * s.down_row : (f + 1) * s.down_row, p * s.cell : (p + 1) * s.cell] = late[
                    f, start : start + s.down_row
                ]
        for ref, at in zip(blocks, row_blocks()):
            upstream[at * s.block : (at + 1) * s.block] = ref[...]
        step = 2 * HEAD_SIZE
        for n in range(s.hidden // step):
            columns = slice(n * step, (n + 1) * step)
            grad_hidden[:, columns] = dot_last(upstream[...], down[columns])

    return body


def mlp_forward_back(s):
    step = 2 * HEAD_SIZE

    def body(*refs):
        blocks = refs[:8]
        weight, grad_hidden, normed, hidden, grads, far = refs[8:]
        for ref, at in zip(blocks, row_blocks()):
            normed[at * s.block : (at + 1) * s.block] = ref[...]
        for n in range(s.hidden // step):
            columns = slice(n * step, (n + 1) * step)
            second = slice(s.hidden + n * step, s.hidden + (n + 1) * step)
            gate = dot(normed[...], weight[:, columns])
            up = dot(normed[...], weight[:, second])
            sigma = jax.nn.sigmoid(gate)
            active = gate * sigma
            hidden[:, columns] = (active * up).astype(BF)
            grad = grad_hidden[:, columns]
            grads[:, columns] = (grad * up * sigma * (1.0 + gate * (1.0 - sigma))).astype(BF)
            grads[:, second] = (grad * active).astype(BF)
        back_half(s, grads, weight, far, 1)

    return body


def back_half(s, grads, weight, target, core):
    step = 2 * HEAD_SIZE
    for group in range(2):
        rows = pl.ds(group * s.group + core * s.half, s.half)
        for n in range(s.width // step):
            columns = slice(n * step, (n + 1) * step)
            target[pl.ds(group * s.half, s.half), columns] = dot_last(grads[rows], weight[columns]).astype(BF)


def mlp_near(s):
    def body(grads, weight, near):
        back_half(s, grads, weight, near, 0)

    return body


def mlp_weight_grads(s, args, after):
    step = 4 * s.row * 4

    def body(normed, grads, hidden, upstream, *rest):
        target = rest[-1]
        pair = pl.program_id(0)
        for near_z in range(2):
            for xl in range(2):
                at = pl.multiple_of(pair * (s.width // 2) + (near_z * 2 + xl) * step, step)
                tile = dot_first(normed[:, pl.ds(at, step)], grads[...]).astype(BF)
                for y in range(4):
                    for part in range(4):
                        line = (y * 4 + part) * s.row
                        for p in range(s.mlp_parts):
                            start = (xl * 4 + part) * s.mlp_rows + p * s.row
                            target[near_z * 4 + y, start : start + s.row] = tile[
                                line : line + s.row, p * s.cell : (p + 1) * s.cell
                            ]
        wide = s.hidden // 2
        columns = hidden[:, pl.ds(pl.multiple_of(pair * wide, wide), wide)]
        for p in range(s.out_parts):
            tile = dot_first(columns, upstream[:, p * s.cell : (p + 1) * s.cell]).astype(BF)
            for f in range(8):
                start = SHARE * s.mlp_rows + p * s.down_row
                target[f, start : start + s.down_row] = tile[f * s.down_row : (f + 1) * s.down_row]

    whole = pl.BlockSpec(memory_space=pltpu.VMEM, pipeline_mode=pl.Buffered(1))
    return pl.pallas_call(
        body,
        grid=(2,),
        out_shape=shape((16, s.late, s.cell)),
        in_specs=[
            pl.BlockSpec(a.shape, lambda i: (0, 0), pipeline_mode=pl.Buffered(1)) for a in args
        ]
        + [pl.BlockSpec(memory_space=pl.ANY)] * len(after),
        out_specs=pl.BlockSpec((8, s.late, s.cell), lambda i: (i, 0, 0)),
        compiler_params=pltpu.CompilerParams(vmem_limit_bytes=48 * 2**20),
        cost_estimate=pl.CostEstimate(
            flops=6 * s.rows * s.width * s.hidden, bytes_accessed=24 * 2**20, transcendentals=0
        ),
        name="mlp_weight_grads",
    )(*args, *after)


def mlp_out(s):
    step = 4 * HEAD_SIZE

    def body(hidden, down, near, far):
        for target, core in ((far, 1), (near, 0)):
            for group in range(2):
                rows = pl.ds(group * s.group + core * s.half, s.half)
                for n in range(s.width // step):
                    columns = slice(n * step, (n + 1) * step)
                    target[pl.ds(group * s.half, s.half), columns] = dot(hidden[rows], down[:, columns]).astype(BF)

    return body


def mlp_back_end(s):
    def body(own, first, second, third, cotangent, hidden_two, gain_two, grad_hidden_two, low, terms):
        grad = total_of(own, (first, second, third))
        back, gains = norm_back(hidden_two[...], gain_two[...], grad)
        value = cotangent[...].astype(F32) + back
        grad_hidden_two[...] = value
        low[...] = value.astype(BF)
        terms[...] = jnp.sum(gains, axis=0, keepdims=True)

    return body


def head_back(s):
    scale = HEAD_SIZE ** (-0.5)

    def body(*refs):
        blocks = refs[:8]
        early, mixed, probs, query, key, value, linear, cosine, sine, gain_query, gain_key = refs[8:19]
        grads, out_grad, query_terms, key_terms = refs[19:23]
        branch, out_weight, grad_mixed = refs[23:]
        for ref, at in zip(blocks, row_blocks()):
            branch[at * s.block : (at + 1) * s.block] = ref[...]
        fill_out_weight(s, early, out_weight)
        q, h = s.query, HEAD_SIZE
        query_sum = jnp.zeros((1, h), F32)
        key_sum = jnp.zeros((1, h), F32)
        for group in range(2):
            rows = pl.ds(group * s.group, s.group)
            grad_mixed[rows] = dot_last(branch[rows], out_weight[...]).astype(BF)
            cos, sin = cosine[rows], sine[rows]
            key_grad = jnp.zeros((s.group, h), F32)
            value_grad = jnp.zeros((s.group, h), F32)
            for r in range(s.heads):
                columns = slice(r * h, (r + 1) * h)
                prob = probs[group * s.heads + r]
                out = grad_mixed[rows, columns]
                grad_prob = dot_last(out, value[rows])
                inner = jnp.sum(prob * grad_prob, axis=-1, keepdims=True)
                grad_score = (prob * (grad_prob - inner)).astype(BF)
                value_grad = value_grad + dot_first(prob.astype(BF), out)
                key_grad = key_grad + dot_first(grad_score, query[rows, columns]) * scale
                turned = dot(grad_score, key[rows]) * scale
                back, terms = norm_back(
                    linear[rows, columns], gain_query[...], turned * cos - turn(turned) * sin
                )
                grads[rows, columns] = back.astype(BF)
                query_sum = query_sum + jnp.sum(terms, axis=0, keepdims=True)
            back, terms = norm_back(
                linear[rows, q : q + h], gain_key[...], key_grad * cos - turn(key_grad) * sin
            )
            grads[rows, q : q + h] = back.astype(BF)
            key_sum = key_sum + jnp.sum(terms, axis=0, keepdims=True)
            grads[rows, q + h :] = value_grad.astype(BF)
        query_terms[...] = query_sum
        key_terms[...] = key_sum
        for p in range(s.out_parts):
            columns = slice(p * s.cell, (p + 1) * s.cell)
            out_grad[:, columns] = dot_first(mixed[...], branch[:, columns]).astype(BF)

    return body


def input_back(s):
    def body(grads, early, normed, gain_one, near, far, terms, weight):
        fill_head_weight(s, early, weight)
        step = 4 * HEAD_SIZE
        for n in range(s.width // step):
            columns = slice(n * step, (n + 1) * step)
            total = jnp.zeros((1, step), F32)
            for target, core in ((far, 1), (near, 0)):
                for group in range(2):
                    rows = pl.ds(group * s.group + core * s.half, s.half)
                    part = dot_last(grads[rows], weight[columns])
                    target[pl.ds(group * s.half, s.half), columns] = part.astype(BF)
                    total = total + jnp.sum(part * normed[rows, columns].astype(F32), axis=0, keepdims=True)
            terms[:, columns] = total / gain_one[:, columns]

    return body


def head_weight_grads(s):
    step = 4 * s.row * 4

    def body(normed, grads, out_grad, gain_rows, target):
        for z in range(4):
            for xl in range(2):
                at = (z * 2 + xl) * step
                tile = dot_first(normed[:, at : at + step], grads[...]).astype(BF)
                for y in range(4):
                    target[z * 4 + y, xl * 4 * s.row : (xl + 1) * 4 * s.row] = tile[y * 4 * s.row : (y + 1) * 4 * s.row]
        for f in range(16):
            for p in range(s.out_parts):
                start = s.ring_rows + p * s.row
                target[f, start : start + s.row] = out_grad[f * s.row : (f + 1) * s.row, p * s.cell : (p + 1) * s.cell]
            target[f, s.ring_rows + s.out_rows :] = gain_rows[f]

    return body


def input_end(s):
    def body(own, first, second, third, tokens, grad_hidden_two, gain_one, input_grad):
        back, _ = norm_back(tokens[...].astype(F32), gain_one[...], total_of(own, (first, second, third)))
        input_grad[...] = grad_hidden_two[...] + back

    return body


def output_end(s):
    def body(own, first, second, third, hidden_two, block_output):
        block_output[...] = (hidden_two[...] + total_of(own, (first, second, third))).astype(BF)

    return body


def pack_head_grads(s):
    def body(grads, columns, lines, table):
        table[...] = grads[s.ring_rows + s.out_rows :].astype(F32)
        for j in range(SHARE):
            columns[j, : s.row] = grads[j * s.row : (j + 1) * s.row]
            columns[j, s.row :] = jnp.broadcast_to(table[j : j + 1], (s.row, s.cell)).astype(BF)
        lines[...] = grads[s.ring_rows : s.ring_rows + s.out_rows]

    return body


def adam(weight, grad, first, second, rate, decay):
    first_new = BETA_ONE * first + (1.0 - BETA_ONE) * grad
    second_new = BETA_TWO * second + (1.0 - BETA_TWO) * grad * grad
    first_hat = first_new / (1.0 - BETA_ONE**STEP)
    second_hat = second_new / (1.0 - BETA_TWO**STEP)
    weight_new = weight - rate * (first_hat / (jnp.sqrt(second_hat) + ADAM_EPS) + decay * weight)
    return (weight_new, first_new, second_new)


def step_into(ins, outs, columns, grad, rate, decay):
    results = adam(ins[0][:, columns], grad.astype(F32), ins[1][:, columns], ins[2][:, columns], rate, decay)
    for out, value in zip(outs, results):
        out[:, columns] = value


def mlp_update(s):
    def body(*refs):
        columns, lines = refs[:2]
        gate, up, down = refs[2:5], refs[5:8], refs[8:11]
        outs = refs[11:]
        for j in range(SHARE):
            for ins, to, start in ((gate, outs[0:3], 0), (up, outs[3:6], s.hidden)):
                done = 0
                while done < s.hidden:
                    at = start + done
                    part, inside = at // s.cell, at % s.cell
                    size = min(s.cell - inside, s.hidden - done)
                    grad = columns[j, part * s.row : (part + 1) * s.row, inside : inside + size]
                    own = slice(j * s.hidden + done, j * s.hidden + done + size)
                    step_into(ins, to, own, grad, MODEL_WIDTH ** (-0.5), DECAY)
                    done += size
        for p in range(s.out_parts):
            grad = lines[p * s.down_row : (p + 1) * s.down_row]
            step_into(down, outs[6:9], slice(p * s.cell, (p + 1) * s.cell), grad, FF ** (-0.5), DECAY)

    return body


def head_update(s):
    def body(*refs):
        columns, lines = refs[:2]
        query, key, value, out, gains = refs[2:5], refs[5:8], refs[8:11], refs[11:14], refs[14:17]
        outs = refs[17:]
        rate = MODEL_WIDTH ** (-0.5)
        gain_grad = jnp.zeros((1, HEAD_SIZE), F32)
        for j in range(SHARE):
            start = 0
            for ins, to, size in ((query, outs[0:3], s.query), (key, outs[3:6], HEAD_SIZE), (value, outs[6:9], HEAD_SIZE)):
                grad = columns[j, : s.row, start : start + size]
                step_into(ins, to, slice(j * size, (j + 1) * size), grad, rate, DECAY)
                start += size
            gain_grad = gain_grad + columns[j, s.row :, :HEAD_SIZE].astype(F32)[:1]
        out_rate = (TOK_DEV / (QUERY_HEADS * HEAD_SIZE)) ** 0.5
        for p in range(s.out_parts):
            grad = lines[p * s.row : (p + 1) * s.row]
            step_into(out, outs[9:12], slice(p * s.cell, (p + 1) * s.cell), grad, out_rate, DECAY)
        step_into(gains, outs[12:15], slice(0, HEAD_SIZE), gain_grad, 0.5, 0.0)

    return body


def layout(lengths, span_ids):
    span = TOK_DEV // 2
    table = jnp.concatenate([lengths[0], span_ids[0]])
    other = lax.ppermute(table, "xl", [(0, 1), (1, 0)])
    both = jnp.stack([table, other])
    sizes, spans = both[:, :2], both[:, 2:]
    chip = lax.axis_index("xh") * 2 + lax.axis_index("xl")
    core = lax.axis_index("c")
    offset = jnp.arange(2)[:, None, None] + 2 * jnp.arange(2)[None, None, :]
    place = ((chip + offset) % 4) // 2 * 2 + (core + jnp.arange(2)[None, :, None]) % 2
    block = (2 * place[..., None] + jnp.arange(2)).reshape(2, 8)
    owner = jnp.sum(jnp.where(block[:, :, None] == jnp.arange(8), spans[:, None, :], 0), axis=-1)
    slots = (owner[:, :, None] * span + jnp.arange(span)).reshape(2, -1)
    ends = jnp.cumsum(sizes, axis=1)
    passed = slots[:, :, None] >= ends[:, None, :]
    sequence = jnp.sum(passed.astype(jnp.int32), axis=-1)
    position = slots - jnp.sum(jnp.where(passed, sizes[:, None, :], 0), axis=-1)
    return slots, sequence, position


def local(
    tokens,
    cotangent,
    lengths,
    span_ids,
    query_weight,
    key_matrix,
    value_matrix,
    out_weight,
    gate_weight,
    up_weight,
    down_weight,
    norm_gains,
    query_first,
    key_first_moment,
    value_first_moment,
    out_first,
    gate_first,
    up_first,
    down_first,
    gains_first,
    query_second,
    key_second_moment,
    value_second_moment,
    out_second,
    gate_second,
    up_second,
    down_second,
    gains_second,
):
    s = Sizes()
    block = (s.block, s.width)
    half_rows = (s.group, s.width)

    def ring_scatter(near, far, name):
        arrived = from_core(far)
        own, *others = call(
            ring_add(s), [shape(block, F32)] + [shape(block)] * 3, [near, arrived], vmem=16, name=name + "_add"
        )
        arrived = [from_chip(piece, -OFFSETS[i + 1]) for i, piece in enumerate(others)]
        return [own] + arrived, others

    def padded(vector):
        return jnp.pad(vector, (0, HEAD_SIZE - s.gains))[None]

    gains_wide = jnp.broadcast_to(padded(norm_gains), (s.row, HEAD_SIZE))
    columns, lines = call(
        pack_weights(s),
        [shape((SHARE, 2 * s.row + s.mlp_rows, s.cell)), shape((s.out_rows + s.down_rows, s.cell))],
        [query_weight, key_matrix, value_matrix, out_weight, gate_weight, up_weight, down_weight, gains_wide],
        vmem=16,
        name="pack_weights",
    )
    inputs = gather_rows(tokens)
    columns = lax.all_to_all(columns, RING, 0, 0, tiled=True)
    lines = lax.ppermute(lines, AXES, row_route())
    early, late = call(
        place_weights(s),
        [shape((s.early, s.cell)), shape((s.late, s.cell))],
        [columns, lines],
        after=inputs[1:4],
        scratch=[pltpu.VMEM((s.row, s.cell), F32)],
        vmem=16,
        name="place_weights",
    )
    early = lax.all_gather(early, PLANE, axis=0)
    late, early = lax.optimization_barrier((late, early))
    late = lax.all_gather(late, PLANE, axis=0)
    upstream_blocks = gather_rows(cotangent)

    gain_at = s.ring_rows + s.out_rows
    gains = early[:, gain_at : gain_at + SHARE, : s.gains].astype(F32)
    gains = gains.reshape(4, 4, 2, -1).transpose(0, 2, 1, 3).reshape(1, -1)
    gain_one = gains[:, : s.width]
    gain_two = gains[:, s.width : 2 * s.width]
    gain_query = gains[:, 2 * s.width : 2 * s.width + HEAD_SIZE]
    gain_key = gains[:, 2 * s.width + HEAD_SIZE :]

    slots, sequence, position = layout(lengths, span_ids)
    freq = THETA ** (-(2.0 * jnp.arange(HEAD_SIZE // 2, dtype=F32)) / HEAD_SIZE)
    angle = position.reshape(-1).astype(F32)[:, None] * freq
    cosine, sine = jnp.cos(angle), jnp.sin(angle)
    cosine = jnp.concatenate([cosine, cosine], axis=1)
    sine = jnp.concatenate([-sine, sine], axis=1)
    allowed = (sequence[:, :, None] == sequence[:, None, :]) & (slots[:, None, :] <= slots[:, :, None])
    bias = jnp.where(allowed, 0.0, -1e30).astype(F32)

    normed_one, linear, query, key, value, probs, mixed, near, far = call(
        head_forward(s),
        [
            shape((s.rows, s.width)),
            shape((s.rows, s.query + HEAD_SIZE), F32),
            shape((s.rows, s.query)),
            shape((s.rows, HEAD_SIZE)),
            shape((s.rows, HEAD_SIZE)),
            shape((2 * s.heads, s.group, s.group), F32),
            shape((s.rows, s.query)),
            shape(half_rows),
            shape(half_rows),
        ],
        [*inputs, early, bias, cosine, sine, gain_one, gain_query, gain_key],
        scratch=[pltpu.VMEM((s.width, s.cell), BF), pltpu.VMEM((s.query, s.width), BF)],
        flops=2 * s.rows * s.width * (s.cell + s.query),
        name="head_forward",
    )
    parts, _ = ring_scatter(near, far, "branch")
    hidden_two, normed_two = call(
        branch_end(s), [shape(block, F32), shape(block)], [*parts, tokens, gain_two], vmem=16, name="branch_end"
    )
    normed_blocks = gather_rows(normed_two)
    weight, down, upstream, grad_hidden = call(
        mlp_weights(s),
        [
            shape((s.width, 2 * s.hidden)),
            shape((s.hidden, s.width)),
            shape((s.rows, s.width)),
            shape((s.rows, s.hidden), F32),
        ],
        [late, *upstream_blocks],
        flops=2 * s.rows * s.width * s.hidden,
        name="mlp_weights",
    )
    normed_two, hidden, grads, far = call(
        mlp_forward_back(s),
        [shape((s.rows, s.width)), shape((s.rows, s.hidden)), shape((s.rows, 2 * s.hidden)), shape(half_rows)],
        [*normed_blocks, weight, grad_hidden],
        flops=6 * s.rows * s.width * s.hidden,
        name="mlp_forward_back",
    )
    (near,) = call(
        mlp_near(s),
        [shape(half_rows)],
        [grads, weight],
        flops=2 * s.rows * s.width * s.hidden,
        name="mlp_near",
    )
    parts, sent = ring_scatter(near, far, "mlp_back")
    late_grad = mlp_weight_grads(s, [normed_two, grads, hidden, upstream], sent)
    grad_hidden_two, grad_branch, gain_two_terms = call(
        mlp_back_end(s),
        [shape(block, F32), shape(block), shape((1, s.width), F32)],
        [*parts, cotangent, hidden_two, gain_two],
        after=[late_grad],
        vmem=16,
        name="mlp_back_end",
    )
    late_grad = lax.psum_scatter(
        late_grad.reshape(-1, s.cell), PLANE, scatter_dimension=0, tiled=True
    )
    branch_blocks = gather_rows(grad_branch)
    out_near, out_far = call(
        mlp_out(s),
        [shape(half_rows)] * 2,
        [hidden, down],
        after=[grad_branch],
        flops=2 * s.rows * s.width * s.hidden,
        name="mlp_out",
    )

    grads, out_grad, query_terms, key_terms = call(
        head_back(s),
        [
            shape((s.rows, s.cell)),
            shape((s.query, s.width)),
            shape((1, HEAD_SIZE), F32),
            shape((1, HEAD_SIZE), F32),
        ],
        [*branch_blocks, early, mixed, probs, query, key, value, linear, cosine, sine, gain_query, gain_key],
        after=[out_near],
        scratch=[
            pltpu.VMEM((s.rows, s.width), BF),
            pltpu.VMEM((s.query, s.width), BF),
            pltpu.VMEM((s.rows, s.query), BF),
        ],
        flops=4 * s.rows * s.width * s.query,
        name="head_back",
    )
    near, far, gain_one_terms = call(
        input_back(s),
        [shape(half_rows), shape(half_rows), shape((1, s.width), F32)],
        [grads, early, normed_one, gain_one],
        scratch=[pltpu.VMEM((s.width, s.cell), BF)],
        flops=2 * s.rows * s.width * s.cell,
        name="input_back",
    )
    gain_terms = jnp.concatenate([gain_one_terms, gain_two_terms, query_terms, key_terms], axis=1)
    gain_terms = gain_terms.reshape(4, 2, 4, -1).transpose(0, 2, 1, 3).reshape(16, SHARE, s.gains)
    gain_rows = jnp.pad(gain_terms.astype(BF), ((0, 0), (0, s.row - SHARE), (0, s.cell - s.gains)))
    early_grad = call(
        head_weight_grads(s),
        [shape((16, s.early, s.cell))],
        [normed_one, grads, out_grad, gain_rows],
        flops=2 * s.rows * s.width * s.cell,
        name="head_weight_grads",
    )[0]
    early_grad = lax.psum_scatter(
        early_grad.reshape(-1, s.cell), PLANE, scatter_dimension=0, tiled=True
    )
    parts, _ = ring_scatter(near, far, "input")
    (input_grad,) = call(
        input_end(s), [shape(block, F32)], [*parts, tokens, grad_hidden_two, gain_one], vmem=16, name="input_end"
    )
    parts, _ = ring_scatter(out_near, out_far, "output")
    (block_output,) = call(output_end(s), [shape(block)], [*parts, hidden_two], vmem=16, name="output_end")

    home = [(to, own) for own, to in row_route()]
    mlp_end = SHARE * s.mlp_rows
    columns = lax.all_to_all(late_grad[:mlp_end].reshape(SHARE, s.mlp_rows, s.cell), RING, 0, 0, tiled=True)
    lines = lax.ppermute(late_grad[mlp_end:], AXES, home)
    mlp_states = [
        (gate_weight, gate_first, gate_second),
        (up_weight, up_first, up_second),
        (down_weight, down_first, down_second),
    ]
    mlp_new = call(
        mlp_update(s),
        [shape(a.shape, F32) for group in mlp_states for a in group],
        [columns, lines] + [a for group in mlp_states for a in group],
        vmem=24,
        name="mlp_update",
    )
    columns, lines = call(
        pack_head_grads(s),
        [shape((SHARE, 2 * s.row, s.cell)), shape((s.out_rows, s.cell))],
        [early_grad],
        scratch=[pltpu.VMEM((s.row, s.cell), F32)],
        vmem=16,
        name="pack_head_grads",
    )
    columns = lax.all_to_all(columns, RING, 0, 0, tiled=True)
    lines = lax.ppermute(lines, AXES, home)
    head_states = [
        (query_weight, query_first, query_second),
        (key_matrix, key_first_moment, key_second_moment),
        (value_matrix, value_first_moment, value_second_moment),
        (out_weight, out_first, out_second),
        (padded(norm_gains), padded(gains_first), padded(gains_second)),
    ]
    head_new = call(
        head_update(s),
        [shape(a.shape, F32) for group in head_states for a in group],
        [columns, lines] + [a for group in head_states for a in group],
        vmem=16,
        name="head_update",
    )
    gains_new = tuple(value[0, : s.gains] for value in head_new[12:])
    return (block_output, input_grad, *head_new[:12], *mlp_new, *gains_new)


def solution(mesh):
    fine = Mesh(mesh.devices.reshape(SIZES), AXES)
    matrix, vector, grouped = P(AXES, None), P(AXES), P(("z", "xl", "y"), None)
    states = (matrix,) * 7 + (vector,)
    return jax.shard_map(
        local,
        mesh=fine,
        in_specs=(matrix, matrix, grouped, grouped) + states * 3,
        out_specs=(matrix, matrix) + (matrix,) * 21 + (vector,) * 3,
        check_vma=False,
    )
```

```python
import math

import jax
import jax.numpy as jnp
from jax import lax
from jax.experimental import pallas as pl
from jax.experimental.pallas import tpu as pltpu
from jax.sharding import Mesh
from jax.sharding import PartitionSpec as P

MODEL_WIDTH = 2048
QUERY_HEADS = 16
KEY_VALUE_HEADS = 8
HEAD_SIZE = 128
FF = 6144
TOK_DEV = 128
STEP = 10

EPS = 1e-06
THETA = 1000000.0
BETA_ONE = 0.9
BETA_TWO = 0.95
ADAM_EPS = 1e-08
DECAY = 0.1

AXES = ("z", "xl", "y", "xh", "c")
SIZES = (4, 2, 4, 2, 2)
RING = ("xl", "xh", "c")
PLANE = ("z", "y")
CHIPS = ("xl", "xh")
SHARE = 8
OFFSETS = (0, 2, 1, 3)
BF = jnp.bfloat16
F32 = jnp.float32


def chip_number(x):
    return (x % 2) * 2 + x // 2


def from_chip(value, offset):
    pairs = [(chip_number((x + offset) % 4), chip_number(x)) for x in range(4)]
    return lax.ppermute(value, CHIPS, pairs)


def from_core(value):
    return lax.ppermute(value, "c", [(0, 1), (1, 0)])


def row_route():
    pairs = []
    for z in range(4):
        for xl in range(2):
            for y in range(4):
                for xh in range(2):
                    for c in range(2):
                        own = (((z * 2 + xl) * 4 + y) * 2 + xh) * 2 + c
                        part = 2 * z + xl
                        to = (((y * 2 + part // 4) * 4 + (xh * 2 + c)) * 2 + (part // 2) % 2) * 2 + part % 2
                        pairs.append((own, to))
    return pairs


def from_plane(value, axis, offset):
    return lax.ppermute(value, axis, [((i + offset) % 4, i) for i in range(4)])


def from_chips(block):
    return [block] + [from_chip(block, offset) for offset in OFFSETS[1:]]


def with_cores(near):
    return near + [from_core(value) for value in near]


def row_blocks():
    return [group * 4 + core * 2 + chip for core in range(2) for group in range(2) for chip in range(2)]


def dot(left, right):
    return jnp.dot(left, right, preferred_element_type=F32)


def dot_last(left, right):
    return lax.dot_general(left, right, (((1,), (1,)), ((), ())), preferred_element_type=F32)


def dot_first(left, right):
    return lax.dot_general(left, right, (((0,), (0,)), ((), ())), preferred_element_type=F32)


def inverse_rms(values):
    return lax.rsqrt(jnp.mean(values * values, axis=-1, keepdims=True) + EPS)


class Arriving:
    def __init__(self, source, buffer, sem):
        self.buffer, self.shape, self.here = buffer, buffer.shape, False
        self.copy = pltpu.make_async_copy(source, buffer, sem)
        self.copy.start()

    def wait(self):
        if not self.here:
            self.copy.wait()
        self.here = True

    def __getitem__(self, index):
        self.wait()
        return self.buffer[index]


class Leaving:
    def __init__(self, buffer, target, sem):
        self.buffer, self.shape, self.sent = buffer, buffer.shape, False
        self.copy = pltpu.make_async_copy(buffer, target, sem)

    def __getitem__(self, index):
        return self.buffer[index]

    def __setitem__(self, index, value):
        self.buffer[index] = value

    def send(self):
        self.sent = True
        self.copy.start()


def bytes_of(values):
    return sum(math.prod(v.shape) * jnp.dtype(v.dtype).itemsize for v in values)


class Far:
    def __init__(self, value):
        self.value = value


def call(body, outs, args, after=(), scratch=(), flops=0, any_first=0, any_out=False, scalars=0, hidden=False, name=None):
    far_in = [isinstance(a, Far) for a in args]
    far_out = [isinstance(o, Far) for o in outs]
    args = [a.value if isinstance(a, Far) else a for a in args]
    outs = [o.value if isinstance(o, Far) else o for o in outs]
    size = bytes_of((*args, *outs))
    held = bytes_of(args[any_first:]) + bytes_of(() if any_out else outs)
    held += bytes_of([v for v in scratch if v.memory_space == pltpu.VMEM])
    moved = [v for v, far in zip((*args, *outs), far_in + far_out) if far]
    n_in, n_out, n_move = len(args), len(outs), len(moved)

    def run(*refs):
        ins, refs = list(refs[:n_in]), refs[n_in + len(after) :]
        results, refs = list(refs[:n_out]), refs[n_out:]
        own, refs = refs[: len(scratch)], refs[len(scratch) :]
        buffers, sems = list(refs[:n_move]), list(refs[n_move:])
        for i, far in enumerate(far_in):
            if far:
                ins[i] = Arriving(ins[i], buffers.pop(0), sems.pop(0))
        for i, far in enumerate(far_out):
            if far:
                results[i] = Leaving(buffers.pop(0), results[i], sems.pop(0))
        body(*ins, *results, *own)
        for value in ins:
            if isinstance(value, Arriving):
                value.wait()
        for value in results:
            if isinstance(value, Leaving) and not value.sent:
                value.send()
        for value in results:
            if isinstance(value, Leaving):
                value.copy.wait()

    def spec(far):
        return pl.BlockSpec(memory_space=pl.ANY if far else pltpu.VMEM)

    in_specs = [spec(far or i < any_first) for i, far in enumerate(far_in)]
    in_specs[:scalars] = [pl.BlockSpec(memory_space=pltpu.SMEM)] * scalars

    return pl.pallas_call(
        run,
        out_shape=tuple(outs),
        in_specs=in_specs + [spec(True)] * len(after),
        out_specs=tuple(spec(far or any_out) for far in far_out),
        scratch_shapes=list(scratch)
        + [pltpu.VMEM(v.shape, v.dtype) for v in moved]
        + [pltpu.SemaphoreType.DMA for _ in moved],
        compiler_params=pltpu.CompilerParams(vmem_limit_bytes=held + 12 * 2**20),
        cost_estimate=pl.CostEstimate(flops=flops, bytes_accessed=0 if hidden else size, transcendentals=0),
        name=name,
    )(*args, *after)


def tie(values, after, name):
    count = len(values)

    def body(*refs):
        pass

    return pl.pallas_call(
        body,
        out_shape=tuple(jax.ShapeDtypeStruct(v.shape, v.dtype) for v in values),
        in_specs=[pl.BlockSpec(memory_space=pl.ANY)] * (count + len(after)),
        out_specs=tuple(pl.BlockSpec(memory_space=pl.ANY) for _ in values),
        input_output_aliases={i: i for i in range(count)},
        name=name,
    )(*values, *after)


def shape(dims, dtype=BF):
    return jax.ShapeDtypeStruct(tuple(dims), dtype)


class Sizes:
    def __init__(self):
        self.width = MODEL_WIDTH
        self.heads = QUERY_HEADS // SHARE
        self.query = self.heads * HEAD_SIZE
        self.cell = self.query + 2 * HEAD_SIZE
        self.hidden = FF // SHARE
        self.row = MODEL_WIDTH // 128
        self.down_row = FF // 128
        self.out_parts = self.width // self.cell
        self.mlp_parts = 2 * self.hidden // self.cell
        self.ring_rows = SHARE * self.row
        self.mlp_rows = self.mlp_parts * self.row
        self.out_rows = self.out_parts * self.row
        self.down_rows = self.out_parts * self.down_row
        self.early = self.ring_rows + self.out_rows + self.row
        self.late = SHARE * self.mlp_rows + self.down_rows
        self.gains = (2 * MODEL_WIDTH + 2 * HEAD_SIZE) // 128
        self.block = TOK_DEV
        self.rows = 8 * TOK_DEV
        self.group = 4 * TOK_DEV
        self.half = 2 * TOK_DEV


def pack_weights(s):
    def body(query, key, value, out, gate, up, down, gains, columns, lines):
        for j in range(SHARE):
            q, h = s.query, HEAD_SIZE
            columns[j, : s.row, :q] = query[:, j * q : (j + 1) * q].astype(BF)
            columns[j, : s.row, q : q + h] = key[:, j * h : (j + 1) * h].astype(BF)
            columns[j, : s.row, q + h :] = value[:, j * h : (j + 1) * h].astype(BF)
            for source, start in ((gate, 0), (up, s.hidden)):
                done = 0
                while done < s.hidden:
                    at = start + done
                    part, inside = at // s.cell, at % s.cell
                    size = min(s.cell - inside, s.hidden - done)
                    columns[j, s.row * (1 + part) : s.row * (2 + part), inside : inside + size] = source[
                        :, j * s.hidden + done : j * s.hidden + done + size
                    ].astype(BF)
                    done += size
            columns[j, s.row + s.mlp_rows :, :] = jnp.zeros((s.row, s.cell), BF)
            columns[j, s.row + s.mlp_rows :, :HEAD_SIZE] = gains[...].astype(BF)
        for p in range(s.out_parts):
            lines[p * s.row : (p + 1) * s.row] = out[:, p * s.cell : (p + 1) * s.cell].astype(BF)
            at = s.out_rows + p * s.down_row
            lines[at : at + s.down_row] = down[:, p * s.cell : (p + 1) * s.cell].astype(BF)

    return body


def place_weights(s):
    def body(columns, lines, early, late, table):
        gain_at = s.row + s.mlp_rows
        table[...] = jnp.zeros_like(table)
        for j in range(SHARE):
            early[j * s.row : (j + 1) * s.row] = columns[j, : s.row]
            late[j * s.mlp_rows : (j + 1) * s.mlp_rows] = columns[j, s.row : gain_at]
            table[j : j + 1] = columns[j, gain_at : gain_at + s.row].astype(F32)[:1]
        early[s.ring_rows : s.ring_rows + s.out_rows] = lines[: s.out_rows]
        early[s.ring_rows + s.out_rows :] = table[...].astype(BF)
        late[SHARE * s.mlp_rows :] = lines[s.out_rows :]

    return body


def fill_head_weight(s, early, target):
    part = 4 * s.row
    for z in range(4):
        for xl in range(2):
            for y in range(4):
                at = ((z * 2 + xl) * 4 + y) * part
                target[at : at + part] = early[z * 4 + y, xl * part : (xl + 1) * part]


def fill_out_weight(s, early, target):
    for f in range(16):
        for p in range(s.out_parts):
            at = s.ring_rows + p * s.row
            target[f * s.row : (f + 1) * s.row, p * s.cell : (p + 1) * s.cell] = early[f, at : at + s.row]


def turn(value):
    return pltpu.roll(value, HEAD_SIZE // 2, 1)


def head_forward(s):
    scale = HEAD_SIZE ** (-0.5)

    def body(*refs):
        blocks = refs[:8]
        early, cosine, sine, bias, gain_one, gain_query, gain_key = refs[8:15]
        weight, out_weight, normed, linear, probs, query, key, value, mixed, near, far = refs[15:]
        for ref, at in zip(blocks, row_blocks()):
            wide = ref[...].astype(F32)
            normed[at * s.block : (at + 1) * s.block] = (wide * inverse_rms(wide) * gain_one[...]).astype(BF)
        normed.send()
        fill_head_weight(s, early, weight)
        weight.send()
        q, h = s.query, HEAD_SIZE
        for group in range(2):
            rows = pl.ds(group * s.group, s.group)
            lin = dot(normed[rows], weight[...])
            linear[rows] = lin[:, : q + h]
            value[rows] = lin[:, q + h :].astype(BF)
            cos, sin = cosine[rows], sine[rows]

            def turned(part, gain):
                part = part * inverse_rms(part) * gain[...]
                return (part * cos + turn(part) * sin).astype(BF)

            key[rows] = turned(lin[:, q : q + h], gain_key)
            for r in range(s.heads):
                query[rows, r * h : (r + 1) * h] = turned(lin[:, r * h : (r + 1) * h], gain_query)
        linear.send()
        fill_out_weight(s, early, out_weight)
        out_weight.send()
        for group in range(2):
            rows = pl.ds(group * s.group, s.group)
            for r in range(s.heads):
                score = dot_last(query[rows, r * h : (r + 1) * h], key[rows]) * scale + bias[group]
                expo = jnp.exp(score - jnp.max(score, axis=-1, keepdims=True))
                prob = expo * (1.0 / jnp.sum(expo, axis=-1, keepdims=True))
                probs[group * s.heads + r] = prob
                mixed[rows, r * h : (r + 1) * h] = dot(prob.astype(BF), value[rows]).astype(BF)
        probs.send()
        for target, core in ((far, 1), (near, 0)):
            for group in range(2):
                rows = pl.ds(group * s.group + core * s.half, s.half)
                target[pl.ds(group * s.half, s.half)] = dot(mixed[rows], out_weight[...]).astype(BF)
            if core:
                far.send()

    return body


def ring_add(s):
    def body(near, arrived, own, *others):
        own[...] = near[: s.block].astype(F32) + arrived[: s.block].astype(F32)
        for i, other in enumerate(others):
            rows = pl.ds((i + 1) * s.block, s.block)
            other[...] = (near[rows].astype(F32) + arrived[rows].astype(F32)).astype(BF)

    return body


def total_of(own, parts):
    total = own[...]
    for part in parts:
        total = total + part[...].astype(F32)
    return total


def branch_end(s):
    def body(own, first, second, third, tokens, gain_two, hidden_two, normed):
        value = tokens[...].astype(F32) + total_of(own, (first, second, third))
        hidden_two[...] = value
        normed[...] = (value * inverse_rms(value) * gain_two[...]).astype(BF)

    return body


def norm_back(values, gain, grad):
    scale = inverse_rms(values)
    normalized = values * scale
    inner = grad * gain
    back = scale * inner - normalized * scale * jnp.mean(inner * normalized, axis=-1, keepdims=True)
    return back, grad * normalized


def gather_into(s, blocks, buffer, sems):
    copies = []
    for i, (ref, at) in enumerate(zip(blocks, row_blocks())):
        copy = pltpu.make_async_copy(ref, buffer.at[pl.ds(at * s.block, s.block)], sems.at[i])
        copy.start()
        copies.append(copy)
    return copies


def mlp_weights(s):
    def body(*refs):
        blocks = refs[:8]
        late, down, weight, grad_hidden, upstream, sems = refs[8:]
        copies = gather_into(s, blocks, upstream, sems)
        for f in range(16):
            for p in range(s.out_parts):
                start = SHARE * s.mlp_rows + p * s.down_row
                down[f * s.down_row : (f + 1) * s.down_row, p * s.cell : (p + 1) * s.cell] = late[
                    f, start : start + s.down_row
                ]
        down.send()
        for f in range(16):
            z, y = divmod(f, 4)
            for j in range(SHARE):
                xl, part = divmod(j, 4)
                at = (((z * 2 + xl) * 4 + y) * 4 + part) * s.row
                for p in range(s.mlp_parts):
                    start = j * s.mlp_rows + p * s.row
                    weight[at : at + s.row, p * s.cell : (p + 1) * s.cell] = late[f, start : start + s.row]
        weight.send()
        for copy in copies:
            copy.wait()
        step = 2 * HEAD_SIZE
        for n in range(s.hidden // step):
            columns = slice(n * step, (n + 1) * step)
            grad_hidden[:, columns] = dot_last(upstream[...], down[columns])

    return body


def mlp_forward_back(s):
    step = 2 * HEAD_SIZE

    def body(*refs):
        blocks = refs[:8]
        weight, grad_hidden, hidden, grads, far, normed, kept, sems, weight_sems = refs[8:]
        copies = gather_into(s, blocks, normed, sems)
        tiles = []
        for n in range(s.hidden // step):
            for half in range(2):
                columns = pl.ds(half * s.hidden + n * step, step)
                tile = pltpu.make_async_copy(
                    weight.at[:, columns], kept.at[:, columns], weight_sems.at[2 * n + half]
                )
                tile.start()
                tiles.append(tile)
        for copy in copies:
            copy.wait()
        for n in range(s.hidden // step):
            columns = slice(n * step, (n + 1) * step)
            second = slice(s.hidden + n * step, s.hidden + (n + 1) * step)
            tiles[2 * n].wait()
            tiles[2 * n + 1].wait()
            gate = dot(normed[...], kept[:, columns])
            up = dot(normed[...], kept[:, second])
            sigma = jax.nn.sigmoid(gate)
            active = gate * sigma
            hidden[:, columns] = (active * up).astype(BF)
            grad = grad_hidden[:, columns]
            grads[:, columns] = (grad * up * (sigma * (1.0 + gate * (1.0 - sigma)))).astype(BF)
            grads[:, second] = (grad * active).astype(BF)
        hidden.send()
        grads.send()
        for n in range(s.width // step):
            back_tile(s, grads, kept, far, 1, n)

    return body


def back_tile(s, grads, weight, target, core, n):
    columns = slice(n * 2 * HEAD_SIZE, (n + 1) * 2 * HEAD_SIZE)
    for group in range(2):
        rows = pl.ds(group * s.group + core * s.half, s.half)
        target[pl.ds(group * s.half, s.half), columns] = dot_last(grads[rows], weight[columns]).astype(BF)


def mlp_near(s):
    step = 2 * HEAD_SIZE

    def body(weight, grads, near, kept, sems):
        tiles = []
        for n in range(s.width // step):
            rows = pl.ds(n * step, step)
            tile = pltpu.make_async_copy(weight.at[rows], kept.at[rows], sems.at[n])
            tile.start()
            tiles.append(tile)
        for n, tile in enumerate(tiles):
            tile.wait()
            back_tile(s, grads, kept, near, 0, n)

    return body


def mlp_weight_grads(s):
    step = 4 * s.row * 4

    def body(*refs):
        normed_blocks, blocks = refs[:8], refs[8:16]
        grads, hidden, target, normed, upstream, made, normed_sems, sems, out_sems = refs[16:]
        normed_copies = gather_into(s, normed_blocks, normed, normed_sems)
        copies = gather_into(s, blocks, upstream, sems)
        leaving = []
        for copy in normed_copies:
            copy.wait()
        for z in range(4):
            for xl in range(2):
                at = (z * 2 + xl) * step
                tile = dot_first(normed[:, at : at + step], grads[...]).astype(BF)
                for y in range(4):
                    for part in range(4):
                        line = (y * 4 + part) * s.row
                        for p in range(s.mlp_parts):
                            start = (xl * 4 + part) * s.mlp_rows + p * s.row
                            made[z * 4 + y, start : start + s.row] = tile[
                                line : line + s.row, p * s.cell : (p + 1) * s.cell
                            ]
            if z % 2:
                pair = z // 2
                if pair == 0:
                    for copy in copies:
                        copy.wait()
                wide = s.hidden // 2
                columns = hidden[:, pair * wide : (pair + 1) * wide]
                for p in range(s.out_parts):
                    tile = dot_first(columns, upstream[:, p * s.cell : (p + 1) * s.cell]).astype(BF)
                    for f in range(8):
                        start = SHARE * s.mlp_rows + p * s.down_row
                        made[pair * 8 + f, start : start + s.down_row] = tile[f * s.down_row : (f + 1) * s.down_row]
                half = pl.ds(pair * 8, 8)
                copy = pltpu.make_async_copy(made.at[half], target.at[half], out_sems.at[pair])
                copy.start()
                leaving.append(copy)
        for copy in leaving:
            copy.wait()

    return body


def mlp_out(s):
    step = 4 * HEAD_SIZE

    def body(hidden, down, near, far):
        for target, core in ((far, 1), (near, 0)):
            for group in range(2):
                rows = pl.ds(group * s.group + core * s.half, s.half)
                for n in range(s.width // step):
                    columns = slice(n * step, (n + 1) * step)
                    target[pl.ds(group * s.half, s.half), columns] = dot(hidden[rows], down[:, columns]).astype(BF)

    return body


def mlp_back_end(s):
    def body(own, first, second, third, cotangent, hidden_two, gain_two, grad_hidden_two, low, terms):
        grad = total_of(own, (first, second, third))
        back, gains = norm_back(hidden_two[...], gain_two[...], grad)
        value = cotangent[...].astype(F32) + back
        grad_hidden_two[...] = value
        low[...] = value.astype(BF)
        terms[...] = jnp.sum(gains, axis=0, keepdims=True)

    return body


def head_back(s):
    scale = HEAD_SIZE ** (-0.5)

    def body(*refs):
        blocks = refs[:8]
        out_weight, probs, linear, cosine, sine, mixed, query, key, value, gain_query, gain_key = refs[8:19]
        grads, out_grad, query_terms, key_terms, branch, grad_mixed, sems = refs[19:]
        for copy in gather_into(s, blocks, branch, sems):
            copy.wait()
        q, h = s.query, HEAD_SIZE
        query_sum = jnp.zeros((1, h), F32)
        key_sum = jnp.zeros((1, h), F32)
        for group in range(2):
            rows = pl.ds(group * s.group, s.group)
            grad_mixed[rows] = dot_last(branch[rows], out_weight[...]).astype(BF)
            cos, sin = cosine[rows], sine[rows]
            key_grad = jnp.zeros((s.group, h), F32)
            value_grad = jnp.zeros((s.group, h), F32)
            for r in range(s.heads):
                columns = slice(r * h, (r + 1) * h)
                prob = probs[group * s.heads + r]
                out = grad_mixed[rows, columns]
                grad_prob = dot_last(out, value[rows])
                inner = jnp.sum(prob * grad_prob, axis=-1, keepdims=True)
                grad_score = (prob * (grad_prob - inner)).astype(BF)
                value_grad = value_grad + dot_first(prob.astype(BF), out)
                key_grad = key_grad + dot_first(grad_score, query[rows, columns]) * scale
                turned = dot(grad_score, key[rows]) * scale
                back, terms = norm_back(
                    linear[rows, columns], gain_query[...], turned * cos - turn(turned) * sin
                )
                grads[rows, columns] = back.astype(BF)
                query_sum = query_sum + jnp.sum(terms, axis=0, keepdims=True)
            back, terms = norm_back(
                linear[rows, q : q + h], gain_key[...], key_grad * cos - turn(key_grad) * sin
            )
            grads[rows, q : q + h] = back.astype(BF)
            key_sum = key_sum + jnp.sum(terms, axis=0, keepdims=True)
            grads[rows, q + h :] = value_grad.astype(BF)
        query_terms[...] = query_sum
        key_terms[...] = key_sum
        for p in range(s.out_parts):
            columns = slice(p * s.cell, (p + 1) * s.cell)
            out_grad[:, columns] = dot_first(mixed[...], branch[:, columns]).astype(BF)

    return body


def input_back(s):
    def body(grads, weight, normed, gain_one, near, far, terms):
        step = 4 * HEAD_SIZE
        for n in range(s.width // step):
            columns = slice(n * step, (n + 1) * step)
            total = jnp.zeros((1, step), F32)
            for target, core in ((far, 1), (near, 0)):
                for group in range(2):
                    rows = pl.ds(group * s.group + core * s.half, s.half)
                    part = dot_last(grads[rows], weight[columns])
                    target[pl.ds(group * s.half, s.half), columns] = part.astype(BF)
                    total = total + jnp.sum(part * normed[rows, columns].astype(F32), axis=0, keepdims=True)
            terms[:, columns] = total / gain_one[:, columns]

    return body


def cut_row(s):
    return s.ring_rows * 3 // 4


def head_weight_grads(s):
    step = 4 * s.row * 4
    part, cut = 4 * s.row, cut_row(s)

    def body(place, normed, grads, out_grad, gain_rows, *refs):
        first, second, tiles = refs[:4], refs[4:8], refs[8]
        for kz in range(4):
            z = lax.rem(place[0] + kz, 4)
            for xl in range(2):
                at = pl.multiple_of((z * 2 + xl) * step, step)
                tile = dot_first(normed[:, pl.ds(at, step)], grads[...]).astype(BF)
                for y in range(4):
                    tiles[xl, y] = tile[y * part : (y + 1) * part]
            for ky in range(4):
                y = lax.rem(place[1] + ky, 4)
                f = z * 4 + y
                head, tail = first[ky], second[kz]
                head[kz, :part] = tiles[0, y]
                head[kz, part:] = tiles[1, y, : cut - part]
                tail[ky, : 2 * part - cut] = tiles[1, y, cut - part :]
                at = 2 * part - cut
                rows = pl.ds(pl.multiple_of(f * s.row, s.row), s.row)
                for p in range(s.out_parts):
                    tail[ky, at : at + s.row] = out_grad[rows, p * s.cell : (p + 1) * s.cell]
                    at += s.row
                tail[ky, at:] = gain_rows[f]

    return body


def plane_add(s):
    def body(*refs):
        outs = refs[8:]
        for part in range(2):
            group = refs[part * 4 : part * 4 + 4]
            for k in range(4):
                total = group[0][k].astype(F32)
                for ref in group[1:]:
                    total = total + ref[k].astype(F32)
                out = outs[part * 4 + k]
                out[...] = total.astype(out.dtype)

    return body


def input_end(s):
    def body(own, first, second, third, tokens, grad_hidden_two, gain_one, input_grad):
        back, _ = norm_back(tokens[...].astype(F32), gain_one[...], total_of(own, (first, second, third)))
        input_grad[...] = grad_hidden_two[...] + back

    return body


def output_end(s):
    def body(own, first, second, third, hidden_two, block_output):
        block_output[...] = (hidden_two[...] + total_of(own, (first, second, third))).astype(BF)

    return body


def pack_grads(s):
    cut = cut_row(s)

    def body(*refs):
        late, columns, lines, whole = refs[8:]
        whole[:cut] = total_of(refs[0], refs[1:4])
        whole[cut:] = total_of(refs[4], refs[5:8])
        out_end = s.ring_rows + s.out_rows
        for j in range(SHARE):
            columns[j, : s.row] = whole[j * s.row : (j + 1) * s.row].astype(BF)
            gains = whole[out_end + j : out_end + j + 1]
            columns[j, s.row : 2 * s.row] = jnp.broadcast_to(gains, (s.row, s.cell)).astype(BF)
            columns[j, 2 * s.row :] = late[j * s.mlp_rows : (j + 1) * s.mlp_rows]
        lines[: s.out_rows] = whole[s.ring_rows : out_end].astype(BF)
        lines[s.out_rows :] = late[SHARE * s.mlp_rows :]

    return body


def adam(weight, grad, first, second, rate, decay):
    first_new = BETA_ONE * first + (1.0 - BETA_ONE) * grad
    second_new = BETA_TWO * second + (1.0 - BETA_TWO) * grad * grad
    first_hat = first_new / (1.0 - BETA_ONE**STEP)
    second_hat = second_new / (1.0 - BETA_TWO**STEP)
    weight_new = weight - rate * (first_hat / (jnp.sqrt(second_hat) + ADAM_EPS) + decay * weight)
    return (weight_new, first_new, second_new)


def step_into(ins, outs, columns, grad, rate, decay):
    results = adam(ins[0][:, columns], grad.astype(F32), ins[1][:, columns], ins[2][:, columns], rate, decay)
    for out, value in zip(outs, results):
        out[:, columns] = value


def mlp_update(s):
    def body(*refs):
        columns, lines = refs[:2]
        gate, up, down = refs[2:5], refs[5:8], refs[8:11]
        outs = refs[11:]
        for j in range(SHARE):
            for ins, to, start in ((gate, outs[0:3], 0), (up, outs[3:6], s.hidden)):
                done = 0
                while done < s.hidden:
                    at = start + done
                    part, inside = at // s.cell, at % s.cell
                    size = min(s.cell - inside, s.hidden - done)
                    grad = columns[j, (part + 2) * s.row : (part + 3) * s.row, inside : inside + size]
                    own = slice(j * s.hidden + done, j * s.hidden + done + size)
                    step_into(ins, to, own, grad, MODEL_WIDTH ** (-0.5), DECAY)
                    done += size
        for p in range(s.out_parts):
            at = s.out_rows + p * s.down_row
            grad = lines[at : at + s.down_row]
            step_into(down, outs[6:9], slice(p * s.cell, (p + 1) * s.cell), grad, FF ** (-0.5), DECAY)

    return body


def head_update(s):
    def body(*refs):
        columns, lines = refs[:2]
        query, key, value, out, gains = refs[2:5], refs[5:8], refs[8:11], refs[11:14], refs[14:17]
        outs = refs[17:]
        rate = MODEL_WIDTH ** (-0.5)
        gain_grad = jnp.zeros((1, HEAD_SIZE), F32)
        for j in range(SHARE):
            start = 0
            for ins, to, size in ((query, outs[0:3], s.query), (key, outs[3:6], HEAD_SIZE), (value, outs[6:9], HEAD_SIZE)):
                grad = columns[j, : s.row, start : start + size]
                step_into(ins, to, slice(j * size, (j + 1) * size), grad, rate, DECAY)
                start += size
            gain_grad = gain_grad + columns[j, s.row : 2 * s.row, :HEAD_SIZE].astype(F32)[:1]
        out_rate = (TOK_DEV / (QUERY_HEADS * HEAD_SIZE)) ** 0.5
        for p in range(s.out_parts):
            grad = lines[p * s.row : (p + 1) * s.row]
            step_into(out, outs[9:12], slice(p * s.cell, (p + 1) * s.cell), grad, out_rate, DECAY)
        step_into(gains, outs[12:15], slice(0, HEAD_SIZE), gain_grad, 0.5, 0.0)

    return body


def layout(lengths, span_ids):
    span = TOK_DEV // 2
    table = jnp.concatenate([lengths[0], span_ids[0]])
    other = lax.ppermute(table, "xl", [(0, 1), (1, 0)])
    both = jnp.stack([table, other])
    sizes, spans = both[:, :2], both[:, 2:]
    chip = lax.axis_index("xh") * 2 + lax.axis_index("xl")
    core = lax.axis_index("c")
    offset = jnp.arange(2)[:, None, None] + 2 * jnp.arange(2)[None, None, :]
    place = ((chip + offset) % 4) // 2 * 2 + (core + jnp.arange(2)[None, :, None]) % 2
    block = (2 * place[..., None] + jnp.arange(2)).reshape(2, 8)
    owner = jnp.sum(jnp.where(block[:, :, None] == jnp.arange(8), spans[:, None, :], 0), axis=-1)
    slots = (owner[:, :, None] * span + jnp.arange(span)).reshape(2, -1)
    ends = jnp.cumsum(sizes, axis=1)
    passed = slots[:, :, None] >= ends[:, None, :]
    sequence = jnp.sum(passed.astype(jnp.int32), axis=-1)
    position = slots - jnp.sum(jnp.where(passed, sizes[:, None, :], 0), axis=-1)
    return slots, sequence, position


def local(
    tokens,
    cotangent,
    lengths,
    span_ids,
    query_weight,
    key_matrix,
    value_matrix,
    out_weight,
    gate_weight,
    up_weight,
    down_weight,
    norm_gains,
    query_first,
    key_first_moment,
    value_first_moment,
    out_first,
    gate_first,
    up_first,
    down_first,
    gains_first,
    query_second,
    key_second_moment,
    value_second_moment,
    out_second,
    gate_second,
    up_second,
    down_second,
    gains_second,
):
    s = Sizes()
    block = (s.block, s.width)
    half_rows = (s.group, s.width)

    def ring_scatter(near, arrived, name, after=()):
        own, *others = call(
            ring_add(s), [shape(block, F32)] + [shape(block)] * 3, [near, arrived], after=after, name=name + "_add"
        )
        arrived = [from_chip(piece, -OFFSETS[i + 1]) for i, piece in enumerate(others)]
        return [own] + arrived, others

    def padded(vector):
        return jnp.pad(vector, (0, HEAD_SIZE - s.gains))[None]

    gains_wide = jnp.broadcast_to(padded(norm_gains), (s.row, HEAD_SIZE))
    columns, lines = call(
        pack_weights(s),
        [shape((SHARE, 2 * s.row + s.mlp_rows, s.cell)), shape((s.out_rows + s.down_rows, s.cell))],
        [Far(query_weight), Far(key_matrix), Far(value_matrix), Far(out_weight), Far(gate_weight), Far(up_weight)]
        + [Far(down_weight), gains_wide],
        name="pack_weights",
    )
    columns = lax.all_to_all(columns, RING, 0, 0, tiled=True)
    lines = lax.ppermute(lines, AXES, row_route())

    slots, sequence, position = layout(lengths, span_ids)
    freq = THETA ** (-(2.0 * jnp.arange(HEAD_SIZE // 2, dtype=F32)) / HEAD_SIZE)
    angle = position.reshape(-1).astype(F32)[:, None] * freq
    cosine, sine = jnp.cos(angle), jnp.sin(angle)
    cosine = jnp.concatenate([cosine, cosine], axis=1)
    sine = jnp.concatenate([-sine, sine], axis=1)
    allowed = (sequence[:, :, None] == sequence[:, None, :]) & (slots[:, None, :] <= slots[:, :, None])
    bias = jnp.where(allowed, 0.0, -1e30).astype(F32)

    early, late = call(
        place_weights(s),
        [shape((s.early, s.cell)), shape((s.late, s.cell))],
        [columns, lines],
        after=[cosine, sine, bias],
        scratch=[pltpu.VMEM((s.row, s.cell), F32)],
        name="place_weights",
    )
    early = lax.all_gather(early, PLANE, axis=0)
    (tokens_then,) = tie([tokens], [columns], "tokens_then")
    input_near = from_chips(tokens_then)
    inputs = with_cores(input_near)
    (cotangent_then,) = tie([cotangent], [input_near[1]], "cotangent_then")
    upstream_near = from_chips(cotangent_then)
    (late,) = tie([late], [*inputs[1:], *upstream_near[1:]], "late_then")
    late = lax.all_gather(late, PLANE, axis=0)
    upstream = with_cores(upstream_near)

    gain_at = s.ring_rows + s.out_rows
    gains = early[:, gain_at : gain_at + SHARE, : s.gains].astype(F32)
    gains = gains.reshape(4, 4, 2, -1).transpose(0, 2, 1, 3).reshape(1, -1)
    gain_one = gains[:, : s.width]
    gain_two = gains[:, s.width : 2 * s.width]
    gain_query = gains[:, 2 * s.width : 2 * s.width + HEAD_SIZE]
    gain_key = gains[:, 2 * s.width + HEAD_SIZE :]

    eight = pltpu.SemaphoreType.DMA((8,))
    head_weight, out_slice, normed_one, linear, probs, query, key, value, mixed, near, far = call(
        head_forward(s),
        [
            Far(shape((s.width, s.cell))),
            Far(shape((s.query, s.width))),
            Far(shape((s.rows, s.width))),
            Far(shape((s.rows, s.query + HEAD_SIZE), F32)),
            Far(shape((2 * s.heads, s.group, s.group), F32)),
            shape((s.rows, s.query)),
            shape((s.rows, HEAD_SIZE)),
            shape((s.rows, HEAD_SIZE)),
            shape((s.rows, s.query)),
            shape(half_rows),
            Far(shape(half_rows)),
        ],
        [*[Far(v) for v in inputs], Far(early), Far(cosine), Far(sine), Far(bias), gain_one, gain_query, gain_key],
        flops=2 * s.rows * s.width * (s.cell + s.query),
        name="head_forward",
    )
    parts, _ = ring_scatter(near, from_core(far), "branch")
    hidden_two, normed_two = call(
        branch_end(s), [shape(block, F32), shape(block)], [*parts, tokens, gain_two], name="branch_end"
    )
    down, weight, grad_hidden = call(
        mlp_weights(s),
        [Far(shape((s.hidden, s.width))), Far(shape((s.width, 2 * s.hidden))), Far(shape((s.rows, s.hidden), F32))],
        [*upstream, Far(late)],
        any_first=8,
        scratch=[pltpu.VMEM((s.rows, s.width), BF), eight],
        flops=2 * s.rows * s.width * s.hidden,
        name="mlp_weights",
    )
    normed_blocks = with_cores(from_chips(normed_two))
    hidden, grads, far = call(
        mlp_forward_back(s),
        [Far(shape((s.rows, s.hidden))), Far(shape((s.rows, 2 * s.hidden))), shape(half_rows)],
        [*normed_blocks, weight, Far(grad_hidden)],
        any_first=9,
        scratch=[
            pltpu.VMEM((s.rows, s.width), BF),
            pltpu.VMEM((s.width, 2 * s.hidden), BF),
            eight,
            pltpu.SemaphoreType.DMA((s.hidden // HEAD_SIZE,)),
        ],
        flops=6 * s.rows * s.width * s.hidden,
        name="mlp_forward_back",
    )
    (near,) = call(
        mlp_near(s),
        [shape(half_rows)],
        [weight, Far(grads)],
        any_first=1,
        scratch=[pltpu.VMEM((s.width, 2 * s.hidden), BF), pltpu.SemaphoreType.DMA((s.width // (2 * HEAD_SIZE),))],
        flops=2 * s.rows * s.width * s.hidden,
        name="mlp_near",
    )
    parts, sent = ring_scatter(near, from_core(far), "mlp_back")
    (late_grad,) = call(
        mlp_weight_grads(s),
        [shape((16, s.late, s.cell))],
        [*normed_blocks, *upstream, Far(grads), Far(hidden)],
        any_first=16,
        any_out=True,
        after=sent,
        scratch=[
            pltpu.VMEM((s.rows, s.width), BF),
            pltpu.VMEM((s.rows, s.width), BF),
            pltpu.VMEM((16, s.late, s.cell), BF),
            eight,
            eight,
            pltpu.SemaphoreType.DMA((2,)),
        ],
        flops=6 * s.rows * s.width * s.hidden,
        name="mlp_weight_grads",
    )
    out_near, out_far = call(
        mlp_out(s),
        [shape(half_rows)] * 2,
        [Far(hidden), Far(down)],
        after=[late_grad],
        flops=2 * s.rows * s.width * s.hidden,
        name="mlp_out",
    )
    grad_hidden_two, grad_branch, gain_two_terms = call(
        mlp_back_end(s),
        [shape(block, F32), shape(block), shape((1, s.width), F32)],
        [*parts, cotangent, hidden_two, gain_two],
        after=[out_near],
        name="mlp_back_end",
    )
    (late_grad,) = tie([late_grad], [grad_branch], "late_grad_then")
    late_grad = lax.psum_scatter(late_grad.reshape(-1, s.cell), PLANE, scatter_dimension=0, tiled=True)
    branch_near = from_chips(grad_branch)
    out_arrived = from_core(out_far)
    branch_blocks = with_cores(branch_near)
    out_parts, out_sent = ring_scatter(out_near, out_arrived, "output", branch_near[1:])

    grads, out_grad, query_terms, key_terms = call(
        head_back(s),
        [
            shape((s.rows, s.cell)),
            shape((s.query, s.width)),
            shape((1, HEAD_SIZE), F32),
            shape((1, HEAD_SIZE), F32),
        ],
        [*branch_blocks, Far(out_slice), Far(probs), Far(linear), Far(cosine), Far(sine)]
        + [mixed, query, key, value, gain_query, gain_key],
        any_first=8,
        after=out_sent,
        scratch=[pltpu.VMEM((s.rows, s.width), BF), pltpu.VMEM((s.rows, s.query), BF), eight],
        hidden=True,
        name="head_back",
    )
    near, far, gain_one_terms = call(
        input_back(s),
        [shape(half_rows), shape(half_rows), shape((1, s.width), F32)],
        [grads, Far(head_weight), Far(normed_one), gain_one],
        hidden=True,
        name="input_back",
    )
    (block_output,) = call(output_end(s), [shape(block)], [*out_parts, hidden_two], name="output_end")
    (gain_one_terms,) = tie([gain_one_terms], [block_output], "gain_one_then")
    gain_terms = jnp.concatenate([gain_one_terms, gain_two_terms, query_terms, key_terms], axis=1)
    gain_terms = gain_terms.reshape(4, 2, 4, -1).transpose(0, 2, 1, 3).reshape(16, SHARE, s.gains)
    gain_rows = jnp.pad(gain_terms.astype(BF), ((0, 0), (0, s.row - SHARE), (0, s.cell - s.gains)))
    place = jnp.stack([lax.axis_index("z"), lax.axis_index("y")]).astype(jnp.int32)
    cut = cut_row(s)
    first, second = (4, cut, s.cell), (4, s.early - cut, s.cell)
    chunks = call(
        head_weight_grads(s),
        [shape(first)] * 4 + [shape(second)] * 4,
        [place, Far(normed_one), grads, out_grad, gain_rows],
        scalars=1,
        scratch=[pltpu.VMEM((2, 4, 4 * s.row, s.cell), BF)],
        flops=2 * s.rows * s.width * s.cell,
        name="head_weight_grads",
    )
    (far,) = tie([far], [chunks[0]], "input_far_then")
    parts, sent = ring_scatter(near, from_core(far), "input")
    (input_grad,) = call(
        input_end(s), [shape(block, F32)], [*parts, tokens, grad_hidden_two, gain_one], name="input_end"
    )
    heads = [chunks[0]] + [from_plane(chunks[k], "y", -k) for k in range(1, 4)]
    tails = [chunks[4]] + [from_plane(chunks[4 + k], "z", -k) for k in range(1, 4)]
    sums = call(
        plane_add(s),
        ([shape(first[1:], F32)] + [shape(first[1:])] * 3) + ([shape(second[1:], F32)] + [shape(second[1:])] * 3),
        [*heads, *tails],
        after=sent,
        name="plane_add",
    )
    heads = [sums[0]] + [from_plane(sums[k], "z", -k) for k in range(1, 4)]
    tails = [sums[4]] + [from_plane(sums[4 + k], "y", -k) for k in range(1, 4)]
    columns, lines = call(
        pack_grads(s),
        [shape((SHARE, 2 * s.row + s.mlp_rows, s.cell)), shape((s.out_rows + s.down_rows, s.cell))],
        [*heads, *tails, Far(late_grad)],
        after=[input_grad, block_output],
        scratch=[pltpu.VMEM((s.early, s.cell), F32)],
        name="pack_grads",
    )
    columns = lax.all_to_all(columns, RING, 0, 0, tiled=True)
    lines = lax.ppermute(lines, AXES, [(to, own) for own, to in row_route()])
    head_states = [
        (query_weight, query_first, query_second),
        (key_matrix, key_first_moment, key_second_moment),
        (value_matrix, value_first_moment, value_second_moment),
        (out_weight, out_first, out_second),
        (padded(norm_gains), padded(gains_first), padded(gains_second)),
    ]
    head_new = call(
        head_update(s),
        [shape(a.shape, F32) for group in head_states for a in group],
        [columns, lines] + [a for group in head_states for a in group],
        name="head_update",
    )
    mlp_states = [
        (gate_weight, gate_first, gate_second),
        (up_weight, up_first, up_second),
        (down_weight, down_first, down_second),
    ]
    mlp_new = call(
        mlp_update(s),
        [shape(a.shape, F32) for group in mlp_states for a in group],
        [columns, lines] + [a for group in mlp_states for a in group],
        name="mlp_update",
    )
    gains_new = tuple(value[0, : s.gains] for value in head_new[12:])
    return (block_output, input_grad, *head_new[:12], *mlp_new, *gains_new)


def solution(mesh):
    fine = Mesh(mesh.devices.reshape(SIZES), AXES)
    matrix, vector, grouped = P(AXES, None), P(AXES), P(("z", "xl", "y"), None)
    states = (matrix,) * 7 + (vector,)
    return jax.shard_map(
        local,
        mesh=fine,
        in_specs=(matrix, matrix, grouped, grouped) + states * 3,
        out_specs=(matrix, matrix) + (matrix,) * 21 + (vector,) * 3,
        check_vma=False,
    )
```

```python
import math

import jax
import jax.numpy as jnp
import ml_dtypes
import numpy as np
from jax import lax
from jax.experimental import pallas as pl
from jax.experimental.pallas import tpu as pltpu
from jax.sharding import Mesh
from jax.sharding import PartitionSpec as P

MODEL_WIDTH = 2048
QUERY_HEADS = 16
KEY_VALUE_HEADS = 8
HEAD_SIZE = 128
FF = 6144
TOK_DEV = 128
STEP = 10

EPS = 1e-06
THETA = 1000000.0
BETA_ONE = 0.9
BETA_TWO = 0.95
ADAM_EPS = 1e-08
DECAY = 0.1

AXES = ("z", "xl", "y", "xh", "c")
SIZES = (4, 2, 4, 2, 2)
RING = ("xl", "xh", "c")
PLANE = ("z", "y")
CHIPS = ("xl", "xh")
SHARE = 8
OFFSETS = (0, 2, 1, 3)
BF = jnp.bfloat16
F32 = jnp.float32


def chip_number(x):
    return (x % 2) * 2 + x // 2


def from_chip(value, offset):
    pairs = [(chip_number((x + offset) % 4), chip_number(x)) for x in range(4)]
    return lax.ppermute(value, CHIPS, pairs)


def from_core(value):
    return lax.ppermute(value, "c", [(0, 1), (1, 0)])


def row_route():
    pairs = []
    for z in range(4):
        for xl in range(2):
            for y in range(4):
                for xh in range(2):
                    for c in range(2):
                        own = (((z * 2 + xl) * 4 + y) * 2 + xh) * 2 + c
                        part = 2 * z + xl
                        to = (((y * 2 + part // 4) * 4 + (xh * 2 + c)) * 2 + (part // 2) % 2) * 2 + part % 2
                        pairs.append((own, to))
    return pairs


def from_chips(block):
    return [block] + [from_chip(block, offset) for offset in OFFSETS[1:]]


def with_cores(near):
    return near + [from_core(value) for value in near]


def row_blocks():
    return [group * 4 + core * 2 + chip for core in range(2) for group in range(2) for chip in range(2)]


def dot(left, right):
    return jnp.dot(left, right, preferred_element_type=F32)


def dot_last(left, right):
    return lax.dot_general(left, right, (((1,), (1,)), ((), ())), preferred_element_type=F32)


def dot_first(left, right):
    return lax.dot_general(left, right, (((0,), (0,)), ((), ())), preferred_element_type=F32)


def inverse_rms(values):
    return lax.rsqrt(jnp.mean(values * values, axis=-1, keepdims=True) + EPS)


class Arriving:
    def __init__(self, source, buffer, sem):
        self.buffer, self.shape, self.here = buffer, buffer.shape, False
        self.copy = pltpu.make_async_copy(source, buffer, sem)

    def start(self):
        self.copy.start()

    def wait(self):
        if not self.here:
            self.copy.wait()
        self.here = True

    def __getitem__(self, index):
        self.wait()
        return self.buffer[index]


class Leaving:
    def __init__(self, buffer, target, sem):
        self.buffer, self.shape, self.sent = buffer, buffer.shape, False
        self.copy = pltpu.make_async_copy(buffer, target, sem)

    def __getitem__(self, index):
        return self.buffer[index]

    def __setitem__(self, index, value):
        self.buffer[index] = value

    def send(self):
        self.sent = True
        self.copy.start()


def bytes_of(values):
    return sum(math.prod(v.shape) * jnp.dtype(v.dtype).itemsize for v in values)


class Far:
    def __init__(self, value, later=False):
        self.value, self.later = value, later


HBM = pl.BlockSpec(memory_space=pltpu.HBM)
ANY = pl.BlockSpec(memory_space=pl.ANY)


def order_specs(after):
    return [HBM if isinstance(a, Far) else ANY for a in after], [a.value if isinstance(a, Far) else a for a in after]


def call(body, outs, args, after=(), scratch=(), flops=0, any_first=0, any_out=False, scalars=0, near=(), hidden=False, large=False, mark=False, name=None):
    if mark:
        outs = [*outs, shape((8, 128), F32)]
    after_specs, after = order_specs(after)
    far_in = [isinstance(a, Far) for a in args]
    later = [isinstance(a, Far) and a.later for a in args]
    far_out = [isinstance(o, Far) for o in outs]
    args = [a.value if isinstance(a, Far) else a for a in args]
    outs = [o.value if isinstance(o, Far) else o for o in outs]
    size = bytes_of((*args, *outs))
    held = bytes_of(args[any_first:]) + bytes_of(() if any_out else outs)
    held += bytes_of([v for v in scratch if v.memory_space == pltpu.VMEM])
    moved = [v for v, far in zip((*args, *outs), far_in + far_out) if far]
    n_in, n_out, n_move = len(args), len(outs), len(moved)

    def run(*refs):
        ins, refs = list(refs[:n_in]), refs[n_in + len(after) :]
        results, refs = list(refs[:n_out]), refs[n_out:]
        own, refs = refs[: len(scratch)], refs[len(scratch) :]
        buffers, sems = list(refs[:n_move]), list(refs[n_move:])
        for i, far in enumerate(far_in):
            if far:
                ins[i] = Arriving(ins[i], buffers.pop(0), sems.pop(0))
                if not later[i]:
                    ins[i].start()
        for i, far in enumerate(far_out):
            if far:
                results[i] = Leaving(buffers.pop(0), results[i], sems.pop(0))
        if mark:
            results[-1][...] = jnp.zeros((8, 128), F32)
        body(*ins, *(results[:-1] if mark else results), *own)
        for value in ins:
            if isinstance(value, Arriving):
                value.wait()
        for value in results:
            if isinstance(value, Leaving) and not value.sent:
                value.send()
        for value in results:
            if isinstance(value, Leaving):
                value.copy.wait()

    def spec(far):
        return HBM if far else pl.BlockSpec(memory_space=pltpu.VMEM)

    in_specs = [spec(far or (i < any_first and i not in near)) for i, far in enumerate(far_in)]
    in_specs[:scalars] = [pl.BlockSpec(memory_space=pltpu.SMEM)] * scalars

    return pl.pallas_call(
        run,
        out_shape=tuple(outs),
        in_specs=in_specs + after_specs,
        out_specs=tuple(spec(far or (any_out and i == 0)) for i, far in enumerate(far_out)),
        scratch_shapes=list(scratch)
        + [pltpu.VMEM(v.shape, v.dtype) for v in moved]
        + [pltpu.SemaphoreType.DMA for _ in moved],
        compiler_params=pltpu.CompilerParams(vmem_limit_bytes=large * 2**20 if large else held + 12 * 2**20),
        cost_estimate=pl.CostEstimate(flops=flops, bytes_accessed=0 if hidden else size, transcendentals=0),
        name=name,
    )(*args, *after)


def tie(values, after, name, spec=ANY):
    count = len(values)
    after_specs, after = order_specs(after)

    def body(*refs):
        pass

    return pl.pallas_call(
        body,
        out_shape=tuple(jax.ShapeDtypeStruct(v.shape, v.dtype) for v in values),
        in_specs=[spec] * count + after_specs,
        out_specs=tuple(spec for _ in values),
        input_output_aliases={i: i for i in range(count)},
        name=name,
    )(*values, *after)


def shape(dims, dtype=BF):
    return jax.ShapeDtypeStruct(tuple(dims), dtype)


class Sizes:
    def __init__(self):
        self.width = MODEL_WIDTH
        self.heads = QUERY_HEADS // SHARE
        self.query = self.heads * HEAD_SIZE
        self.cell = self.query + 2 * HEAD_SIZE
        self.hidden = FF // SHARE
        self.row = MODEL_WIDTH // 128
        self.down_row = FF // 128
        self.out_parts = self.width // self.cell
        self.mlp_parts = 2 * self.hidden // self.cell
        self.ring_rows = SHARE * self.row
        self.mlp_rows = self.mlp_parts * self.row
        self.out_rows = self.out_parts * self.row
        self.down_rows = self.out_parts * self.down_row
        self.early = self.ring_rows + self.out_rows + self.row
        self.late = SHARE * self.mlp_rows + self.down_rows
        self.gains = (2 * MODEL_WIDTH + 2 * HEAD_SIZE) // 128
        self.block = TOK_DEV
        self.rows = 8 * TOK_DEV
        self.group = 4 * TOK_DEV
        self.half = 2 * TOK_DEV


def pack_weights(s):
    def body(query, key, value, out, gate, up, down, gains, columns, lines):
        for j in range(SHARE):
            q, h = s.query, HEAD_SIZE
            columns[j, : s.row, :q] = query[:, j * q : (j + 1) * q].astype(BF)
            columns[j, : s.row, q : q + h] = key[:, j * h : (j + 1) * h].astype(BF)
            columns[j, : s.row, q + h :] = value[:, j * h : (j + 1) * h].astype(BF)
            for source, start in ((gate, 0), (up, s.hidden)):
                done = 0
                while done < s.hidden:
                    at = start + done
                    part, inside = at // s.cell, at % s.cell
                    size = min(s.cell - inside, s.hidden - done)
                    columns[j, s.row * (1 + part) : s.row * (2 + part), inside : inside + size] = source[
                        :, j * s.hidden + done : j * s.hidden + done + size
                    ].astype(BF)
                    done += size
            columns[j, s.row + s.mlp_rows :, :] = jnp.zeros((s.row, s.cell), BF)
            columns[j, s.row + s.mlp_rows :, : s.gains] = jnp.broadcast_to(gains[...], (s.row, s.gains)).astype(BF)
        for p in range(s.out_parts):
            lines[p * s.row : (p + 1) * s.row] = out[:, p * s.cell : (p + 1) * s.cell].astype(BF)
            at = s.out_rows + p * s.down_row
            lines[at : at + s.down_row] = down[:, p * s.cell : (p + 1) * s.cell].astype(BF)

    return body


def place_weights(s):
    def body(columns, lines, early, late, table):
        gain_at = s.row + s.mlp_rows
        table[...] = jnp.zeros_like(table)
        for j in range(SHARE):
            early[j * s.row : (j + 1) * s.row] = columns[j, : s.row]
            late[j * s.mlp_rows : (j + 1) * s.mlp_rows] = columns[j, s.row : gain_at]
            table[j : j + 1] = columns[j, gain_at : gain_at + s.row].astype(F32)[:1]
        early[s.ring_rows : s.ring_rows + s.out_rows] = lines[: s.out_rows]
        early[s.ring_rows + s.out_rows :] = table[...].astype(BF)
        late[SHARE * s.mlp_rows :] = lines[s.out_rows :]

    return body


def fill_head_weight(s, early, target):
    part = 4 * s.row
    for z in range(4):
        for xl in range(2):
            for y in range(4):
                at = ((z * 2 + xl) * 4 + y) * part
                target[at : at + part] = early[z * 4 + y, xl * part : (xl + 1) * part]


def fill_out_weight(s, early, target):
    for f in range(16):
        for p in range(s.out_parts):
            at = s.ring_rows + p * s.row
            target[f * s.row : (f + 1) * s.row, p * s.cell : (p + 1) * s.cell] = early[f, at : at + s.row]


def turn(value):
    return pltpu.roll(value, HEAD_SIZE // 2, 1)


def head_forward(s):
    scale = HEAD_SIZE ** (-0.5)

    def body(*refs):
        blocks = refs[:8]
        early, cosine, sine, bias, gain_one, gain_query, gain_key = refs[8:15]
        weight, out_weight, normed, linear, probs, query, key, value, mixed, near, far = refs[15:]
        for ref, at in zip(blocks, row_blocks()):
            wide = ref[...].astype(F32)
            normed[at * s.block : (at + 1) * s.block] = (wide * inverse_rms(wide) * gain_one[...]).astype(BF)
        normed.send()
        fill_head_weight(s, early, weight)
        weight.send()
        q, h = s.query, HEAD_SIZE
        for group in range(2):
            rows = pl.ds(group * s.group, s.group)
            lin = dot(normed[rows], weight[...])
            linear[rows] = lin[:, : q + h]
            value[rows] = lin[:, q + h :].astype(BF)
            cos, sin = cosine[rows], sine[rows]

            def turned(part, gain):
                part = part * inverse_rms(part) * gain[...]
                return (part * cos + turn(part) * sin).astype(BF)

            key[rows] = turned(lin[:, q : q + h], gain_key)
            for r in range(s.heads):
                query[rows, r * h : (r + 1) * h] = turned(lin[:, r * h : (r + 1) * h], gain_query)
        linear.send()
        fill_out_weight(s, early, out_weight)
        out_weight.send()
        for group in range(2):
            rows = pl.ds(group * s.group, s.group)
            for r in range(s.heads):
                score = dot_last(query[rows, r * h : (r + 1) * h], key[rows]) * scale + bias[group]
                expo = jnp.exp(score - jnp.max(score, axis=-1, keepdims=True))
                prob = expo * (1.0 / jnp.sum(expo, axis=-1, keepdims=True))
                probs[group * s.heads + r] = prob
                mixed[rows, r * h : (r + 1) * h] = dot(prob.astype(BF), value[rows]).astype(BF)
        probs.send()
        for target, core in ((far, 1), (near, 0)):
            for group in range(2):
                rows = pl.ds(group * s.group + core * s.half, s.half)
                target[pl.ds(group * s.half, s.half)] = dot(mixed[rows], out_weight[...]).astype(BF)
            if core:
                far.send()

    return body


def ring_add(s):
    def body(near, arrived, own, *others):
        own[...] = near[: s.block].astype(F32) + arrived[: s.block].astype(F32)
        for i, other in enumerate(others):
            rows = pl.ds((i + 1) * s.block, s.block)
            other[...] = (near[rows].astype(F32) + arrived[rows].astype(F32)).astype(BF)

    return body


def total_of(own, parts):
    total = own[...]
    for part in parts:
        total = total + part[...].astype(F32)
    return total


def branch_end(s):
    def body(own, first, second, third, tokens, gain_two, hidden_two, normed):
        value = tokens[...].astype(F32) + total_of(own, (first, second, third))
        hidden_two[...] = value
        normed[...] = (value * inverse_rms(value) * gain_two[...]).astype(BF)

    return body


def norm_back(values, gain, grad):
    scale = inverse_rms(values)
    normalized = values * scale
    inner = grad * gain
    back = scale * inner - normalized * scale * jnp.mean(inner * normalized, axis=-1, keepdims=True)
    return back, grad * normalized


def gather_into(s, blocks, buffer, sems):
    copies = {}
    for i, (ref, at) in enumerate(zip(blocks, row_blocks())):
        copies[at] = pltpu.make_async_copy(ref, buffer.at[pl.ds(at * s.block, s.block)], sems.at[i])
        copies[at].start()
    return copies


def wait_all(copies):
    for copy in copies.values():
        copy.wait()


def mlp_block(s):
    step = 2 * HEAD_SIZE

    def body(*refs):
        blocks, upstream_blocks, late = refs[:8], refs[8:16], refs[16]
        down, hidden, grads, far, near, normed, upstream, weight, grad_hidden, sems, up_sems = refs[17:]
        copies = gather_into(s, upstream_blocks, upstream, up_sems)
        late.start()
        normed_copies = gather_into(s, blocks, normed, sems)
        for f in range(16):
            for p in range(s.out_parts):
                start = SHARE * s.mlp_rows + p * s.down_row
                down[f * s.down_row : (f + 1) * s.down_row, p * s.cell : (p + 1) * s.cell] = late[
                    f, start : start + s.down_row
                ]
        down.send()
        wait_all(copies)
        for n in range(s.hidden // step):
            columns = slice(n * step, (n + 1) * step)
            grad_hidden[:, columns] = dot_last(upstream[...], down[columns])
        for f in range(16):
            z, y = divmod(f, 4)
            for j in range(SHARE):
                xl, part = divmod(j, 4)
                at = (((z * 2 + xl) * 4 + y) * 4 + part) * s.row
                for p in range(s.mlp_parts):
                    start = j * s.mlp_rows + p * s.row
                    weight[at : at + s.row, p * s.cell : (p + 1) * s.cell] = late[f, start : start + s.row]
        wait_all(normed_copies)
        for n in range(s.hidden // step):
            columns = slice(n * step, (n + 1) * step)
            second = slice(s.hidden + n * step, s.hidden + (n + 1) * step)
            gate = dot(normed[...], weight[:, columns])
            up = dot(normed[...], weight[:, second])
            sigma = jax.nn.sigmoid(gate)
            active = gate * sigma
            hidden[:, columns] = (active * up).astype(BF)
            grad = grad_hidden[:, columns]
            grads[:, columns] = (grad * up * (sigma * (1.0 + gate * (1.0 - sigma)))).astype(BF)
            grads[:, second] = (grad * active).astype(BF)
        hidden.send()
        grads.send()
        for target, core in ((far, 1), (near, 0)):
            for n in range(s.width // step):
                columns = slice(n * step, (n + 1) * step)
                for group in range(2):
                    rows = pl.ds(group * s.group + core * s.half, s.half)
                    part = dot_last(grads[rows], weight[columns])
                    target[pl.ds(group * s.half, s.half), columns] = part.astype(BF)
            target.send()

    return body


def mlp_weight_grads(s):
    step = 4 * s.row * 4

    def body(*refs):
        normed_blocks, blocks = refs[:8], refs[8:16]
        grads, hidden, target, normed, upstream, made, normed_sems, sems, out_sems = refs[16:]
        normed_copies = gather_into(s, normed_blocks, normed, normed_sems)
        copies = gather_into(s, blocks, upstream, sems)
        leaving = []
        grads.start()
        hidden.start()
        wait_all(normed_copies)
        for z in range(4):
            for xl in range(2):
                at = (z * 2 + xl) * step
                tile = dot_first(normed[:, at : at + step], grads[...]).astype(BF)
                for y in range(4):
                    for part in range(4):
                        line = (y * 4 + part) * s.row
                        for p in range(s.mlp_parts):
                            start = (xl * 4 + part) * s.mlp_rows + p * s.row
                            made[z * 4 + y, start : start + s.row] = tile[
                                line : line + s.row, p * s.cell : (p + 1) * s.cell
                            ]
            if z % 2:
                pair = z // 2
                if pair == 0:
                    wait_all(copies)
                wide = s.hidden // 2
                columns = hidden[:, pair * wide : (pair + 1) * wide]
                for p in range(s.out_parts):
                    tile = dot_first(columns, upstream[:, p * s.cell : (p + 1) * s.cell]).astype(BF)
                    for f in range(8):
                        start = SHARE * s.mlp_rows + p * s.down_row
                        made[pair * 8 + f, start : start + s.down_row] = tile[f * s.down_row : (f + 1) * s.down_row]
                half = pl.ds(pair * 8, 8)
                copy = pltpu.make_async_copy(made.at[half], target.at[half], out_sems.at[pair])
                copy.start()
                leaving.append(copy)
        for copy in leaving:
            copy.wait()

    return body


def mlp_out(s):
    step = 4 * HEAD_SIZE

    def body(hidden, down, near, far):
        for target, core in ((far, 1), (near, 0)):
            for group in range(2):
                rows = pl.ds(group * s.group + core * s.half, s.half)
                for n in range(s.width // step):
                    columns = slice(n * step, (n + 1) * step)
                    target[pl.ds(group * s.half, s.half), columns] = dot(hidden[rows], down[:, columns]).astype(BF)

    return body


def mlp_back_end(s):
    def body(own, first, second, third, cotangent, hidden_two, gain_two, grad_hidden_two, low, terms):
        grad = total_of(own, (first, second, third))
        back, gains = norm_back(hidden_two[...], gain_two[...], grad)
        value = cotangent[...].astype(F32) + back
        grad_hidden_two[...] = value
        low[...] = value.astype(BF)
        terms[...] = jnp.sum(gains, axis=0, keepdims=True)

    return body


def out_weight_grads(s):
    def body(*refs):
        mixed, out_grad, branch, sems = refs[8:]
        wait_all(gather_into(s, refs[:8], branch, sems))
        for p in range(s.out_parts):
            columns = slice(p * s.cell, (p + 1) * s.cell)
            out_grad[:, columns] = dot_first(mixed[...], branch[:, columns]).astype(BF)

    return body


def head_back(s):
    scale = HEAD_SIZE ** (-0.5)

    def body(*refs):
        blocks = refs[:8]
        out_weight, probs, linear, cosine, sine, query, key, value, normed, weight = refs[8:18]
        gain_query, gain_key, gain_one, gain_two_terms, owner, lane = refs[18:24]
        near, far, owned_rows, branch, grad_mixed, grads, gain_row, sems = refs[24:]
        copies = gather_into(s, blocks, branch, sems)
        for later in (out_weight, probs, linear, cosine, sine, query, key, value, normed, weight):
            later.start()
        q, h = s.query, HEAD_SIZE
        query_sum = jnp.zeros((1, h), F32)
        key_sum = jnp.zeros((1, h), F32)
        for group in range(2):
            rows = pl.ds(group * s.group, s.group)
            for at in range(group * 4, group * 4 + 4):
                copies[at].wait()
            grad_mixed[rows] = dot_last(branch[rows], out_weight[...]).astype(BF)
            cos, sin = cosine[rows], sine[rows]
            key_grad = jnp.zeros((s.group, h), F32)
            value_grad = jnp.zeros((s.group, h), F32)
            for r in range(s.heads):
                columns = slice(r * h, (r + 1) * h)
                prob = probs[group * s.heads + r]
                out = grad_mixed[rows, columns]
                grad_prob = dot_last(out, value[rows])
                inner = jnp.sum(prob * grad_prob, axis=-1, keepdims=True)
                grad_score = (prob * (grad_prob - inner)).astype(BF)
                value_grad = value_grad + dot_first(prob.astype(BF), out)
                key_grad = key_grad + dot_first(grad_score, query[rows, columns]) * scale
                turned = dot(grad_score, key[rows]) * scale
                back, terms = norm_back(
                    linear[rows, columns], gain_query[...], turned * cos - turn(turned) * sin
                )
                grads[rows, columns] = back.astype(BF)
                query_sum = query_sum + jnp.sum(terms, axis=0, keepdims=True)
            back, terms = norm_back(
                linear[rows, q : q + h], gain_key[...], key_grad * cos - turn(key_grad) * sin
            )
            grads[rows, q : q + h] = back.astype(BF)
            key_sum = key_sum + jnp.sum(terms, axis=0, keepdims=True)
            grads[rows, q + h :] = value_grad.astype(BF)
        wide = 4 * HEAD_SIZE
        for n in range(s.width // wide):
            columns = slice(n * wide, (n + 1) * wide)
            total = jnp.zeros((1, wide), F32)
            for target, core in ((far, 1), (near, 0)):
                for group in range(2):
                    rows = pl.ds(group * s.group + core * s.half, s.half)
                    part = dot_last(grads[rows], weight[columns])
                    target[pl.ds(group * s.half, s.half), columns] = part.astype(BF)
                    total = total + jnp.sum(part * normed[rows, columns].astype(F32), axis=0, keepdims=True)
            gain_row[:, columns] = total / gain_one[:, columns]
        far.send()
        near.send()
        gain_row[:, s.width : 2 * s.width] = gain_two_terms[...]
        gain_row[:, 2 * s.width : 2 * s.width + h] = query_sum
        gain_row[:, 2 * s.width + h :] = key_sum
        owned = dot((owner[...].astype(F32) * gain_row[...]).astype(BF), lane[...])
        for o in range(128):
            owned_rows[o, :, s.cell :] = jnp.broadcast_to(owned[o : o + 1], (s.row, h)).astype(BF)
        step = 16 * s.row
        for n in range(8):
            tile = dot_first(normed[:, n * step : (n + 1) * step], grads[...]).astype(BF)
            owned_rows[n * 16 : (n + 1) * 16, :, : s.cell] = tile.reshape(16, s.row, s.cell)

    return body


def plane_sum(s):
    def body(parts, total):
        value = parts[0].astype(F32)
        for f in range(1, 16):
            value = value + parts[f].astype(F32)
        total[...] = value.astype(BF)

    return body


def input_end(s):
    def body(own, first, second, third, tokens, grad_hidden_two, gain_one, input_grad):
        back, _ = norm_back(tokens[...].astype(F32), gain_one[...], total_of(own, (first, second, third)))
        input_grad[...] = grad_hidden_two[...] + back

    return body


def output_end(s):
    def body(own, first, second, third, hidden_two, block_output):
        block_output[...] = (hidden_two[...] + total_of(own, (first, second, third))).astype(BF)

    return body


def adam(weight, grad, first, second, rate, decay):
    first_new = BETA_ONE * first + (1.0 - BETA_ONE) * grad
    second_new = BETA_TWO * second + (1.0 - BETA_TWO) * grad * grad
    first_hat = first_new / (1.0 - BETA_ONE**STEP)
    second_hat = second_new / (1.0 - BETA_TWO**STEP)
    weight_new = weight - rate * (first_hat / (jnp.sqrt(second_hat) + ADAM_EPS) + decay * weight)
    return (weight_new, first_new, second_new)


def step_into(ins, outs, columns, grad, rate, decay):
    results = adam(ins[0][:, columns], grad.astype(F32), ins[1][:, columns], ins[2][:, columns], rate, decay)
    for out, value in zip(outs, results):
        out[:, columns] = value


def split_refs(refs, first, count):
    ins = [refs[first + 3 * i : first + 3 * i + 3] for i in range(count)]
    outs = [refs[first + 3 * (count + i) : first + 3 * (count + i) + 3] for i in range(count)]
    return ins, outs


def send_all(outs):
    for out in outs:
        out.send()


def head_update(s):
    def body(*refs):
        owned, lines = refs[:2]
        ins, outs = split_refs(refs, 2, 5)
        rate = MODEL_WIDTH ** (-0.5)
        out_rate = (TOK_DEV / (QUERY_HEADS * HEAD_SIZE)) ** 0.5
        gain_grad = jnp.zeros((s.row, HEAD_SIZE), F32)
        for j in range(SHARE):
            xl, part = divmod(j, 4)
            grad = jnp.zeros((s.row, s.cell), F32)
            for z in range(4):
                for y in range(4):
                    source = ((z * 2 + xl) * 4 + y) * 4 + part
                    grad = grad + owned[source, :, : s.cell].astype(F32)
                    gain_grad = gain_grad + owned[source, :, s.cell :].astype(F32)
            start = 0
            for i, size in enumerate((s.query, HEAD_SIZE, HEAD_SIZE)):
                columns = slice(j * size, (j + 1) * size)
                step_into(ins[i], outs[i], columns, grad[:, start : start + size], rate, DECAY)
                start += size
        for i in range(3):
            send_all(outs[i])
        for p in range(s.out_parts):
            columns = slice(p * s.cell, (p + 1) * s.cell)
            step_into(ins[3], outs[3], columns, lines[:, columns], out_rate, DECAY)
        send_all(outs[3])
        step_into(ins[4], outs[4], slice(0, s.gains), gain_grad[:1, : s.gains], 0.5, 0.0)

    return body


def mlp_update(s):
    def body(*refs):
        columns, lines = refs[:2]
        ins, outs = split_refs(refs, 2, 3)
        for i, start in ((0, 0), (1, s.hidden)):
            for j in range(SHARE):
                done = 0
                while done < s.hidden:
                    at = start + done
                    part, inside = at // s.cell, at % s.cell
                    size = min(s.cell - inside, s.hidden - done)
                    grad = columns[j, part * s.row : (part + 1) * s.row, inside : inside + size]
                    own = slice(j * s.hidden + done, j * s.hidden + done + size)
                    step_into(ins[i], outs[i], own, grad, MODEL_WIDTH ** (-0.5), DECAY)
                    done += size
            send_all(outs[i])
        for p in range(s.out_parts):
            grad = lines[p * s.down_row : (p + 1) * s.down_row]
            step_into(ins[2], outs[2], slice(p * s.cell, (p + 1) * s.cell), grad, FF ** (-0.5), DECAY)

    return body


def layout(table):
    span = TOK_DEV // 2
    other = lax.ppermute(table, "xl", [(0, 1), (1, 0)])
    both = jnp.stack([table, other])
    sizes, spans = both[:, :2], both[:, 2:]
    chip = lax.axis_index("xh") * 2 + lax.axis_index("xl")
    core = lax.axis_index("c")
    offset = jnp.arange(2)[:, None, None] + 2 * jnp.arange(2)[None, None, :]
    place = ((chip + offset) % 4) // 2 * 2 + (core + jnp.arange(2)[None, :, None]) % 2
    block = (2 * place[..., None] + jnp.arange(2)).reshape(2, 8)
    owner = jnp.sum(jnp.where(block[:, :, None] == jnp.arange(8), spans[:, None, :], 0), axis=-1)
    slots = (owner[:, :, None] * span + jnp.arange(span)).reshape(2, -1)
    ends = jnp.cumsum(sizes, axis=1)
    passed = slots[:, :, None] >= ends[:, None, :]
    sequence = jnp.sum(passed.astype(jnp.int32), axis=-1)
    position = slots - jnp.sum(jnp.where(passed, sizes[:, None, :], 0), axis=-1)
    return slots, sequence, position


def local(
    tokens,
    cotangent,
    lengths,
    span_ids,
    query_weight,
    key_matrix,
    value_matrix,
    out_weight,
    gate_weight,
    up_weight,
    down_weight,
    norm_gains,
    query_first,
    key_first_moment,
    value_first_moment,
    out_first,
    gate_first,
    up_first,
    down_first,
    gains_first,
    query_second,
    key_second_moment,
    value_second_moment,
    out_second,
    gate_second,
    up_second,
    down_second,
    gains_second,
):
    s = Sizes()
    block = (s.block, s.width)
    half_rows = (s.group, s.width)

    def ring_scatter(near, arrived, name, after=()):
        own, *others = call(
            ring_add(s), [shape(block, F32)] + [shape(block)] * 3, [near, arrived], after=after, name=name + "_add"
        )
        arrived = [from_chip(piece, -OFFSETS[i + 1]) for i, piece in enumerate(others)]
        return [own] + arrived, others

    columns, lines = call(
        pack_weights(s),
        [shape((SHARE, 2 * s.row + s.mlp_rows, s.cell)), shape((s.out_rows + s.down_rows, s.cell))],
        [Far(query_weight), Far(key_matrix), Far(value_matrix), Far(out_weight), Far(gate_weight), Far(up_weight)]
        + [Far(down_weight), norm_gains[None]],
        large=54,
        name="pack_weights",
    )
    columns = lax.all_to_all(columns, RING, 0, 0, tiled=True)
    lines = lax.ppermute(lines, AXES, row_route())

    count = 128 * s.gains
    owner = np.asarray(np.arange(count)[None] // s.gains == np.arange(128)[:, None], ml_dtypes.bfloat16)
    lane = np.asarray(np.arange(count)[:, None] % s.gains == np.arange(HEAD_SIZE)[None], ml_dtypes.bfloat16)

    early, late, mark = call(
        place_weights(s),
        [shape((s.early, s.cell)), shape((s.late, s.cell))],
        [columns, lines],
        scratch=[pltpu.VMEM((s.row, s.cell), F32)],
        mark=True,
        name="place_weights",
    )
    early = lax.all_gather(early, PLANE, axis=0)
    (tokens_then,) = tie([tokens], [mark], "tokens_then", HBM)
    input_near = from_chips(tokens_then)
    inputs = with_cores(input_near)
    (cotangent_then,) = tie([cotangent], [Far(input_near[1])], "cotangent_then", HBM)
    upstream_near = from_chips(cotangent_then)
    (table,) = tie([jnp.concatenate([lengths[0], span_ids[0]])], [input_near[1]], "table_then")
    slots, sequence, position = layout(table)
    freq = THETA ** (-(2.0 * jnp.arange(HEAD_SIZE // 2, dtype=F32)) / HEAD_SIZE)
    angle = position.reshape(-1).astype(F32)[:, None] * freq
    cosine, sine = jnp.cos(angle), jnp.sin(angle)
    cosine = jnp.concatenate([cosine, cosine], axis=1)
    sine = jnp.concatenate([-sine, sine], axis=1)
    allowed = (sequence[:, :, None] == sequence[:, None, :]) & (slots[:, None, :] <= slots[:, :, None])
    bias = jnp.where(allowed, 0.0, -1e30).astype(F32)

    (late,) = tie(
        [late], [*inputs[1:], *upstream_near[1:], cosine, sine, bias], "late_then", HBM
    )
    late = lax.all_gather(late, PLANE, axis=0)
    upstream = with_cores(upstream_near)

    gain_at = s.ring_rows + s.out_rows
    gains = early[:, gain_at : gain_at + SHARE, : s.gains].astype(F32)
    gains = gains.reshape(4, 4, 2, -1).transpose(0, 2, 1, 3).reshape(1, -1)
    gain_one = gains[:, : s.width]
    gain_two = gains[:, s.width : 2 * s.width]
    gain_query = gains[:, 2 * s.width : 2 * s.width + HEAD_SIZE]
    gain_key = gains[:, 2 * s.width + HEAD_SIZE :]

    eight = pltpu.SemaphoreType.DMA((8,))
    head_weight, out_slice, normed_one, linear, probs, query, key, value, mixed, near, far = call(
        head_forward(s),
        [
            Far(shape((s.width, s.cell))),
            Far(shape((s.query, s.width))),
            Far(shape((s.rows, s.width))),
            Far(shape((s.rows, s.query + HEAD_SIZE), F32)),
            Far(shape((2 * s.heads, s.group, s.group), F32)),
            shape((s.rows, s.query)),
            shape((s.rows, HEAD_SIZE)),
            shape((s.rows, HEAD_SIZE)),
            shape((s.rows, s.query)),
            shape(half_rows),
            Far(shape(half_rows)),
        ],
        [*[Far(v) for v in inputs], Far(early), Far(cosine), Far(sine), Far(bias), gain_one, gain_query, gain_key],
        flops=2 * s.rows * s.width * (s.cell + s.query),
        large=54,
        name="head_forward",
    )
    parts, _ = ring_scatter(near, from_core(far), "branch")
    hidden_two, normed_two = call(
        branch_end(s), [shape(block, F32), shape(block)], [*parts, tokens, gain_two], name="branch_end"
    )
    normed_blocks = with_cores(from_chips(normed_two))
    down, hidden, grads, far, near = call(
        mlp_block(s),
        [
            Far(shape((s.hidden, s.width))),
            Far(shape((s.rows, s.hidden))),
            Far(shape((s.rows, 2 * s.hidden))),
            Far(shape(half_rows)),
            Far(shape(half_rows)),
        ],
        [*normed_blocks, *upstream, Far(late, later=True)],
        any_first=16,
        near=(0,),
        scratch=[
            pltpu.VMEM((s.rows, s.width), BF),
            pltpu.VMEM((s.rows, s.width), BF),
            pltpu.VMEM((s.width, 2 * s.hidden), BF),
            pltpu.VMEM((s.rows, s.hidden), F32),
            eight,
            eight,
        ],
        flops=10 * s.rows * s.width * s.hidden,
        large=60,
        name="mlp_block",
    )
    parts, sent = ring_scatter(near, from_core(far), "mlp_back")
    late_grad, mark = call(
        mlp_weight_grads(s),
        [shape((16, s.late, s.cell))],
        [*normed_blocks, *upstream, Far(grads, later=True), Far(hidden, later=True)],
        any_first=16,
        near=(0,),
        any_out=True,
        after=sent,
        scratch=[
            pltpu.VMEM((s.rows, s.width), BF),
            pltpu.VMEM((s.rows, s.width), BF),
            pltpu.VMEM((16, s.late, s.cell), BF),
            eight,
            eight,
            pltpu.SemaphoreType.DMA((2,)),
        ],
        flops=6 * s.rows * s.width * s.hidden,
        large=54,
        mark=True,
        name="mlp_weight_grads",
    )
    grad_hidden_two, grad_branch, gain_two_terms = call(
        mlp_back_end(s),
        [shape(block, F32), shape(block), shape((1, s.width), F32)],
        [*parts, cotangent, hidden_two, gain_two],
        after=[mark],
        name="mlp_back_end",
    )
    (late_grad,) = tie([late_grad], [grad_branch], "late_grad_then", HBM)
    late_grad = lax.psum_scatter(late_grad.reshape(-1, s.cell), PLANE, scatter_dimension=0, tiled=True)
    branch_near = from_chips(grad_branch)
    out_near, out_far = call(
        mlp_out(s),
        [shape(half_rows)] * 2,
        [Far(hidden), Far(down)],
        after=[grad_branch],
        flops=2 * s.rows * s.width * s.hidden,
        large=54,
        name="mlp_out",
    )
    out_far, *branch_near[1:] = tie([out_far, *branch_near[1:]], [], "branch_then")
    branch_blocks = with_cores(branch_near)
    output_parts, out_sent = ring_scatter(out_near, from_core(out_far), "output")

    moved = (out_slice, probs, linear, cosine, sine, query, key, value, normed_one, head_weight)
    (out_grad,) = call(
        out_weight_grads(s),
        [Far(shape((s.query, s.width)))],
        [*branch_blocks, Far(mixed)],
        any_first=8,
        near=(0,),
        scratch=[pltpu.VMEM((s.rows, s.width), BF), eight],
        flops=2 * s.rows * s.width * s.query,
        large=54,
        name="out_weight_grads",
    )
    out_parts = lax.all_to_all(out_grad.reshape(16, s.row, s.width), PLANE, 0, 0, tiled=True)
    near, far, owned, mark = call(
        head_back(s),
        [
            Far(shape(half_rows)),
            Far(shape(half_rows)),
            Far(shape((128, s.row, s.cell + HEAD_SIZE))),
        ],
        [*branch_blocks, *[Far(v, later=True) for v in moved]]
        + [gain_query, gain_key, gain_one, gain_two_terms, owner, lane],
        any_first=8,
        near=(0,),
        after=out_sent,
        scratch=[
            pltpu.VMEM((s.rows, s.width), BF),
            pltpu.VMEM((s.rows, s.query), BF),
            pltpu.VMEM((s.rows, s.cell), BF),
            pltpu.VMEM((1, count), F32),
            eight,
        ],
        hidden=True,
        large=54,
        mark=True,
        name="head_back",
    )
    (block_output,) = call(output_end(s), [shape(block)], [*output_parts, hidden_two], name="output_end")
    (out_lines,) = call(plane_sum(s), [shape((s.row, s.width))], [out_parts], after=[mark], name="plane_sum")
    owned, far = tie([owned, far], [block_output, out_lines], "head_grads_then")
    owned = lax.all_to_all(owned, AXES, 0, 0, tiled=True)
    parts, sent = ring_scatter(near, from_core(far), "input")
    (late_grad,) = tie([late_grad], parts[1:], "late_grad_last")
    input_grad, input_mark = call(
        input_end(s), [shape(block, F32)], [*parts, tokens, grad_hidden_two, gain_one], mark=True, name="input_end"
    )

    home = [(to, own) for own, to in row_route()]
    mlp_end = SHARE * s.mlp_rows
    columns = lax.all_to_all(late_grad[:mlp_end].reshape(SHARE, s.mlp_rows, s.cell), RING, 0, 0, tiled=True)
    lines = lax.ppermute(late_grad[mlp_end:], AXES, home)
    out_lines = lax.ppermute(out_lines, AXES, home)

    def states(*groups):
        return [Far(a) for group in groups for a in group]

    mlp_states = states(
        (gate_weight, gate_first, gate_second),
        (up_weight, up_first, up_second),
        (down_weight, down_first, down_second),
    )
    mlp_new = call(
        mlp_update(s),
        [Far(shape(a.value.shape, F32)) for a in mlp_states],
        [columns, lines] + mlp_states,
        after=[Far(owned)],
        mark=True,
        large=62,
        name="mlp_update",
    )
    head_states = states(
        (query_weight, query_first, query_second),
        (key_matrix, key_first_moment, key_second_moment),
        (value_matrix, value_first_moment, value_second_moment),
        (out_weight, out_first, out_second),
    )
    gains_state = [a[None] for a in (norm_gains, gains_first, gains_second)]
    head_new = call(
        head_update(s),
        [Far(shape(a.value.shape, F32)) for a in head_states] + [shape(a.shape, F32) for a in gains_state],
        [owned, out_lines] + head_states + gains_state,
        after=[input_mark, mlp_new[-1]],
        large=62,
        name="head_update",
    )
    return (block_output, input_grad, *head_new[:12], *mlp_new[:9], *[value[0] for value in head_new[12:]])


def solution(mesh):
    fine = Mesh(mesh.devices.reshape(SIZES), AXES)
    matrix, vector, grouped = P(AXES, None), P(AXES), P(("z", "xl", "y"), None)
    states = (matrix,) * 7 + (vector,)
    return jax.shard_map(
        local,
        mesh=fine,
        in_specs=(matrix, matrix, grouped, grouped) + states * 3,
        out_specs=(matrix, matrix) + (matrix,) * 21 + (vector,) * 3,
        check_vma=False,
    )
```

```python
import math

import jax
import jax.numpy as jnp
import ml_dtypes
import numpy as np
from jax import lax
from jax.experimental import pallas as pl
from jax.experimental.pallas import tpu as pltpu
from jax.sharding import Mesh
from jax.sharding import PartitionSpec as P

MODEL_WIDTH = 2048
QUERY_HEADS = 16
KEY_VALUE_HEADS = 8
HEAD_SIZE = 128
FF = 6144
TOK_DEV = 128
STEP = 10

EPS = 1e-06
THETA = 1000000.0
BETA_ONE = 0.9
BETA_TWO = 0.95
ADAM_EPS = 1e-08
DECAY = 0.1

AXES = ("z", "xl", "y", "xh", "c")
SIZES = (4, 2, 4, 2, 2)
RING = ("xl", "xh", "c")
PLANE = ("z", "y")
CHIPS = ("xl", "xh")
SHARE = 8
OFFSETS = (0, 2, 1, 3)
BF = jnp.bfloat16
F32 = jnp.float32


def chip_number(x):
    return (x % 2) * 2 + x // 2


def from_chip(value, offset):
    pairs = [(chip_number((x + offset) % 4), chip_number(x)) for x in range(4)]
    return lax.ppermute(value, CHIPS, pairs)


def from_core(value):
    return lax.ppermute(value, "c", [(0, 1), (1, 0)])


def row_route():
    pairs = []
    for z in range(4):
        for xl in range(2):
            for y in range(4):
                for xh in range(2):
                    for c in range(2):
                        own = (((z * 2 + xl) * 4 + y) * 2 + xh) * 2 + c
                        part = 2 * z + xl
                        to = (((y * 2 + part // 4) * 4 + (xh * 2 + c)) * 2 + (part // 2) % 2) * 2 + part % 2
                        pairs.append((own, to))
    return pairs


def from_chips(block):
    return [block] + [from_chip(block, offset) for offset in OFFSETS[1:]]


def with_cores(near):
    return near + [from_core(value) for value in near]


def row_blocks():
    return [group * 4 + core * 2 + chip for core in range(2) for group in range(2) for chip in range(2)]


def dot(left, right):
    return jnp.dot(left, right, preferred_element_type=F32)


def dot_last(left, right):
    return lax.dot_general(left, right, (((1,), (1,)), ((), ())), preferred_element_type=F32)


def dot_first(left, right):
    return lax.dot_general(left, right, (((0,), (0,)), ((), ())), preferred_element_type=F32)


def inverse_rms(values):
    return lax.rsqrt(jnp.mean(values * values, axis=-1, keepdims=True) + EPS)


class Arriving:
    def __init__(self, source, buffer, sem):
        self.buffer, self.shape, self.here = buffer, buffer.shape, False
        self.copy = pltpu.make_async_copy(source, buffer, sem)

    def start(self):
        self.copy.start()

    def wait(self):
        if not self.here:
            self.copy.wait()
        self.here = True

    def __getitem__(self, index):
        self.wait()
        return self.buffer[index]


class Leaving:
    def __init__(self, buffer, target, sem):
        self.buffer, self.shape, self.sent = buffer, buffer.shape, False
        self.copy = pltpu.make_async_copy(buffer, target, sem)

    def __getitem__(self, index):
        return self.buffer[index]

    def __setitem__(self, index, value):
        self.buffer[index] = value

    def send(self):
        self.sent = True
        self.copy.start()


def bytes_of(values):
    return sum(math.prod(v.shape) * jnp.dtype(v.dtype).itemsize for v in values)


class Far:
    def __init__(self, value, later=False):
        self.value, self.later = value, later


HBM = pl.BlockSpec(memory_space=pltpu.HBM)
ANY = pl.BlockSpec(memory_space=pl.ANY)


def order_specs(after):
    return [HBM if isinstance(a, Far) else ANY for a in after], [a.value if isinstance(a, Far) else a for a in after]


def call(body, outs, args, after=(), scratch=(), flops=0, any_first=0, any_out=False, scalars=0, near=(), hidden=False, large=False, mark=False, name=None):
    if mark:
        outs = [*outs, shape((8, 128), F32)]
    after_specs, after = order_specs(after)
    far_in = [isinstance(a, Far) for a in args]
    later = [isinstance(a, Far) and a.later for a in args]
    far_out = [isinstance(o, Far) for o in outs]
    args = [a.value if isinstance(a, Far) else a for a in args]
    outs = [o.value if isinstance(o, Far) else o for o in outs]
    size = bytes_of((*args, *outs))
    held = bytes_of(args[any_first:]) + bytes_of(() if any_out else outs)
    held += bytes_of([v for v in scratch if v.memory_space == pltpu.VMEM])
    moved = [v for v, far in zip((*args, *outs), far_in + far_out) if far]
    n_in, n_out, n_move = len(args), len(outs), len(moved)

    def run(*refs):
        ins, refs = list(refs[:n_in]), refs[n_in + len(after) :]
        results, refs = list(refs[:n_out]), refs[n_out:]
        own, refs = refs[: len(scratch)], refs[len(scratch) :]
        buffers, sems = list(refs[:n_move]), list(refs[n_move:])
        for i, far in enumerate(far_in):
            if far:
                ins[i] = Arriving(ins[i], buffers.pop(0), sems.pop(0))
                if not later[i]:
                    ins[i].start()
        for i, far in enumerate(far_out):
            if far:
                results[i] = Leaving(buffers.pop(0), results[i], sems.pop(0))
        if mark:
            results[-1][...] = jnp.zeros((8, 128), F32)
        body(*ins, *(results[:-1] if mark else results), *own)
        for value in ins:
            if isinstance(value, Arriving):
                value.wait()
        for value in results:
            if isinstance(value, Leaving) and not value.sent:
                value.send()
        for value in results:
            if isinstance(value, Leaving):
                value.copy.wait()

    def spec(far):
        return HBM if far else pl.BlockSpec(memory_space=pltpu.VMEM)

    in_specs = [spec(far or (i < any_first and i not in near)) for i, far in enumerate(far_in)]
    in_specs[:scalars] = [pl.BlockSpec(memory_space=pltpu.SMEM)] * scalars

    return pl.pallas_call(
        run,
        out_shape=tuple(outs),
        in_specs=in_specs + after_specs,
        out_specs=tuple(spec(far or (any_out and i == 0)) for i, far in enumerate(far_out)),
        scratch_shapes=list(scratch)
        + [pltpu.VMEM(v.shape, v.dtype) for v in moved]
        + [pltpu.SemaphoreType.DMA for _ in moved],
        compiler_params=pltpu.CompilerParams(vmem_limit_bytes=large * 2**20 if large else held + 12 * 2**20),
        cost_estimate=pl.CostEstimate(flops=flops, bytes_accessed=0 if hidden else size, transcendentals=0),
        name=name,
    )(*args, *after)


def tie(values, after, name, spec=ANY):
    count = len(values)
    after_specs, after = order_specs(after)

    def body(*refs):
        pass

    return pl.pallas_call(
        body,
        out_shape=tuple(jax.ShapeDtypeStruct(v.shape, v.dtype) for v in values),
        in_specs=[spec] * count + after_specs,
        out_specs=tuple(spec for _ in values),
        input_output_aliases={i: i for i in range(count)},
        name=name,
    )(*values, *after)


def shape(dims, dtype=BF):
    return jax.ShapeDtypeStruct(tuple(dims), dtype)


class Sizes:
    def __init__(self):
        self.width = MODEL_WIDTH
        self.heads = QUERY_HEADS // SHARE
        self.query = self.heads * HEAD_SIZE
        self.cell = self.query + 2 * HEAD_SIZE
        self.hidden = FF // SHARE
        self.row = MODEL_WIDTH // 128
        self.down_row = FF // 128
        self.out_parts = self.width // self.cell
        self.mlp_parts = 2 * self.hidden // self.cell
        self.ring_rows = SHARE * self.row
        self.mlp_rows = self.mlp_parts * self.row
        self.out_rows = self.out_parts * self.row
        self.down_rows = self.out_parts * self.down_row
        self.early = self.ring_rows + self.out_rows + self.row
        self.late = SHARE * self.mlp_rows + self.down_rows
        self.gains = (2 * MODEL_WIDTH + 2 * HEAD_SIZE) // 128
        self.block = TOK_DEV
        self.rows = 8 * TOK_DEV
        self.group = 4 * TOK_DEV
        self.half = 2 * TOK_DEV


def pack_weights(s):
    def body(query, key, value, out, gate, up, down, gains, columns, lines):
        for j in range(SHARE):
            q, h = s.query, HEAD_SIZE
            columns[j, : s.row, :q] = query[:, j * q : (j + 1) * q].astype(BF)
            columns[j, : s.row, q : q + h] = key[:, j * h : (j + 1) * h].astype(BF)
            columns[j, : s.row, q + h :] = value[:, j * h : (j + 1) * h].astype(BF)
            for source, start in ((gate, 0), (up, s.hidden)):
                done = 0
                while done < s.hidden:
                    at = start + done
                    part, inside = at // s.cell, at % s.cell
                    size = min(s.cell - inside, s.hidden - done)
                    columns[j, s.row * (1 + part) : s.row * (2 + part), inside : inside + size] = source[
                        :, j * s.hidden + done : j * s.hidden + done + size
                    ].astype(BF)
                    done += size
            columns[j, s.row + s.mlp_rows :, :] = jnp.zeros((s.row, s.cell), BF)
            columns[j, s.row + s.mlp_rows :, : s.gains] = jnp.broadcast_to(gains[...], (s.row, s.gains)).astype(BF)
        for p in range(s.out_parts):
            lines[p * s.row : (p + 1) * s.row] = out[:, p * s.cell : (p + 1) * s.cell].astype(BF)
            at = s.out_rows + p * s.down_row
            lines[at : at + s.down_row] = down[:, p * s.cell : (p + 1) * s.cell].astype(BF)

    return body


def place_weights(s):
    def body(columns, lines, early, late, table):
        gain_at = s.row + s.mlp_rows
        table[...] = jnp.zeros_like(table)
        for j in range(SHARE):
            early[j * s.row : (j + 1) * s.row] = columns[j, : s.row]
            late[j * s.mlp_rows : (j + 1) * s.mlp_rows] = columns[j, s.row : gain_at]
            table[j : j + 1] = columns[j, gain_at : gain_at + s.row].astype(F32)[:1]
        early[s.ring_rows : s.ring_rows + s.out_rows] = lines[: s.out_rows]
        early[s.ring_rows + s.out_rows :] = table[...].astype(BF)
        late[SHARE * s.mlp_rows :] = lines[s.out_rows :]

    return body


def fill_head_weight(s, early, target):
    part = 4 * s.row
    for z in range(4):
        for xl in range(2):
            for y in range(4):
                at = ((z * 2 + xl) * 4 + y) * part
                target[at : at + part] = early[z * 4 + y, xl * part : (xl + 1) * part]


def fill_out_weight(s, early, target):
    for f in range(16):
        for p in range(s.out_parts):
            at = s.ring_rows + p * s.row
            target[f * s.row : (f + 1) * s.row, p * s.cell : (p + 1) * s.cell] = early[f, at : at + s.row]


def turn(value):
    return pltpu.roll(value, HEAD_SIZE // 2, 1)


def head_forward(s):
    scale = HEAD_SIZE ** (-0.5)

    def body(*refs):
        blocks = refs[:8]
        early, cosine, sine, bias, gain_one, gain_query, gain_key = refs[8:15]
        weight, out_weight, normed, linear, probs, query, key, value, mixed, near, far = refs[15:]
        for ref, at in zip(blocks, row_blocks()):
            wide = ref[...].astype(F32)
            normed[at * s.block : (at + 1) * s.block] = (wide * inverse_rms(wide) * gain_one[...]).astype(BF)
        normed.send()
        fill_head_weight(s, early, weight)
        weight.send()
        q, h = s.query, HEAD_SIZE
        for group in range(2):
            rows = pl.ds(group * s.group, s.group)
            lin = dot(normed[rows], weight[...])
            linear[rows] = lin[:, : q + h]
            value[rows] = lin[:, q + h :].astype(BF)
            cos, sin = cosine[rows], sine[rows]

            def turned(part, gain):
                part = part * inverse_rms(part) * gain[...]
                return (part * cos + turn(part) * sin).astype(BF)

            key[rows] = turned(lin[:, q : q + h], gain_key)
            for r in range(s.heads):
                query[rows, r * h : (r + 1) * h] = turned(lin[:, r * h : (r + 1) * h], gain_query)
        linear.send()
        fill_out_weight(s, early, out_weight)
        out_weight.send()
        for group in range(2):
            rows = pl.ds(group * s.group, s.group)
            for r in range(s.heads):
                score = dot_last(query[rows, r * h : (r + 1) * h], key[rows]) * scale + bias[group]
                expo = jnp.exp(score - jnp.max(score, axis=-1, keepdims=True))
                prob = expo * (1.0 / jnp.sum(expo, axis=-1, keepdims=True))
                probs[group * s.heads + r] = prob
                mixed[rows, r * h : (r + 1) * h] = dot(prob.astype(BF), value[rows]).astype(BF)
        probs.send()
        for target, core in ((far, 1), (near, 0)):
            for group in range(2):
                rows = pl.ds(group * s.group + core * s.half, s.half)
                target[pl.ds(group * s.half, s.half)] = dot(mixed[rows], out_weight[...]).astype(BF)
            if core:
                far.send()

    return body


def ring_add(s):
    def body(near, arrived, own, *others):
        own[...] = near[: s.block].astype(F32) + arrived[: s.block].astype(F32)
        for i, other in enumerate(others):
            rows = pl.ds((i + 1) * s.block, s.block)
            other[...] = (near[rows].astype(F32) + arrived[rows].astype(F32)).astype(BF)

    return body


def total_of(own, parts):
    total = own[...]
    for part in parts:
        total = total + part[...].astype(F32)
    return total


def branch_end(s):
    def body(own, first, second, third, tokens, gain_two, hidden_two, normed):
        value = tokens[...].astype(F32) + total_of(own, (first, second, third))
        hidden_two[...] = value
        normed[...] = (value * inverse_rms(value) * gain_two[...]).astype(BF)

    return body


def norm_back(values, gain, grad):
    scale = inverse_rms(values)
    normalized = values * scale
    inner = grad * gain
    back = scale * inner - normalized * scale * jnp.mean(inner * normalized, axis=-1, keepdims=True)
    return back, grad * normalized


def gather_into(s, blocks, buffer, sems):
    copies = {}
    for i, (ref, at) in enumerate(zip(blocks, row_blocks())):
        copies[at] = pltpu.make_async_copy(ref, buffer.at[pl.ds(at * s.block, s.block)], sems.at[i])
        copies[at].start()
    return copies


def wait_all(copies):
    for copy in copies.values():
        copy.wait()


def mlp_block(s):
    step = 2 * HEAD_SIZE

    def body(*refs):
        blocks, upstream_blocks, gathered = refs[:8], refs[8:16], refs[16]
        down, hidden, grads, far, near, normed, upstream, weight, grad_hidden, late, sems, up_sems, late_sems = refs[17:]
        copies = gather_into(s, upstream_blocks, upstream, up_sems)
        split = SHARE * s.mlp_rows
        arriving = []
        for i, rows in enumerate((pl.ds(split, s.down_rows), pl.ds(0, split))):
            arriving.append(pltpu.make_async_copy(gathered.at[:, rows], late.at[:, rows], late_sems.at[i]))
            arriving[i].start()
        normed_copies = gather_into(s, blocks, normed, sems)
        arriving[0].wait()
        for f in range(16):
            for p in range(s.out_parts):
                start = SHARE * s.mlp_rows + p * s.down_row
                down[f * s.down_row : (f + 1) * s.down_row, p * s.cell : (p + 1) * s.cell] = late[
                    f, start : start + s.down_row
                ]
        down.send()
        wait_all(copies)
        for n in range(s.hidden // step):
            columns = slice(n * step, (n + 1) * step)
            grad_hidden[:, columns] = dot_last(upstream[...], down[columns])
        arriving[1].wait()
        for f in range(16):
            z, y = divmod(f, 4)
            for j in range(SHARE):
                xl, part = divmod(j, 4)
                at = (((z * 2 + xl) * 4 + y) * 4 + part) * s.row
                for p in range(s.mlp_parts):
                    start = j * s.mlp_rows + p * s.row
                    weight[at : at + s.row, p * s.cell : (p + 1) * s.cell] = late[f, start : start + s.row]
        wait_all(normed_copies)
        for n in range(s.hidden // step):
            columns = slice(n * step, (n + 1) * step)
            second = slice(s.hidden + n * step, s.hidden + (n + 1) * step)
            gate = dot(normed[...], weight[:, columns])
            up = dot(normed[...], weight[:, second])
            sigma = jax.nn.sigmoid(gate)
            active = gate * sigma
            hidden[:, columns] = (active * up).astype(BF)
            grad = grad_hidden[:, columns]
            grads[:, columns] = (grad * up * (sigma * (1.0 + gate * (1.0 - sigma)))).astype(BF)
            grads[:, second] = (grad * active).astype(BF)
        hidden.send()
        grads.send()
        for target, core in ((far, 1), (near, 0)):
            for n in range(s.width // step):
                columns = slice(n * step, (n + 1) * step)
                for group in range(2):
                    rows = pl.ds(group * s.group + core * s.half, s.half)
                    part = dot_last(grads[rows], weight[columns])
                    target[pl.ds(group * s.half, s.half), columns] = part.astype(BF)
            target.send()

    return body


def mlp_weight_grads(s):
    step = 4 * s.row * 4

    def body(*refs):
        normed_blocks, blocks = refs[:8], refs[8:16]
        grads, hidden, target, normed, upstream, made, normed_sems, sems, out_sems = refs[16:]
        normed_copies = gather_into(s, normed_blocks, normed, normed_sems)
        copies = gather_into(s, blocks, upstream, sems)
        leaving = []
        grads.start()
        hidden.start()
        wait_all(normed_copies)
        for z in range(4):
            for xl in range(2):
                at = (z * 2 + xl) * step
                tile = dot_first(normed[:, at : at + step], grads[...]).astype(BF)
                for y in range(4):
                    for part in range(4):
                        line = (y * 4 + part) * s.row
                        for p in range(s.mlp_parts):
                            start = (xl * 4 + part) * s.mlp_rows + p * s.row
                            made[z * 4 + y, start : start + s.row] = tile[
                                line : line + s.row, p * s.cell : (p + 1) * s.cell
                            ]
            if z % 2:
                pair = z // 2
                if pair == 0:
                    wait_all(copies)
                wide = s.hidden // 2
                columns = hidden[:, pair * wide : (pair + 1) * wide]
                for p in range(s.out_parts):
                    tile = dot_first(columns, upstream[:, p * s.cell : (p + 1) * s.cell]).astype(BF)
                    for f in range(8):
                        start = SHARE * s.mlp_rows + p * s.down_row
                        made[pair * 8 + f, start : start + s.down_row] = tile[f * s.down_row : (f + 1) * s.down_row]
                half = pl.ds(pair * 8, 8)
                copy = pltpu.make_async_copy(made.at[half], target.at[half], out_sems.at[pair])
                copy.start()
                leaving.append(copy)
        for copy in leaving:
            copy.wait()

    return body


def mlp_out(s):
    step = 4 * HEAD_SIZE

    def body(hidden, down, near, far):
        for target, core in ((far, 1), (near, 0)):
            for group in range(2):
                rows = pl.ds(group * s.group + core * s.half, s.half)
                for n in range(s.width // step):
                    columns = slice(n * step, (n + 1) * step)
                    target[pl.ds(group * s.half, s.half), columns] = dot(hidden[rows], down[:, columns]).astype(BF)

    return body


def mlp_back_end(s):
    def body(own, first, second, third, cotangent, hidden_two, gain_two, grad_hidden_two, low, terms):
        grad = total_of(own, (first, second, third))
        back, gains = norm_back(hidden_two[...], gain_two[...], grad)
        value = cotangent[...].astype(F32) + back
        grad_hidden_two[...] = value
        low[...] = value.astype(BF)
        terms[...] = jnp.sum(gains, axis=0, keepdims=True)

    return body


def out_weight_grads(s):
    def body(*refs):
        mixed, out_grad, branch, sems = refs[8:]
        wait_all(gather_into(s, refs[:8], branch, sems))
        for p in range(s.out_parts):
            columns = slice(p * s.cell, (p + 1) * s.cell)
            out_grad[:, columns] = dot_first(mixed[...], branch[:, columns]).astype(BF)

    return body


def head_back(s):
    scale = HEAD_SIZE ** (-0.5)

    def body(*refs):
        blocks = refs[:8]
        out_weight, probs, linear, cosine, sine, query, key, value, normed, weight = refs[8:18]
        gain_query, gain_key, gain_one, gain_two_terms, owner, lane = refs[18:24]
        near, far, owned_rows, branch, grad_mixed, grads, gain_row, sems = refs[24:]
        copies = gather_into(s, blocks, branch, sems)
        for later in (out_weight, probs, linear, cosine, sine, query, key, value, normed, weight):
            later.start()
        q, h = s.query, HEAD_SIZE
        query_sum = jnp.zeros((1, h), F32)
        key_sum = jnp.zeros((1, h), F32)
        for group in range(2):
            rows = pl.ds(group * s.group, s.group)
            for at in range(group * 4, group * 4 + 4):
                copies[at].wait()
            grad_mixed[rows] = dot_last(branch[rows], out_weight[...]).astype(BF)
            cos, sin = cosine[rows], sine[rows]
            key_grad = jnp.zeros((s.group, h), F32)
            value_grad = jnp.zeros((s.group, h), F32)
            for r in range(s.heads):
                columns = slice(r * h, (r + 1) * h)
                prob = probs[group * s.heads + r]
                out = grad_mixed[rows, columns]
                grad_prob = dot_last(out, value[rows])
                inner = jnp.sum(prob * grad_prob, axis=-1, keepdims=True)
                grad_score = (prob * (grad_prob - inner)).astype(BF)
                value_grad = value_grad + dot_first(prob.astype(BF), out)
                key_grad = key_grad + dot_first(grad_score, query[rows, columns]) * scale
                turned = dot(grad_score, key[rows]) * scale
                back, terms = norm_back(
                    linear[rows, columns], gain_query[...], turned * cos - turn(turned) * sin
                )
                grads[rows, columns] = back.astype(BF)
                query_sum = query_sum + jnp.sum(terms, axis=0, keepdims=True)
            back, terms = norm_back(
                linear[rows, q : q + h], gain_key[...], key_grad * cos - turn(key_grad) * sin
            )
            grads[rows, q : q + h] = back.astype(BF)
            key_sum = key_sum + jnp.sum(terms, axis=0, keepdims=True)
            grads[rows, q + h :] = value_grad.astype(BF)
        wide = 4 * HEAD_SIZE
        for n in range(s.width // wide):
            columns = slice(n * wide, (n + 1) * wide)
            total = jnp.zeros((1, wide), F32)
            for target, core in ((far, 1), (near, 0)):
                for group in range(2):
                    rows = pl.ds(group * s.group + core * s.half, s.half)
                    part = dot_last(grads[rows], weight[columns])
                    target[pl.ds(group * s.half, s.half), columns] = part.astype(BF)
                    total = total + jnp.sum(part * normed[rows, columns].astype(F32), axis=0, keepdims=True)
            gain_row[:, columns] = total / gain_one[:, columns]
        far.send()
        near.send()
        gain_row[:, s.width : 2 * s.width] = gain_two_terms[...]
        gain_row[:, 2 * s.width : 2 * s.width + h] = query_sum
        gain_row[:, 2 * s.width + h :] = key_sum
        owned = dot((owner[...].astype(F32) * gain_row[...]).astype(BF), lane[...])
        for o in range(128):
            owned_rows[o, :, s.cell :] = jnp.broadcast_to(owned[o : o + 1], (s.row, h)).astype(BF)
        step = 16 * s.row
        for n in range(8):
            tile = dot_first(normed[:, n * step : (n + 1) * step], grads[...]).astype(BF)
            owned_rows[n * 16 : (n + 1) * 16, :, : s.cell] = tile.reshape(16, s.row, s.cell)

    return body


def plane_sum(s):
    def body(parts, total):
        value = parts[0].astype(F32)
        for f in range(1, 16):
            value = value + parts[f].astype(F32)
        total[...] = value.astype(BF)

    return body


def input_end(s):
    def body(own, first, second, third, tokens, grad_hidden_two, gain_one, input_grad):
        back, _ = norm_back(tokens[...].astype(F32), gain_one[...], total_of(own, (first, second, third)))
        input_grad[...] = grad_hidden_two[...] + back

    return body


def output_end(s):
    def body(own, first, second, third, hidden_two, block_output):
        block_output[...] = (hidden_two[...] + total_of(own, (first, second, third))).astype(BF)

    return body


def adam(weight, grad, first, second, rate, decay):
    first_new = BETA_ONE * first + (1.0 - BETA_ONE) * grad
    second_new = BETA_TWO * second + (1.0 - BETA_TWO) * grad * grad
    first_hat = first_new / (1.0 - BETA_ONE**STEP)
    second_hat = second_new / (1.0 - BETA_TWO**STEP)
    weight_new = weight - rate * (first_hat / (jnp.sqrt(second_hat) + ADAM_EPS) + decay * weight)
    return (weight_new, first_new, second_new)


def step_into(ins, outs, columns, grad, rate, decay):
    results = adam(ins[0][:, columns], grad.astype(F32), ins[1][:, columns], ins[2][:, columns], rate, decay)
    for out, value in zip(outs, results):
        out[:, columns] = value


def split_refs(refs, first, count):
    ins = [refs[first + 3 * i : first + 3 * i + 3] for i in range(count)]
    outs = [refs[first + 3 * (count + i) : first + 3 * (count + i) + 3] for i in range(count)]
    return ins, outs


def send_all(outs):
    for out in outs:
        out.send()


def head_update(s):
    def body(*refs):
        owned, lines = refs[:2]
        ins, outs = split_refs(refs, 2, 5)
        rate = MODEL_WIDTH ** (-0.5)
        out_rate = (TOK_DEV / (QUERY_HEADS * HEAD_SIZE)) ** 0.5
        gain_grad = jnp.zeros((s.row, HEAD_SIZE), F32)
        for j in range(SHARE):
            xl, part = divmod(j, 4)
            grad = jnp.zeros((s.row, s.cell), F32)
            for z in range(4):
                for y in range(4):
                    source = ((z * 2 + xl) * 4 + y) * 4 + part
                    grad = grad + owned[source, :, : s.cell].astype(F32)
                    gain_grad = gain_grad + owned[source, :, s.cell :].astype(F32)
            start = 0
            for i, size in enumerate((s.query, HEAD_SIZE, HEAD_SIZE)):
                columns = slice(j * size, (j + 1) * size)
                step_into(ins[i], outs[i], columns, grad[:, start : start + size], rate, DECAY)
                start += size
        for i in range(3):
            send_all(outs[i])
        for p in range(s.out_parts):
            columns = slice(p * s.cell, (p + 1) * s.cell)
            step_into(ins[3], outs[3], columns, lines[:, columns], out_rate, DECAY)
        send_all(outs[3])
        step_into(ins[4], outs[4], slice(0, s.gains), gain_grad[:1, : s.gains], 0.5, 0.0)

    return body


def mlp_update(s):
    def body(*refs):
        columns, lines = refs[:2]
        ins, outs = split_refs(refs, 2, 3)
        for i, start in ((0, 0), (1, s.hidden)):
            for j in range(SHARE):
                done = 0
                while done < s.hidden:
                    at = start + done
                    part, inside = at // s.cell, at % s.cell
                    size = min(s.cell - inside, s.hidden - done)
                    grad = columns[j, part * s.row : (part + 1) * s.row, inside : inside + size]
                    own = slice(j * s.hidden + done, j * s.hidden + done + size)
                    step_into(ins[i], outs[i], own, grad, MODEL_WIDTH ** (-0.5), DECAY)
                    done += size
            send_all(outs[i])
        for p in range(s.out_parts):
            grad = lines[p * s.down_row : (p + 1) * s.down_row]
            step_into(ins[2], outs[2], slice(p * s.cell, (p + 1) * s.cell), grad, FF ** (-0.5), DECAY)

    return body


def layout(table, other):
    span = TOK_DEV // 2
    both = jnp.stack([table, other])
    sizes, spans = both[:, :2], both[:, 2:]
    chip = lax.axis_index("xh") * 2 + lax.axis_index("xl")
    core = lax.axis_index("c")
    offset = jnp.arange(2)[:, None, None] + 2 * jnp.arange(2)[None, None, :]
    place = ((chip + offset) % 4) // 2 * 2 + (core + jnp.arange(2)[None, :, None]) % 2
    block = (2 * place[..., None] + jnp.arange(2)).reshape(2, 8)
    owner = jnp.sum(jnp.where(block[:, :, None] == jnp.arange(8), spans[:, None, :], 0), axis=-1)
    slots = (owner[:, :, None] * span + jnp.arange(span)).reshape(2, -1)
    ends = jnp.cumsum(sizes, axis=1)
    passed = slots[:, :, None] >= ends[:, None, :]
    sequence = jnp.sum(passed.astype(jnp.int32), axis=-1)
    position = slots - jnp.sum(jnp.where(passed, sizes[:, None, :], 0), axis=-1)
    return slots, sequence, position


def local(
    tokens,
    cotangent,
    lengths,
    span_ids,
    query_weight,
    key_matrix,
    value_matrix,
    out_weight,
    gate_weight,
    up_weight,
    down_weight,
    norm_gains,
    query_first,
    key_first_moment,
    value_first_moment,
    out_first,
    gate_first,
    up_first,
    down_first,
    gains_first,
    query_second,
    key_second_moment,
    value_second_moment,
    out_second,
    gate_second,
    up_second,
    down_second,
    gains_second,
):
    s = Sizes()
    block = (s.block, s.width)
    half_rows = (s.group, s.width)

    def ring_scatter(near, arrived, name, after=()):
        own, *others = call(
            ring_add(s), [shape(block, F32)] + [shape(block)] * 3, [near, arrived], after=after, name=name + "_add"
        )
        arrived = [from_chip(piece, -OFFSETS[i + 1]) for i, piece in enumerate(others)]
        return [own] + arrived, others

    columns, lines, mark = call(
        pack_weights(s),
        [shape((SHARE, 2 * s.row + s.mlp_rows, s.cell)), shape((s.out_rows + s.down_rows, s.cell))],
        [Far(query_weight), Far(key_matrix), Far(value_matrix), Far(out_weight), Far(gate_weight), Far(up_weight)]
        + [Far(down_weight), norm_gains[None]],
        large=54,
        mark=True,
        name="pack_weights",
    )
    (table,) = tie([jnp.concatenate([lengths[0], span_ids[0]])], [mark], "table_then")
    other_table = lax.ppermute(table, "xl", [(0, 1), (1, 0)])
    (tokens_then,) = tie([tokens], [mark], "tokens_then", HBM)
    input_near = from_chips(tokens_then)
    inputs = with_cores(input_near)
    columns = lax.all_to_all(columns, RING, 0, 0, tiled=True)
    lines = lax.ppermute(lines, AXES, row_route())

    count = 128 * s.gains
    owner = np.asarray(np.arange(count)[None] // s.gains == np.arange(128)[:, None], ml_dtypes.bfloat16)
    lane = np.asarray(np.arange(count)[:, None] % s.gains == np.arange(HEAD_SIZE)[None], ml_dtypes.bfloat16)

    early, late = call(
        place_weights(s),
        [shape((s.early, s.cell)), shape((s.late, s.cell))],
        [columns, lines],
        after=[other_table],
        scratch=[pltpu.VMEM((s.row, s.cell), F32)],
        name="place_weights",
    )
    early = lax.all_gather(early, PLANE, axis=0)
    (cotangent_then,) = tie([cotangent], [Far(input_near[1])], "cotangent_then", HBM)
    upstream_near = from_chips(cotangent_then)
    slots, sequence, position = layout(table, other_table)
    freq = THETA ** (-(2.0 * jnp.arange(HEAD_SIZE // 2, dtype=F32)) / HEAD_SIZE)
    angle = position.reshape(-1).astype(F32)[:, None] * freq
    cosine, sine = jnp.cos(angle), jnp.sin(angle)
    cosine = jnp.concatenate([cosine, cosine], axis=1)
    sine = jnp.concatenate([-sine, sine], axis=1)
    allowed = (sequence[:, :, None] == sequence[:, None, :]) & (slots[:, None, :] <= slots[:, :, None])
    bias = jnp.where(allowed, 0.0, -1e30).astype(F32)

    (late,) = tie(
        [late], [*inputs[1:], *upstream_near[1:], cosine, sine, bias], "late_then", HBM
    )
    late = lax.all_gather(late, PLANE, axis=0)
    upstream = with_cores(upstream_near)

    gain_at = s.ring_rows + s.out_rows
    gains = early[:, gain_at : gain_at + SHARE, : s.gains].astype(F32)
    gains = gains.reshape(4, 4, 2, -1).transpose(0, 2, 1, 3).reshape(1, -1)
    gain_one = gains[:, : s.width]
    gain_two = gains[:, s.width : 2 * s.width]
    gain_query = gains[:, 2 * s.width : 2 * s.width + HEAD_SIZE]
    gain_key = gains[:, 2 * s.width + HEAD_SIZE :]

    eight = pltpu.SemaphoreType.DMA((8,))
    head_weight, out_slice, normed_one, linear, probs, query, key, value, mixed, near, far = call(
        head_forward(s),
        [
            Far(shape((s.width, s.cell))),
            Far(shape((s.query, s.width))),
            Far(shape((s.rows, s.width))),
            Far(shape((s.rows, s.query + HEAD_SIZE), F32)),
            Far(shape((2 * s.heads, s.group, s.group), F32)),
            shape((s.rows, s.query)),
            shape((s.rows, HEAD_SIZE)),
            shape((s.rows, HEAD_SIZE)),
            shape((s.rows, s.query)),
            shape(half_rows),
            Far(shape(half_rows)),
        ],
        [*[Far(v) for v in inputs], Far(early), Far(cosine), Far(sine), Far(bias), gain_one, gain_query, gain_key],
        flops=2 * s.rows * s.width * (s.cell + s.query),
        large=54,
        name="head_forward",
    )
    parts, _ = ring_scatter(near, from_core(far), "branch")
    hidden_two, normed_two = call(
        branch_end(s), [shape(block, F32), shape(block)], [*parts, tokens, gain_two], name="branch_end"
    )
    normed_blocks = with_cores(from_chips(normed_two))
    down, hidden, grads, far, near = call(
        mlp_block(s),
        [
            Far(shape((s.hidden, s.width))),
            Far(shape((s.rows, s.hidden))),
            Far(shape((s.rows, 2 * s.hidden))),
            Far(shape(half_rows)),
            Far(shape(half_rows)),
        ],
        [*normed_blocks, *upstream, late],
        any_first=17,
        near=(0,),
        scratch=[
            pltpu.VMEM((s.rows, s.width), BF),
            pltpu.VMEM((s.rows, s.width), BF),
            pltpu.VMEM((s.width, 2 * s.hidden), BF),
            pltpu.VMEM((s.rows, s.hidden), F32),
            pltpu.VMEM((16, s.late, s.cell), BF),
            eight,
            eight,
            pltpu.SemaphoreType.DMA((2,)),
        ],
        flops=10 * s.rows * s.width * s.hidden,
        large=60,
        name="mlp_block",
    )
    parts, sent = ring_scatter(near, from_core(far), "mlp_back")
    late_grad, mark = call(
        mlp_weight_grads(s),
        [shape((16, s.late, s.cell))],
        [*normed_blocks, *upstream, Far(grads, later=True), Far(hidden, later=True)],
        any_first=16,
        near=(0,),
        any_out=True,
        after=sent,
        scratch=[
            pltpu.VMEM((s.rows, s.width), BF),
            pltpu.VMEM((s.rows, s.width), BF),
            pltpu.VMEM((16, s.late, s.cell), BF),
            eight,
            eight,
            pltpu.SemaphoreType.DMA((2,)),
        ],
        flops=6 * s.rows * s.width * s.hidden,
        large=54,
        mark=True,
        name="mlp_weight_grads",
    )
    grad_hidden_two, grad_branch, gain_two_terms = call(
        mlp_back_end(s),
        [shape(block, F32), shape(block), shape((1, s.width), F32)],
        [*parts, cotangent, hidden_two, gain_two],
        after=[mark],
        name="mlp_back_end",
    )
    (late_grad,) = tie([late_grad], [grad_branch], "late_grad_then", HBM)
    late_grad = lax.psum_scatter(late_grad.reshape(-1, s.cell), PLANE, scatter_dimension=0, tiled=True)
    branch_near = from_chips(grad_branch)
    out_near, out_far = call(
        mlp_out(s),
        [shape(half_rows)] * 2,
        [Far(hidden), Far(down)],
        after=[grad_branch],
        flops=2 * s.rows * s.width * s.hidden,
        large=54,
        name="mlp_out",
    )
    out_far, *branch_near[1:] = tie([out_far, *branch_near[1:]], [], "branch_then")
    branch_blocks = with_cores(branch_near)
    output_parts, out_sent = ring_scatter(out_near, from_core(out_far), "output")

    moved = (out_slice, probs, linear, cosine, sine, query, key, value, normed_one, head_weight)
    (out_grad,) = call(
        out_weight_grads(s),
        [Far(shape((s.query, s.width)))],
        [*branch_blocks, Far(mixed)],
        any_first=8,
        near=(0,),
        scratch=[pltpu.VMEM((s.rows, s.width), BF), eight],
        flops=2 * s.rows * s.width * s.query,
        large=54,
        name="out_weight_grads",
    )
    out_parts = lax.all_to_all(out_grad.reshape(16, s.row, s.width), PLANE, 0, 0, tiled=True)
    near, far, owned, mark = call(
        head_back(s),
        [
            Far(shape(half_rows)),
            Far(shape(half_rows)),
            Far(shape((128, s.row, s.cell + HEAD_SIZE))),
        ],
        [*branch_blocks, *[Far(v, later=True) for v in moved]]
        + [gain_query, gain_key, gain_one, gain_two_terms, owner, lane],
        any_first=8,
        near=(0,),
        after=out_sent,
        scratch=[
            pltpu.VMEM((s.rows, s.width), BF),
            pltpu.VMEM((s.rows, s.query), BF),
            pltpu.VMEM((s.rows, s.cell), BF),
            pltpu.VMEM((1, count), F32),
            eight,
        ],
        hidden=True,
        large=54,
        mark=True,
        name="head_back",
    )
    (block_output,) = call(output_end(s), [shape(block)], [*output_parts, hidden_two], name="output_end")
    (out_lines,) = call(plane_sum(s), [shape((s.row, s.width))], [out_parts], after=[mark], name="plane_sum")
    owned, far = tie([owned, far], [block_output, out_lines], "head_grads_then")
    owned = lax.all_to_all(owned, AXES, 0, 0, tiled=True)
    parts, sent = ring_scatter(near, from_core(far), "input")
    (late_grad,) = tie([late_grad], sent[:1], "late_grad_last")
    input_grad, input_mark = call(
        input_end(s), [shape(block, F32)], [*parts, tokens, grad_hidden_two, gain_one], mark=True, name="input_end"
    )

    home = [(to, own) for own, to in row_route()]
    mlp_end = SHARE * s.mlp_rows
    columns = lax.all_to_all(late_grad[:mlp_end].reshape(SHARE, s.mlp_rows, s.cell), RING, 0, 0, tiled=True)
    lines = lax.ppermute(late_grad[mlp_end:], AXES, home)
    out_lines = lax.ppermute(out_lines, AXES, home)

    def states(*groups):
        return [Far(a) for group in groups for a in group]

    mlp_states = states(
        (gate_weight, gate_first, gate_second),
        (up_weight, up_first, up_second),
        (down_weight, down_first, down_second),
    )
    mlp_new = call(
        mlp_update(s),
        [Far(shape(a.value.shape, F32)) for a in mlp_states],
        [columns, lines] + mlp_states,
        after=[Far(owned), input_mark],
        mark=True,
        large=62,
        name="mlp_update",
    )
    head_states = states(
        (query_weight, query_first, query_second),
        (key_matrix, key_first_moment, key_second_moment),
        (value_matrix, value_first_moment, value_second_moment),
        (out_weight, out_first, out_second),
    )
    gains_state = [a[None] for a in (norm_gains, gains_first, gains_second)]
    head_new = call(
        head_update(s),
        [Far(shape(a.value.shape, F32)) for a in head_states] + [shape(a.shape, F32) for a in gains_state],
        [owned, out_lines] + head_states + gains_state,
        after=[mlp_new[-1]],
        large=62,
        name="head_update",
    )
    return (block_output, input_grad, *head_new[:12], *mlp_new[:9], *[value[0] for value in head_new[12:]])


def solution(mesh):
    fine = Mesh(mesh.devices.reshape(SIZES), AXES)
    matrix, vector, grouped = P(AXES, None), P(AXES), P(("z", "xl", "y"), None)
    states = (matrix,) * 7 + (vector,)
    return jax.shard_map(
        local,
        mesh=fine,
        in_specs=(matrix, matrix, grouped, grouped) + states * 3,
        out_specs=(matrix, matrix) + (matrix,) * 21 + (vector,) * 3,
        check_vma=False,
    )
```

```python
import math

import jax
import jax.numpy as jnp
import ml_dtypes
import numpy as np
from jax import lax
from jax.experimental import pallas as pl
from jax.experimental.pallas import tpu as pltpu
from jax.sharding import Mesh
from jax.sharding import PartitionSpec as P

MODEL_WIDTH = 2048
QUERY_HEADS = 16
KEY_VALUE_HEADS = 8
HEAD_SIZE = 128
FF = 6144
TOK_DEV = 128
STEP = 10

EPS = 1e-06
THETA = 1000000.0
BETA_ONE = 0.9
BETA_TWO = 0.95
ADAM_EPS = 1e-08
DECAY = 0.1

AXES = ("z", "xl", "y", "xh", "c")
SIZES = (4, 2, 4, 2, 2)
RING = ("xl", "xh", "c")
PLANE = ("z", "y")
CHIPS = ("xl", "xh")
SHARE = 8
OFFSETS = (0, 2, 1, 3)
BF = jnp.bfloat16
F32 = jnp.float32


def chip_number(x):
    return (x % 2) * 2 + x // 2


def from_chip(value, offset):
    pairs = [(chip_number((x + offset) % 4), chip_number(x)) for x in range(4)]
    return lax.ppermute(value, CHIPS, pairs)


def from_core(value):
    return lax.ppermute(value, "c", [(0, 1), (1, 0)])


def row_route():
    pairs = []
    for z in range(4):
        for xl in range(2):
            for y in range(4):
                for xh in range(2):
                    for c in range(2):
                        own = (((z * 2 + xl) * 4 + y) * 2 + xh) * 2 + c
                        part = 2 * z + xl
                        to = (((y * 2 + part // 4) * 4 + (xh * 2 + c)) * 2 + (part // 2) % 2) * 2 + part % 2
                        pairs.append((own, to))
    return pairs


def from_chips(block):
    return [block] + [from_chip(block, offset) for offset in OFFSETS[1:]]


def with_cores(near):
    return near + [from_core(value) for value in near]


def row_blocks():
    return [group * 4 + core * 2 + chip for core in range(2) for group in range(2) for chip in range(2)]


def dot(left, right):
    return jnp.dot(left, right, preferred_element_type=F32)


def dot_last(left, right):
    return lax.dot_general(left, right, (((1,), (1,)), ((), ())), preferred_element_type=F32)


def dot_first(left, right):
    return lax.dot_general(left, right, (((0,), (0,)), ((), ())), preferred_element_type=F32)


def inverse_rms(values):
    return lax.rsqrt(jnp.mean(values * values, axis=-1, keepdims=True) + EPS)


class Arriving:
    def __init__(self, source, buffer, sem):
        self.buffer, self.shape, self.here = buffer, buffer.shape, False
        self.copy = pltpu.make_async_copy(source, buffer, sem)

    def start(self):
        self.copy.start()

    def wait(self):
        if not self.here:
            self.copy.wait()
        self.here = True

    def __getitem__(self, index):
        self.wait()
        return self.buffer[index]


class Leaving:
    def __init__(self, buffer, target, sem):
        self.buffer, self.shape, self.sent = buffer, buffer.shape, False
        self.copy = pltpu.make_async_copy(buffer, target, sem)

    def __getitem__(self, index):
        return self.buffer[index]

    def __setitem__(self, index, value):
        self.buffer[index] = value

    def send(self):
        self.sent = True
        self.copy.start()


def bytes_of(values):
    return sum(math.prod(v.shape) * jnp.dtype(v.dtype).itemsize for v in values)


class Far:
    def __init__(self, value, later=False):
        self.value, self.later = value, later


HBM = pl.BlockSpec(memory_space=pltpu.HBM)
ANY = pl.BlockSpec(memory_space=pl.ANY)


def order_specs(after):
    return [HBM if isinstance(a, Far) else ANY for a in after], [a.value if isinstance(a, Far) else a for a in after]


def call(body, outs, args, after=(), scratch=(), flops=0, any_first=0, any_out=False, scalars=0, near=(), hidden=False, large=False, mark=False, name=None):
    if mark:
        outs = [*outs, shape((8, 128), F32)]
    after_specs, after = order_specs(after)
    far_in = [isinstance(a, Far) for a in args]
    later = [isinstance(a, Far) and a.later for a in args]
    far_out = [isinstance(o, Far) for o in outs]
    args = [a.value if isinstance(a, Far) else a for a in args]
    outs = [o.value if isinstance(o, Far) else o for o in outs]
    size = bytes_of((*args, *outs))
    held = bytes_of(args[any_first:]) + bytes_of(() if any_out else outs)
    held += bytes_of([v for v in scratch if v.memory_space == pltpu.VMEM])
    moved = [v for v, far in zip((*args, *outs), far_in + far_out) if far]
    n_in, n_out, n_move = len(args), len(outs), len(moved)

    def run(*refs):
        ins, refs = list(refs[:n_in]), refs[n_in + len(after) :]
        results, refs = list(refs[:n_out]), refs[n_out:]
        own, refs = refs[: len(scratch)], refs[len(scratch) :]
        buffers, sems = list(refs[:n_move]), list(refs[n_move:])
        for i, far in enumerate(far_in):
            if far:
                ins[i] = Arriving(ins[i], buffers.pop(0), sems.pop(0))
                if not later[i]:
                    ins[i].start()
        for i, far in enumerate(far_out):
            if far:
                results[i] = Leaving(buffers.pop(0), results[i], sems.pop(0))
        if mark:
            results[-1][...] = jnp.zeros((8, 128), F32)
        body(*ins, *(results[:-1] if mark else results), *own)
        for value in ins:
            if isinstance(value, Arriving):
                value.wait()
        for value in results:
            if isinstance(value, Leaving) and not value.sent:
                value.send()
        for value in results:
            if isinstance(value, Leaving):
                value.copy.wait()

    def spec(far):
        return HBM if far else pl.BlockSpec(memory_space=pltpu.VMEM)

    in_specs = [spec(far or (i < any_first and i not in near)) for i, far in enumerate(far_in)]
    in_specs[:scalars] = [pl.BlockSpec(memory_space=pltpu.SMEM)] * scalars

    return pl.pallas_call(
        run,
        out_shape=tuple(outs),
        in_specs=in_specs + after_specs,
        out_specs=tuple(spec(far or (any_out and i == 0)) for i, far in enumerate(far_out)),
        scratch_shapes=list(scratch)
        + [pltpu.VMEM(v.shape, v.dtype) for v in moved]
        + [pltpu.SemaphoreType.DMA for _ in moved],
        compiler_params=pltpu.CompilerParams(vmem_limit_bytes=large * 2**20 if large else held + 12 * 2**20),
        cost_estimate=pl.CostEstimate(flops=flops, bytes_accessed=0 if hidden else size, transcendentals=0),
        name=name,
    )(*args, *after)


def tie(values, after, name, spec=ANY):
    count = len(values)
    after_specs, after = order_specs(after)

    def body(*refs):
        pass

    return pl.pallas_call(
        body,
        out_shape=tuple(jax.ShapeDtypeStruct(v.shape, v.dtype) for v in values),
        in_specs=[spec] * count + after_specs,
        out_specs=tuple(spec for _ in values),
        input_output_aliases={i: i for i in range(count)},
        name=name,
    )(*values, *after)


def shape(dims, dtype=BF):
    return jax.ShapeDtypeStruct(tuple(dims), dtype)


class Sizes:
    def __init__(self):
        self.width = MODEL_WIDTH
        self.heads = QUERY_HEADS // SHARE
        self.query = self.heads * HEAD_SIZE
        self.cell = self.query + 2 * HEAD_SIZE
        self.hidden = FF // SHARE
        self.row = MODEL_WIDTH // 128
        self.down_row = FF // 128
        self.out_parts = self.width // self.cell
        self.mlp_parts = 2 * self.hidden // self.cell
        self.ring_rows = SHARE * self.row
        self.mlp_rows = self.mlp_parts * self.row
        self.out_rows = self.out_parts * self.row
        self.down_rows = self.out_parts * self.down_row
        self.early = self.ring_rows + self.out_rows + self.row
        self.late = SHARE * self.mlp_rows + self.down_rows
        self.gains = (2 * MODEL_WIDTH + 2 * HEAD_SIZE) // 128
        self.block = TOK_DEV
        self.rows = 8 * TOK_DEV
        self.group = 4 * TOK_DEV
        self.half = 2 * TOK_DEV


def pack_weights(s):
    def body(query, key, value, out, gate, up, down, gains, columns, lines):
        for j in range(SHARE):
            q, h = s.query, HEAD_SIZE
            columns[j, : s.row, :q] = query[:, j * q : (j + 1) * q].astype(BF)
            columns[j, : s.row, q : q + h] = key[:, j * h : (j + 1) * h].astype(BF)
            columns[j, : s.row, q + h :] = value[:, j * h : (j + 1) * h].astype(BF)
            for source, start in ((gate, 0), (up, s.hidden)):
                done = 0
                while done < s.hidden:
                    at = start + done
                    part, inside = at // s.cell, at % s.cell
                    size = min(s.cell - inside, s.hidden - done)
                    columns[j, s.row * (1 + part) : s.row * (2 + part), inside : inside + size] = source[
                        :, j * s.hidden + done : j * s.hidden + done + size
                    ].astype(BF)
                    done += size
            columns[j, s.row + s.mlp_rows :, :] = jnp.zeros((s.row, s.cell), BF)
            columns[j, s.row + s.mlp_rows :, : s.gains] = jnp.broadcast_to(gains[...], (s.row, s.gains)).astype(BF)
        for p in range(s.out_parts):
            lines[p * s.row : (p + 1) * s.row] = out[:, p * s.cell : (p + 1) * s.cell].astype(BF)
            at = s.out_rows + p * s.down_row
            lines[at : at + s.down_row] = down[:, p * s.cell : (p + 1) * s.cell].astype(BF)

    return body


def place_weights(s):
    def body(columns, lines, early, late, table):
        gain_at = s.row + s.mlp_rows
        table[...] = jnp.zeros_like(table)
        for j in range(SHARE):
            early[j * s.row : (j + 1) * s.row] = columns[j, : s.row]
            late[j * s.mlp_rows : (j + 1) * s.mlp_rows] = columns[j, s.row : gain_at]
            table[j : j + 1] = columns[j, gain_at : gain_at + s.row].astype(F32)[:1]
        early[s.ring_rows : s.ring_rows + s.out_rows] = lines[: s.out_rows]
        early[s.ring_rows + s.out_rows :] = table[...].astype(BF)
        late[SHARE * s.mlp_rows :] = lines[s.out_rows :]

    return body


def fill_head_weight(s, early, target):
    part = 4 * s.row
    for z in range(4):
        for xl in range(2):
            for y in range(4):
                at = ((z * 2 + xl) * 4 + y) * part
                target[at : at + part] = early[z * 4 + y, xl * part : (xl + 1) * part]


def fill_out_weight(s, early, target):
    for f in range(16):
        for p in range(s.out_parts):
            at = s.ring_rows + p * s.row
            target[f * s.row : (f + 1) * s.row, p * s.cell : (p + 1) * s.cell] = early[f, at : at + s.row]


def turn(value):
    return pltpu.roll(value, HEAD_SIZE // 2, 1)


def head_forward(s):
    scale = HEAD_SIZE ** (-0.5)

    def body(*refs):
        blocks = refs[:8]
        early, cosine, sine, bias, gain_one, gain_query, gain_key = refs[8:15]
        weight, out_weight, normed, linear, probs, query, key, value, mixed, near, far = refs[15:]
        for ref, at in zip(blocks, row_blocks()):
            wide = ref[...].astype(F32)
            normed[at * s.block : (at + 1) * s.block] = (wide * inverse_rms(wide) * gain_one[...]).astype(BF)
        normed.send()
        fill_head_weight(s, early, weight)
        weight.send()
        q, h = s.query, HEAD_SIZE
        for group in range(2):
            rows = pl.ds(group * s.group, s.group)
            lin = dot(normed[rows], weight[...])
            linear[rows] = lin[:, : q + h]
            value[rows] = lin[:, q + h :].astype(BF)
            cos, sin = cosine[rows], sine[rows]

            def turned(part, gain):
                part = part * inverse_rms(part) * gain[...]
                return (part * cos + turn(part) * sin).astype(BF)

            key[rows] = turned(lin[:, q : q + h], gain_key)
            for r in range(s.heads):
                query[rows, r * h : (r + 1) * h] = turned(lin[:, r * h : (r + 1) * h], gain_query)
        linear.send()
        fill_out_weight(s, early, out_weight)
        out_weight.send()
        for group in range(2):
            rows = pl.ds(group * s.group, s.group)
            for r in range(s.heads):
                score = dot_last(query[rows, r * h : (r + 1) * h], key[rows]) * scale + bias[group]
                expo = jnp.exp(score - jnp.max(score, axis=-1, keepdims=True))
                prob = expo * (1.0 / jnp.sum(expo, axis=-1, keepdims=True))
                probs[group * s.heads + r] = prob
                mixed[rows, r * h : (r + 1) * h] = dot(prob.astype(BF), value[rows]).astype(BF)
        probs.send()
        for target, core in ((far, 1), (near, 0)):
            for group in range(2):
                rows = pl.ds(group * s.group + core * s.half, s.half)
                target[pl.ds(group * s.half, s.half)] = dot(mixed[rows], out_weight[...]).astype(BF)
            if core:
                far.send()

    return body


def ring_add(s):
    def body(near, arrived, own, *others):
        own[...] = near[: s.block].astype(F32) + arrived[: s.block].astype(F32)
        for i, other in enumerate(others):
            rows = pl.ds((i + 1) * s.block, s.block)
            other[...] = (near[rows].astype(F32) + arrived[rows].astype(F32)).astype(BF)

    return body


def total_of(own, parts):
    total = own[...]
    for part in parts:
        total = total + part[...].astype(F32)
    return total


def branch_end(s):
    def body(own, first, second, third, tokens, gain_two, hidden_two, normed):
        value = tokens[...].astype(F32) + total_of(own, (first, second, third))
        hidden_two[...] = value
        normed[...] = (value * inverse_rms(value) * gain_two[...]).astype(BF)

    return body


def norm_back(values, gain, grad):
    scale = inverse_rms(values)
    normalized = values * scale
    inner = grad * gain
    back = scale * inner - normalized * scale * jnp.mean(inner * normalized, axis=-1, keepdims=True)
    return back, grad * normalized


def gather_into(s, blocks, buffer, sems):
    copies = {}
    for i, (ref, at) in enumerate(zip(blocks, row_blocks())):
        copies[at] = pltpu.make_async_copy(ref, buffer.at[pl.ds(at * s.block, s.block)], sems.at[i])
        copies[at].start()
    return copies


def wait_all(copies):
    for copy in copies.values():
        copy.wait()


def mlp_block(s):
    step = 2 * HEAD_SIZE

    def body(*refs):
        blocks, upstream_blocks, gathered = refs[:8], refs[8:16], refs[16]
        down, hidden, grads, far, near, normed, upstream, weight, grad_hidden, late, sems, up_sems, late_sems = refs[17:]
        copies = gather_into(s, upstream_blocks, upstream, up_sems)
        split = SHARE * s.mlp_rows
        arriving = []
        for i, rows in enumerate((pl.ds(split, s.down_rows), pl.ds(0, split))):
            arriving.append(pltpu.make_async_copy(gathered.at[:, rows], late.at[:, rows], late_sems.at[i]))
            arriving[i].start()
        normed_copies = gather_into(s, blocks, normed, sems)
        arriving[0].wait()
        for f in range(16):
            for p in range(s.out_parts):
                start = SHARE * s.mlp_rows + p * s.down_row
                down[f * s.down_row : (f + 1) * s.down_row, p * s.cell : (p + 1) * s.cell] = late[
                    f, start : start + s.down_row
                ]
        down.send()
        wait_all(copies)
        for n in range(s.hidden // step):
            columns = slice(n * step, (n + 1) * step)
            grad_hidden[:, columns] = dot_last(upstream[...], down[columns])
        arriving[1].wait()
        for f in range(16):
            z, y = divmod(f, 4)
            for j in range(SHARE):
                xl, part = divmod(j, 4)
                at = (((z * 2 + xl) * 4 + y) * 4 + part) * s.row
                for p in range(s.mlp_parts):
                    start = j * s.mlp_rows + p * s.row
                    weight[at : at + s.row, p * s.cell : (p + 1) * s.cell] = late[f, start : start + s.row]
        wait_all(normed_copies)
        for n in range(s.hidden // step):
            columns = slice(n * step, (n + 1) * step)
            second = slice(s.hidden + n * step, s.hidden + (n + 1) * step)
            gate = dot(normed[...], weight[:, columns])
            up = dot(normed[...], weight[:, second])
            sigma = jax.nn.sigmoid(gate)
            active = gate * sigma
            hidden[:, columns] = (active * up).astype(BF)
            grad = grad_hidden[:, columns]
            grads[:, columns] = (grad * up * (sigma * (1.0 + gate * (1.0 - sigma)))).astype(BF)
            grads[:, second] = (grad * active).astype(BF)
        hidden.send()
        grads.send()
        for target, core in ((far, 1), (near, 0)):
            for n in range(s.width // step):
                columns = slice(n * step, (n + 1) * step)
                for group in range(2):
                    rows = pl.ds(group * s.group + core * s.half, s.half)
                    part = dot_last(grads[rows], weight[columns])
                    target[pl.ds(group * s.half, s.half), columns] = part.astype(BF)
            target.send()

    return body


def mlp_weight_grads(s):
    step = 4 * s.row * 4

    def body(*refs):
        normed_blocks, blocks = refs[:8], refs[8:16]
        grads, hidden, target, normed, upstream, made, normed_sems, sems, out_sems = refs[16:]
        normed_copies = gather_into(s, normed_blocks, normed, normed_sems)
        copies = gather_into(s, blocks, upstream, sems)
        leaving = []
        grads.start()
        hidden.start()
        wait_all(normed_copies)
        for z in range(4):
            for xl in range(2):
                at = (z * 2 + xl) * step
                tile = dot_first(normed[:, at : at + step], grads[...]).astype(BF)
                for y in range(4):
                    for part in range(4):
                        line = (y * 4 + part) * s.row
                        for p in range(s.mlp_parts):
                            start = (xl * 4 + part) * s.mlp_rows + p * s.row
                            made[z * 4 + y, start : start + s.row] = tile[
                                line : line + s.row, p * s.cell : (p + 1) * s.cell
                            ]
            if z % 2:
                pair = z // 2
                if pair == 0:
                    wait_all(copies)
                wide = s.hidden // 2
                columns = hidden[:, pair * wide : (pair + 1) * wide]
                for p in range(s.out_parts):
                    tile = dot_first(columns, upstream[:, p * s.cell : (p + 1) * s.cell]).astype(BF)
                    for f in range(8):
                        start = SHARE * s.mlp_rows + p * s.down_row
                        made[pair * 8 + f, start : start + s.down_row] = tile[f * s.down_row : (f + 1) * s.down_row]
                half = pl.ds(pair * 8, 8)
                copy = pltpu.make_async_copy(made.at[half], target.at[half], out_sems.at[pair])
                copy.start()
                leaving.append(copy)
        for copy in leaving:
            copy.wait()

    return body


def mlp_out(s):
    step = 4 * HEAD_SIZE

    def body(hidden, down, near, far):
        for target, core in ((far, 1), (near, 0)):
            for group in range(2):
                rows = pl.ds(group * s.group + core * s.half, s.half)
                for n in range(s.width // step):
                    columns = slice(n * step, (n + 1) * step)
                    target[pl.ds(group * s.half, s.half), columns] = dot(hidden[rows], down[:, columns]).astype(BF)

    return body


def mlp_back_end(s):
    def body(own, first, second, third, cotangent, hidden_two, gain_two, grad_hidden_two, low, terms):
        grad = total_of(own, (first, second, third))
        back, gains = norm_back(hidden_two[...], gain_two[...], grad)
        value = cotangent[...].astype(F32) + back
        grad_hidden_two[...] = value
        low[...] = value.astype(BF)
        terms[...] = jnp.sum(gains, axis=0, keepdims=True)

    return body


def out_weight_grads(s):
    def body(*refs):
        mixed, out_grad, branch, sems = refs[8:]
        wait_all(gather_into(s, refs[:8], branch, sems))
        for p in range(s.out_parts):
            columns = slice(p * s.cell, (p + 1) * s.cell)
            out_grad[:, columns] = dot_first(mixed[...], branch[:, columns]).astype(BF)

    return body


def head_back(s):
    scale = HEAD_SIZE ** (-0.5)

    def body(*refs):
        blocks = refs[:8]
        out_weight, probs, linear, cosine, sine, query, key, value, normed, weight = refs[8:18]
        gain_query, gain_key, gain_one, gain_two_terms, owner, lane = refs[18:24]
        near, far, owned_rows, branch, grad_mixed, grads, gain_row, sems = refs[24:]
        copies = gather_into(s, blocks, branch, sems)
        for later in (out_weight, probs, linear, cosine, sine, query, key, value, normed, weight):
            later.start()
        q, h = s.query, HEAD_SIZE
        query_sum = jnp.zeros((1, h), F32)
        key_sum = jnp.zeros((1, h), F32)
        for group in range(2):
            rows = pl.ds(group * s.group, s.group)
            for at in range(group * 4, group * 4 + 4):
                copies[at].wait()
            grad_mixed[rows] = dot_last(branch[rows], out_weight[...]).astype(BF)
            cos, sin = cosine[rows], sine[rows]
            key_grad = jnp.zeros((s.group, h), F32)
            value_grad = jnp.zeros((s.group, h), F32)
            for r in range(s.heads):
                columns = slice(r * h, (r + 1) * h)
                prob = probs[group * s.heads + r]
                out = grad_mixed[rows, columns]
                grad_prob = dot_last(out, value[rows])
                inner = jnp.sum(prob * grad_prob, axis=-1, keepdims=True)
                grad_score = (prob * (grad_prob - inner)).astype(BF)
                value_grad = value_grad + dot_first(prob.astype(BF), out)
                key_grad = key_grad + dot_first(grad_score, query[rows, columns]) * scale
                turned = dot(grad_score, key[rows]) * scale
                back, terms = norm_back(
                    linear[rows, columns], gain_query[...], turned * cos - turn(turned) * sin
                )
                grads[rows, columns] = back.astype(BF)
                query_sum = query_sum + jnp.sum(terms, axis=0, keepdims=True)
            back, terms = norm_back(
                linear[rows, q : q + h], gain_key[...], key_grad * cos - turn(key_grad) * sin
            )
            grads[rows, q : q + h] = back.astype(BF)
            key_sum = key_sum + jnp.sum(terms, axis=0, keepdims=True)
            grads[rows, q + h :] = value_grad.astype(BF)
        wide = 4 * HEAD_SIZE
        for n in range(s.width // wide):
            columns = slice(n * wide, (n + 1) * wide)
            total = jnp.zeros((1, wide), F32)
            for target, core in ((far, 1), (near, 0)):
                for group in range(2):
                    rows = pl.ds(group * s.group + core * s.half, s.half)
                    part = dot_last(grads[rows], weight[columns])
                    target[pl.ds(group * s.half, s.half), columns] = part.astype(BF)
                    total = total + jnp.sum(part * normed[rows, columns].astype(F32), axis=0, keepdims=True)
            gain_row[:, columns] = total / gain_one[:, columns]
        far.send()
        near.send()
        gain_row[:, s.width : 2 * s.width] = gain_two_terms[...]
        gain_row[:, 2 * s.width : 2 * s.width + h] = query_sum
        gain_row[:, 2 * s.width + h :] = key_sum
        owned = dot((owner[...].astype(F32) * gain_row[...]).astype(BF), lane[...])
        for o in range(128):
            owned_rows[o, :, s.cell :] = jnp.broadcast_to(owned[o : o + 1], (s.row, h)).astype(BF)
        step = 16 * s.row
        for n in range(8):
            tile = dot_first(normed[:, n * step : (n + 1) * step], grads[...]).astype(BF)
            owned_rows[n * 16 : (n + 1) * 16, :, : s.cell] = tile.reshape(16, s.row, s.cell)

    return body


def plane_sum(s):
    def body(parts, total):
        value = parts[0].astype(F32)
        for f in range(1, 16):
            value = value + parts[f].astype(F32)
        total[...] = value.astype(BF)

    return body


def input_end(s):
    def body(own, first, second, third, tokens, grad_hidden_two, gain_one, input_grad):
        back, _ = norm_back(tokens[...].astype(F32), gain_one[...], total_of(own, (first, second, third)))
        input_grad[...] = grad_hidden_two[...] + back

    return body


def output_end(s):
    def body(own, first, second, third, hidden_two, block_output):
        block_output[...] = (hidden_two[...] + total_of(own, (first, second, third))).astype(BF)

    return body


def adam(weight, grad, first, second, rate, decay):
    first_new = BETA_ONE * first + (1.0 - BETA_ONE) * grad
    second_new = BETA_TWO * second + (1.0 - BETA_TWO) * grad * grad
    first_hat = first_new / (1.0 - BETA_ONE**STEP)
    second_hat = second_new / (1.0 - BETA_TWO**STEP)
    weight_new = weight - rate * (first_hat / (jnp.sqrt(second_hat) + ADAM_EPS) + decay * weight)
    return (weight_new, first_new, second_new)


def step_into(ins, outs, columns, grad, rate, decay):
    results = adam(ins[0][:, columns], grad.astype(F32), ins[1][:, columns], ins[2][:, columns], rate, decay)
    for out, value in zip(outs, results):
        out[:, columns] = value


def split_refs(refs, first, count):
    ins = [refs[first + 3 * i : first + 3 * i + 3] for i in range(count)]
    outs = [refs[first + 3 * (count + i) : first + 3 * (count + i) + 3] for i in range(count)]
    return ins, outs


def send_all(outs):
    for out in outs:
        out.send()


def head_update(s):
    def body(*refs):
        owned, lines = refs[:2]
        ins, outs = split_refs(refs, 2, 5)
        rate = MODEL_WIDTH ** (-0.5)
        out_rate = (TOK_DEV / (QUERY_HEADS * HEAD_SIZE)) ** 0.5
        gain_grad = jnp.zeros((s.row, HEAD_SIZE), F32)
        for j in range(SHARE):
            xl, part = divmod(j, 4)
            grad = jnp.zeros((s.row, s.cell), F32)
            for z in range(4):
                for y in range(4):
                    source = ((z * 2 + xl) * 4 + y) * 4 + part
                    grad = grad + owned[source, :, : s.cell].astype(F32)
                    gain_grad = gain_grad + owned[source, :, s.cell :].astype(F32)
            start = 0
            for i, size in enumerate((s.query, HEAD_SIZE, HEAD_SIZE)):
                columns = slice(j * size, (j + 1) * size)
                step_into(ins[i], outs[i], columns, grad[:, start : start + size], rate, DECAY)
                start += size
        for i in range(3):
            send_all(outs[i])
        for p in range(s.out_parts):
            columns = slice(p * s.cell, (p + 1) * s.cell)
            step_into(ins[3], outs[3], columns, lines[:, columns], out_rate, DECAY)
        send_all(outs[3])
        step_into(ins[4], outs[4], slice(0, s.gains), gain_grad[:1, : s.gains], 0.5, 0.0)

    return body


def mlp_update(s):
    def body(*refs):
        columns, lines = refs[:2]
        ins, outs = split_refs(refs, 2, 3)
        for i, start in ((0, 0), (1, s.hidden)):
            for j in range(SHARE):
                done = 0
                while done < s.hidden:
                    at = start + done
                    part, inside = at // s.cell, at % s.cell
                    size = min(s.cell - inside, s.hidden - done)
                    grad = columns[j, part * s.row : (part + 1) * s.row, inside : inside + size]
                    own = slice(j * s.hidden + done, j * s.hidden + done + size)
                    step_into(ins[i], outs[i], own, grad, MODEL_WIDTH ** (-0.5), DECAY)
                    done += size
            send_all(outs[i])
        for p in range(s.out_parts):
            grad = lines[p * s.down_row : (p + 1) * s.down_row]
            step_into(ins[2], outs[2], slice(p * s.cell, (p + 1) * s.cell), grad, FF ** (-0.5), DECAY)

    return body


def layout(table, other):
    span = TOK_DEV // 2
    both = jnp.stack([table, other])
    sizes, spans = both[:, :2], both[:, 2:]
    chip = lax.axis_index("xh") * 2 + lax.axis_index("xl")
    core = lax.axis_index("c")
    offset = jnp.arange(2)[:, None, None] + 2 * jnp.arange(2)[None, None, :]
    place = ((chip + offset) % 4) // 2 * 2 + (core + jnp.arange(2)[None, :, None]) % 2
    block = (2 * place[..., None] + jnp.arange(2)).reshape(2, 8)
    owner = jnp.sum(jnp.where(block[:, :, None] == jnp.arange(8), spans[:, None, :], 0), axis=-1)
    slots = (owner[:, :, None] * span + jnp.arange(span)).reshape(2, -1)
    ends = jnp.cumsum(sizes, axis=1)
    passed = slots[:, :, None] >= ends[:, None, :]
    sequence = jnp.sum(passed.astype(jnp.int32), axis=-1)
    position = slots - jnp.sum(jnp.where(passed, sizes[:, None, :], 0), axis=-1)
    return slots, sequence, position


def local(
    tokens,
    cotangent,
    lengths,
    span_ids,
    query_weight,
    key_matrix,
    value_matrix,
    out_weight,
    gate_weight,
    up_weight,
    down_weight,
    norm_gains,
    query_first,
    key_first_moment,
    value_first_moment,
    out_first,
    gate_first,
    up_first,
    down_first,
    gains_first,
    query_second,
    key_second_moment,
    value_second_moment,
    out_second,
    gate_second,
    up_second,
    down_second,
    gains_second,
):
    s = Sizes()
    block = (s.block, s.width)
    half_rows = (s.group, s.width)

    def ring_scatter(near, arrived, name, after=()):
        own, *others = call(
            ring_add(s), [shape(block, F32)] + [shape(block)] * 3, [near, arrived], after=after, name=name + "_add"
        )
        arrived = [from_chip(piece, -OFFSETS[i + 1]) for i, piece in enumerate(others)]
        return [own] + arrived, others

    columns, lines, mark = call(
        pack_weights(s),
        [shape((SHARE, 2 * s.row + s.mlp_rows, s.cell)), shape((s.out_rows + s.down_rows, s.cell))],
        [Far(query_weight), Far(key_matrix), Far(value_matrix), Far(out_weight), Far(gate_weight), Far(up_weight)]
        + [Far(down_weight), norm_gains[None]],
        large=54,
        mark=True,
        name="pack_weights",
    )
    (table,) = tie([jnp.concatenate([lengths[0], span_ids[0]])], [mark], "table_then")
    other_table = lax.ppermute(table, "xl", [(0, 1), (1, 0)])
    (tokens_then,) = tie([tokens], [mark], "tokens_then", HBM)
    input_near = from_chips(tokens_then)
    inputs = with_cores(input_near)
    columns = lax.all_to_all(columns, RING, 0, 0, tiled=True)
    lines = lax.ppermute(lines, AXES, row_route())

    count = 128 * s.gains
    owner = np.asarray(np.arange(count)[None] // s.gains == np.arange(128)[:, None], ml_dtypes.bfloat16)
    lane = np.asarray(np.arange(count)[:, None] % s.gains == np.arange(HEAD_SIZE)[None], ml_dtypes.bfloat16)

    early, late = call(
        place_weights(s),
        [shape((s.early, s.cell)), shape((s.late, s.cell))],
        [columns, lines],
        after=[other_table],
        scratch=[pltpu.VMEM((s.row, s.cell), F32)],
        name="place_weights",
    )
    early = lax.all_gather(early, PLANE, axis=0)
    (cotangent_then,) = tie([cotangent], [Far(input_near[1])], "cotangent_then", HBM)
    upstream_near = from_chips(cotangent_then)
    slots, sequence, position = layout(table, other_table)
    freq = THETA ** (-(2.0 * jnp.arange(HEAD_SIZE // 2, dtype=F32)) / HEAD_SIZE)
    angle = position.reshape(-1).astype(F32)[:, None] * freq
    cosine, sine = jnp.cos(angle), jnp.sin(angle)
    cosine = jnp.concatenate([cosine, cosine], axis=1)
    sine = jnp.concatenate([-sine, sine], axis=1)
    allowed = (sequence[:, :, None] == sequence[:, None, :]) & (slots[:, None, :] <= slots[:, :, None])
    bias = jnp.where(allowed, 0.0, -1e30).astype(F32)

    (late,) = tie(
        [late], [*inputs[1:], *upstream_near[1:], cosine, sine, bias], "late_then", HBM
    )
    late = lax.all_gather(late, PLANE, axis=0)
    upstream = with_cores(upstream_near)

    gain_at = s.ring_rows + s.out_rows
    gains = early[:, gain_at : gain_at + SHARE, : s.gains].astype(F32)
    gains = gains.reshape(4, 4, 2, -1).transpose(0, 2, 1, 3).reshape(1, -1)
    gain_one = gains[:, : s.width]
    gain_two = gains[:, s.width : 2 * s.width]
    gain_query = gains[:, 2 * s.width : 2 * s.width + HEAD_SIZE]
    gain_key = gains[:, 2 * s.width + HEAD_SIZE :]

    eight = pltpu.SemaphoreType.DMA((8,))
    head_weight, out_slice, normed_one, linear, probs, query, key, value, mixed, near, far = call(
        head_forward(s),
        [
            Far(shape((s.width, s.cell))),
            Far(shape((s.query, s.width))),
            Far(shape((s.rows, s.width))),
            Far(shape((s.rows, s.query + HEAD_SIZE), F32)),
            Far(shape((2 * s.heads, s.group, s.group), F32)),
            shape((s.rows, s.query)),
            shape((s.rows, HEAD_SIZE)),
            shape((s.rows, HEAD_SIZE)),
            shape((s.rows, s.query)),
            shape(half_rows),
            Far(shape(half_rows)),
        ],
        [*[Far(v) for v in inputs], Far(early), Far(cosine), Far(sine), Far(bias), gain_one, gain_query, gain_key],
        flops=2 * s.rows * s.width * (s.cell + s.query),
        large=54,
        name="head_forward",
    )
    parts, _ = ring_scatter(near, from_core(far), "branch")
    hidden_two, normed_two = call(
        branch_end(s), [shape(block, F32), shape(block)], [*parts, tokens, gain_two], name="branch_end"
    )
    normed_blocks = with_cores(from_chips(normed_two))
    down, hidden, grads, far, near = call(
        mlp_block(s),
        [
            Far(shape((s.hidden, s.width))),
            Far(shape((s.rows, s.hidden))),
            Far(shape((s.rows, 2 * s.hidden))),
            Far(shape(half_rows)),
            Far(shape(half_rows)),
        ],
        [*normed_blocks, *upstream, late],
        any_first=17,
        near=(0,),
        scratch=[
            pltpu.VMEM((s.rows, s.width), BF),
            pltpu.VMEM((s.rows, s.width), BF),
            pltpu.VMEM((s.width, 2 * s.hidden), BF),
            pltpu.VMEM((s.rows, s.hidden), F32),
            pltpu.VMEM((16, s.late, s.cell), BF),
            eight,
            eight,
            pltpu.SemaphoreType.DMA((2,)),
        ],
        flops=10 * s.rows * s.width * s.hidden,
        large=60,
        name="mlp_block",
    )
    parts, sent = ring_scatter(near, from_core(far), "mlp_back")
    late_grad, mark = call(
        mlp_weight_grads(s),
        [shape((16, s.late, s.cell))],
        [*normed_blocks, *upstream, Far(grads, later=True), Far(hidden, later=True)],
        any_first=16,
        near=(0,),
        any_out=True,
        after=sent,
        scratch=[
            pltpu.VMEM((s.rows, s.width), BF),
            pltpu.VMEM((s.rows, s.width), BF),
            pltpu.VMEM((16, s.late, s.cell), BF),
            eight,
            eight,
            pltpu.SemaphoreType.DMA((2,)),
        ],
        flops=6 * s.rows * s.width * s.hidden,
        large=54,
        mark=True,
        name="mlp_weight_grads",
    )
    grad_hidden_two, grad_branch, gain_two_terms = call(
        mlp_back_end(s),
        [shape(block, F32), shape(block), shape((1, s.width), F32)],
        [*parts, cotangent, hidden_two, gain_two],
        after=[mark],
        name="mlp_back_end",
    )
    (late_grad,) = tie([late_grad], [grad_branch], "late_grad_then", HBM)
    late_grad = lax.psum_scatter(late_grad.reshape(-1, s.cell), PLANE, scatter_dimension=0, tiled=True)
    branch_near = from_chips(grad_branch)
    out_near, out_far = call(
        mlp_out(s),
        [shape(half_rows)] * 2,
        [Far(hidden), Far(down)],
        after=[grad_branch],
        flops=2 * s.rows * s.width * s.hidden,
        large=54,
        name="mlp_out",
    )
    out_far, *branch_near[1:] = tie([out_far, *branch_near[1:]], [], "branch_then")
    branch_blocks = with_cores(branch_near)
    output_parts, out_sent = ring_scatter(out_near, from_core(out_far), "output")

    moved = (out_slice, probs, linear, cosine, sine, query, key, value, normed_one, head_weight)
    (out_grad,) = call(
        out_weight_grads(s),
        [Far(shape((s.query, s.width)))],
        [*branch_blocks, Far(mixed)],
        any_first=8,
        near=(0,),
        scratch=[pltpu.VMEM((s.rows, s.width), BF), eight],
        flops=2 * s.rows * s.width * s.query,
        large=54,
        name="out_weight_grads",
    )
    out_parts = lax.all_to_all(out_grad.reshape(16, s.row, s.width), PLANE, 0, 0, tiled=True)
    near, far, owned, mark = call(
        head_back(s),
        [
            Far(shape(half_rows)),
            Far(shape(half_rows)),
            Far(shape((128, s.row, s.cell + HEAD_SIZE))),
        ],
        [*branch_blocks, *[Far(v, later=True) for v in moved]]
        + [gain_query, gain_key, gain_one, gain_two_terms, owner, lane],
        any_first=8,
        near=(0,),
        after=out_sent,
        scratch=[
            pltpu.VMEM((s.rows, s.width), BF),
            pltpu.VMEM((s.rows, s.query), BF),
            pltpu.VMEM((s.rows, s.cell), BF),
            pltpu.VMEM((1, count), F32),
            eight,
        ],
        hidden=True,
        large=54,
        mark=True,
        name="head_back",
    )
    (block_output,) = call(output_end(s), [shape(block)], [*output_parts, hidden_two], name="output_end")
    (out_lines,) = call(plane_sum(s), [shape((s.row, s.width))], [out_parts], after=[mark], name="plane_sum")
    owned, far = tie([owned, far], [block_output, out_lines], "head_grads_then")
    owned = lax.all_to_all(owned, AXES, 0, 0, tiled=True)
    parts, sent = ring_scatter(near, from_core(far), "input")
    (late_grad,) = tie([late_grad], sent[:1], "late_grad_last")
    input_grad, input_mark = call(
        input_end(s), [shape(block, F32)], [*parts, tokens, grad_hidden_two, gain_one], mark=True, name="input_end"
    )

    home = [(to, own) for own, to in row_route()]
    mlp_end = SHARE * s.mlp_rows
    columns = lax.all_to_all(late_grad[:mlp_end].reshape(SHARE, s.mlp_rows, s.cell), RING, 0, 0, tiled=True)
    lines = lax.ppermute(late_grad[mlp_end:], AXES, home)
    out_lines = lax.ppermute(out_lines, AXES, home)

    def states(*groups):
        return [Far(a) for group in groups for a in group]

    mlp_states = states(
        (gate_weight, gate_first, gate_second),
        (up_weight, up_first, up_second),
        (down_weight, down_first, down_second),
    )
    head_states = states(
        (query_weight, query_first, query_second),
        (key_matrix, key_first_moment, key_second_moment),
        (value_matrix, value_first_moment, value_second_moment),
        (out_weight, out_first, out_second),
    )
    gains_state = [a[None] for a in (norm_gains, gains_first, gains_second)]
    head_new = call(
        head_update(s),
        [Far(shape(a.value.shape, F32)) for a in head_states] + [shape(a.shape, F32) for a in gains_state],
        [owned, out_lines] + head_states + gains_state,
        mark=True,
        large=62,
        name="head_update",
    )
    mlp_new = call(
        mlp_update(s),
        [Far(shape(a.value.shape, F32)) for a in mlp_states],
        [columns, lines] + mlp_states,
        after=[head_new[-1]],
        large=62,
        name="mlp_update",
    )
    return (block_output, input_grad, *head_new[:12], *mlp_new, *[value[0] for value in head_new[12:15]])


def solution(mesh):
    fine = Mesh(mesh.devices.reshape(SIZES), AXES)
    matrix, vector, grouped = P(AXES, None), P(AXES), P(("z", "xl", "y"), None)
    states = (matrix,) * 7 + (vector,)
    return jax.shard_map(
        local,
        mesh=fine,
        in_specs=(matrix, matrix, grouped, grouped) + states * 3,
        out_specs=(matrix, matrix) + (matrix,) * 21 + (vector,) * 3,
        check_vma=False,
    )
```

```python
import math

import jax
import jax.numpy as jnp
import ml_dtypes
import numpy as np
from jax import lax
from jax.experimental import pallas as pl
from jax.experimental.pallas import tpu as pltpu
from jax.sharding import Mesh
from jax.sharding import PartitionSpec as P

MODEL_WIDTH = 2048
QUERY_HEADS = 16
KEY_VALUE_HEADS = 8
HEAD_SIZE = 128
FF = 6144
TOK_DEV = 128
STEP = 10

EPS = 1e-06
THETA = 1000000.0
BETA_ONE = 0.9
BETA_TWO = 0.95
ADAM_EPS = 1e-08
DECAY = 0.1

AXES = ("z", "xl", "y", "xh", "c")
SIZES = (4, 2, 4, 2, 2)
RING = ("xl", "xh", "c")
PLANE = ("z", "y")
CHIPS = ("xl", "xh")
SHARE = 8
OFFSETS = (0, 2, 1, 3)
BF = jnp.bfloat16
F32 = jnp.float32


def chip_number(x):
    return (x % 2) * 2 + x // 2


def from_chip(value, offset):
    pairs = [(chip_number((x + offset) % 4), chip_number(x)) for x in range(4)]
    return lax.ppermute(value, CHIPS, pairs)


def from_core(value):
    return lax.ppermute(value, "c", [(0, 1), (1, 0)])


def row_route():
    pairs = []
    for z in range(4):
        for xl in range(2):
            for y in range(4):
                for xh in range(2):
                    for c in range(2):
                        own = (((z * 2 + xl) * 4 + y) * 2 + xh) * 2 + c
                        part = 2 * z + xl
                        to = (((y * 2 + part // 4) * 4 + (xh * 2 + c)) * 2 + (part // 2) % 2) * 2 + part % 2
                        pairs.append((own, to))
    return pairs


def from_chips(block):
    return [block] + [from_chip(block, offset) for offset in OFFSETS[1:]]


def with_cores(near):
    return near + [from_core(value) for value in near]


def row_blocks():
    return [group * 4 + core * 2 + chip for core in range(2) for group in range(2) for chip in range(2)]


def dot(left, right):
    return jnp.dot(left, right, preferred_element_type=F32)


def dot_last(left, right):
    return lax.dot_general(left, right, (((1,), (1,)), ((), ())), preferred_element_type=F32)


def dot_first(left, right):
    return lax.dot_general(left, right, (((0,), (0,)), ((), ())), preferred_element_type=F32)


def inverse_rms(values):
    return lax.rsqrt(jnp.mean(values * values, axis=-1, keepdims=True) + EPS)


class Arriving:
    def __init__(self, source, buffer, sem):
        self.buffer, self.shape, self.here = buffer, buffer.shape, False
        self.copy = pltpu.make_async_copy(source, buffer, sem)

    def start(self):
        self.copy.start()

    def wait(self):
        if not self.here:
            self.copy.wait()
        self.here = True

    def __getitem__(self, index):
        self.wait()
        return self.buffer[index]


class Leaving:
    def __init__(self, buffer, target, sem):
        self.buffer, self.shape, self.sent = buffer, buffer.shape, False
        self.copy = pltpu.make_async_copy(buffer, target, sem)

    def __getitem__(self, index):
        return self.buffer[index]

    def __setitem__(self, index, value):
        self.buffer[index] = value

    def send(self):
        self.sent = True
        self.copy.start()


def bytes_of(values):
    return sum(math.prod(v.shape) * jnp.dtype(v.dtype).itemsize for v in values)


class Far:
    def __init__(self, value, later=False):
        self.value, self.later = value, later


HBM = pl.BlockSpec(memory_space=pltpu.HBM)
ANY = pl.BlockSpec(memory_space=pl.ANY)


def order_specs(after):
    return [HBM if isinstance(a, Far) else ANY for a in after], [a.value if isinstance(a, Far) else a for a in after]


def call(body, outs, args, after=(), scratch=(), flops=0, any_first=0, any_out=False, scalars=0, near=(), hidden=False, large=False, mark=False, name=None):
    if mark:
        outs = [*outs, shape((8, 128), F32)]
    after_specs, after = order_specs(after)
    far_in = [isinstance(a, Far) for a in args]
    later = [isinstance(a, Far) and a.later for a in args]
    far_out = [isinstance(o, Far) for o in outs]
    args = [a.value if isinstance(a, Far) else a for a in args]
    outs = [o.value if isinstance(o, Far) else o for o in outs]
    size = bytes_of((*args, *outs))
    held = bytes_of(args[any_first:]) + bytes_of(() if any_out else outs)
    held += bytes_of([v for v in scratch if v.memory_space == pltpu.VMEM])
    moved = [v for v, far in zip((*args, *outs), far_in + far_out) if far]
    n_in, n_out, n_move = len(args), len(outs), len(moved)

    def run(*refs):
        ins, refs = list(refs[:n_in]), refs[n_in + len(after) :]
        results, refs = list(refs[:n_out]), refs[n_out:]
        own, refs = refs[: len(scratch)], refs[len(scratch) :]
        buffers, sems = list(refs[:n_move]), list(refs[n_move:])
        for i, far in enumerate(far_in):
            if far:
                ins[i] = Arriving(ins[i], buffers.pop(0), sems.pop(0))
                if not later[i]:
                    ins[i].start()
        for i, far in enumerate(far_out):
            if far:
                results[i] = Leaving(buffers.pop(0), results[i], sems.pop(0))
        if mark:
            results[-1][...] = jnp.zeros((8, 128), F32)
        body(*ins, *(results[:-1] if mark else results), *own)
        for value in ins:
            if isinstance(value, Arriving):
                value.wait()
        for value in results:
            if isinstance(value, Leaving) and not value.sent:
                value.send()
        for value in results:
            if isinstance(value, Leaving):
                value.copy.wait()

    def spec(far):
        return HBM if far else pl.BlockSpec(memory_space=pltpu.VMEM)

    in_specs = [spec(far or (i < any_first and i not in near)) for i, far in enumerate(far_in)]
    in_specs[:scalars] = [pl.BlockSpec(memory_space=pltpu.SMEM)] * scalars

    return pl.pallas_call(
        run,
        out_shape=tuple(outs),
        in_specs=in_specs + after_specs,
        out_specs=tuple(spec(far or (any_out and i == 0)) for i, far in enumerate(far_out)),
        scratch_shapes=list(scratch)
        + [pltpu.VMEM(v.shape, v.dtype) for v in moved]
        + [pltpu.SemaphoreType.DMA for _ in moved],
        compiler_params=pltpu.CompilerParams(vmem_limit_bytes=large * 2**20 if large else held + 12 * 2**20),
        cost_estimate=pl.CostEstimate(flops=flops, bytes_accessed=0 if hidden else size, transcendentals=0),
        name=name,
    )(*args, *after)


def tie(values, after, name, spec=ANY):
    count = len(values)
    after_specs, after = order_specs(after)

    def body(*refs):
        pass

    return pl.pallas_call(
        body,
        out_shape=tuple(jax.ShapeDtypeStruct(v.shape, v.dtype) for v in values),
        in_specs=[spec] * count + after_specs,
        out_specs=tuple(spec for _ in values),
        input_output_aliases={i: i for i in range(count)},
        name=name,
    )(*values, *after)


def shape(dims, dtype=BF):
    return jax.ShapeDtypeStruct(tuple(dims), dtype)


class Sizes:
    def __init__(self):
        self.width = MODEL_WIDTH
        self.heads = QUERY_HEADS // SHARE
        self.query = self.heads * HEAD_SIZE
        self.cell = self.query + 2 * HEAD_SIZE
        self.hidden = FF // SHARE
        self.row = MODEL_WIDTH // 128
        self.down_row = FF // 128
        self.out_parts = self.width // self.cell
        self.mlp_parts = 2 * self.hidden // self.cell
        self.ring_rows = SHARE * self.row
        self.mlp_rows = self.mlp_parts * self.row
        self.out_rows = self.out_parts * self.row
        self.down_rows = self.out_parts * self.down_row
        self.early = self.ring_rows + self.out_rows + self.row
        self.late = SHARE * self.mlp_rows + self.down_rows
        self.gains = (2 * MODEL_WIDTH + 2 * HEAD_SIZE) // 128
        self.block = TOK_DEV
        self.rows = 8 * TOK_DEV
        self.group = 4 * TOK_DEV
        self.half = 2 * TOK_DEV


def pack_weights(s):
    def body(query, key, value, out, gate, up, down, gains, columns, lines):
        for j in range(SHARE):
            q, h = s.query, HEAD_SIZE
            columns[j, : s.row, :q] = query[:, j * q : (j + 1) * q].astype(BF)
            columns[j, : s.row, q : q + h] = key[:, j * h : (j + 1) * h].astype(BF)
            columns[j, : s.row, q + h :] = value[:, j * h : (j + 1) * h].astype(BF)
            for source, start in ((gate, 0), (up, s.hidden)):
                done = 0
                while done < s.hidden:
                    at = start + done
                    part, inside = at // s.cell, at % s.cell
                    size = min(s.cell - inside, s.hidden - done)
                    columns[j, s.row * (1 + part) : s.row * (2 + part), inside : inside + size] = source[
                        :, j * s.hidden + done : j * s.hidden + done + size
                    ].astype(BF)
                    done += size
            columns[j, s.row + s.mlp_rows :, :] = jnp.zeros((s.row, s.cell), BF)
            columns[j, s.row + s.mlp_rows :, : s.gains] = jnp.broadcast_to(gains[...], (s.row, s.gains)).astype(BF)
        for p in range(s.out_parts):
            lines[p * s.row : (p + 1) * s.row] = out[:, p * s.cell : (p + 1) * s.cell].astype(BF)
            at = s.out_rows + p * s.down_row
            lines[at : at + s.down_row] = down[:, p * s.cell : (p + 1) * s.cell].astype(BF)

    return body


def place_weights(s):
    def body(columns, lines, early, late, table):
        gain_at = s.row + s.mlp_rows
        table[...] = jnp.zeros_like(table)
        for j in range(SHARE):
            early[j * s.row : (j + 1) * s.row] = columns[j, : s.row]
            late[j * s.mlp_rows : (j + 1) * s.mlp_rows] = columns[j, s.row : gain_at]
            table[j : j + 1] = columns[j, gain_at : gain_at + s.row].astype(F32)[:1]
        early[s.ring_rows : s.ring_rows + s.out_rows] = lines[: s.out_rows]
        early[s.ring_rows + s.out_rows :] = table[...].astype(BF)
        late[SHARE * s.mlp_rows :] = lines[s.out_rows :]

    return body


def fill_head_weight(s, early, target):
    part = 4 * s.row
    for z in range(4):
        for xl in range(2):
            for y in range(4):
                at = ((z * 2 + xl) * 4 + y) * part
                target[at : at + part] = early[z * 4 + y, xl * part : (xl + 1) * part]


def fill_out_weight(s, early, target):
    for f in range(16):
        for p in range(s.out_parts):
            at = s.ring_rows + p * s.row
            target[f * s.row : (f + 1) * s.row, p * s.cell : (p + 1) * s.cell] = early[f, at : at + s.row]


def turn(value):
    return pltpu.roll(value, HEAD_SIZE // 2, 1)


def head_forward(s):
    scale = HEAD_SIZE ** (-0.5)

    def body(*refs):
        blocks = refs[:8]
        early, cosine, sine, bias, gain_one, gain_query, gain_key = refs[8:15]
        weight, out_weight, normed, linear, probs, query, key, value, mixed, near, far = refs[15:]
        for ref, at in zip(blocks, row_blocks()):
            wide = ref[...].astype(F32)
            normed[at * s.block : (at + 1) * s.block] = (wide * inverse_rms(wide) * gain_one[...]).astype(BF)
        normed.send()
        fill_head_weight(s, early, weight)
        weight.send()
        q, h = s.query, HEAD_SIZE
        for group in range(2):
            rows = pl.ds(group * s.group, s.group)
            lin = dot(normed[rows], weight[...])
            linear[rows] = lin[:, : q + h]
            value[rows] = lin[:, q + h :].astype(BF)
            cos, sin = cosine[rows], sine[rows]

            def turned(part, gain):
                part = part * inverse_rms(part) * gain[...]
                return (part * cos + turn(part) * sin).astype(BF)

            key[rows] = turned(lin[:, q : q + h], gain_key)
            for r in range(s.heads):
                query[rows, r * h : (r + 1) * h] = turned(lin[:, r * h : (r + 1) * h], gain_query)
        linear.send()
        fill_out_weight(s, early, out_weight)
        out_weight.send()
        for group in range(2):
            rows = pl.ds(group * s.group, s.group)
            for r in range(s.heads):
                score = dot_last(query[rows, r * h : (r + 1) * h], key[rows]) * scale + bias[group]
                expo = jnp.exp(score - jnp.max(score, axis=-1, keepdims=True))
                prob = expo * (1.0 / jnp.sum(expo, axis=-1, keepdims=True))
                probs[group * s.heads + r] = prob
                mixed[rows, r * h : (r + 1) * h] = dot(prob.astype(BF), value[rows]).astype(BF)
        probs.send()
        for target, core in ((far, 1), (near, 0)):
            for group in range(2):
                rows = pl.ds(group * s.group + core * s.half, s.half)
                target[pl.ds(group * s.half, s.half)] = dot(mixed[rows], out_weight[...]).astype(BF)
            if core:
                far.send()

    return body


def ring_add(s):
    def body(near, arrived, own, *others):
        own[...] = near[: s.block].astype(F32) + arrived[: s.block].astype(F32)
        for i, other in enumerate(others):
            rows = pl.ds((i + 1) * s.block, s.block)
            other[...] = (near[rows].astype(F32) + arrived[rows].astype(F32)).astype(BF)

    return body


def total_of(own, parts):
    total = own[...]
    for part in parts:
        total = total + part[...].astype(F32)
    return total


def branch_end(s):
    def body(own, first, second, third, tokens, gain_two, hidden_two, normed):
        value = tokens[...].astype(F32) + total_of(own, (first, second, third))
        hidden_two[...] = value
        normed[...] = (value * inverse_rms(value) * gain_two[...]).astype(BF)

    return body


def norm_back(values, gain, grad):
    scale = inverse_rms(values)
    normalized = values * scale
    inner = grad * gain
    back = scale * inner - normalized * scale * jnp.mean(inner * normalized, axis=-1, keepdims=True)
    return back, grad * normalized


def gather_into(s, blocks, buffer, sems):
    copies = {}
    for i, (ref, at) in enumerate(zip(blocks, row_blocks())):
        copies[at] = pltpu.make_async_copy(ref, buffer.at[pl.ds(at * s.block, s.block)], sems.at[i])
        copies[at].start()
    return copies


def wait_all(copies):
    for copy in copies.values():
        copy.wait()


def mlp_block(s):
    step = 2 * HEAD_SIZE

    def body(*refs):
        blocks, upstream_blocks, gathered = refs[:8], refs[8:16], refs[16]
        down, hidden, grads, far, near, normed, upstream, weight, grad_hidden, late, sems, up_sems, late_sems = refs[17:]
        copies = gather_into(s, upstream_blocks, upstream, up_sems)
        split = SHARE * s.mlp_rows
        arriving = []
        for i, rows in enumerate((pl.ds(split, s.down_rows), pl.ds(0, split))):
            arriving.append(pltpu.make_async_copy(gathered.at[:, rows], late.at[:, rows], late_sems.at[i]))
            arriving[i].start()
        normed_copies = gather_into(s, blocks, normed, sems)
        arriving[0].wait()
        for f in range(16):
            for p in range(s.out_parts):
                start = SHARE * s.mlp_rows + p * s.down_row
                down[f * s.down_row : (f + 1) * s.down_row, p * s.cell : (p + 1) * s.cell] = late[
                    f, start : start + s.down_row
                ]
        down.send()
        wait_all(copies)
        for n in range(s.hidden // step):
            columns = slice(n * step, (n + 1) * step)
            grad_hidden[:, columns] = dot_last(upstream[...], down[columns])
        arriving[1].wait()
        for f in range(16):
            z, y = divmod(f, 4)
            for j in range(SHARE):
                xl, part = divmod(j, 4)
                at = (((z * 2 + xl) * 4 + y) * 4 + part) * s.row
                for p in range(s.mlp_parts):
                    start = j * s.mlp_rows + p * s.row
                    weight[at : at + s.row, p * s.cell : (p + 1) * s.cell] = late[f, start : start + s.row]
        wait_all(normed_copies)
        for n in range(s.hidden // step):
            columns = slice(n * step, (n + 1) * step)
            second = slice(s.hidden + n * step, s.hidden + (n + 1) * step)
            gate = dot(normed[...], weight[:, columns])
            up = dot(normed[...], weight[:, second])
            sigma = jax.nn.sigmoid(gate)
            active = gate * sigma
            hidden[:, columns] = (active * up).astype(BF)
            grad = grad_hidden[:, columns]
            grads[:, columns] = (grad * up * (sigma * (1.0 + gate * (1.0 - sigma)))).astype(BF)
            grads[:, second] = (grad * active).astype(BF)
        hidden.send()
        grads.send()
        for target, core in ((far, 1), (near, 0)):
            for n in range(s.width // step):
                columns = slice(n * step, (n + 1) * step)
                for group in range(2):
                    rows = pl.ds(group * s.group + core * s.half, s.half)
                    part = dot_last(grads[rows], weight[columns])
                    target[pl.ds(group * s.half, s.half), columns] = part.astype(BF)
            target.send()

    return body


def mlp_weight_grads(s):
    step = 4 * s.row * 4

    def body(*refs):
        normed_blocks, blocks = refs[:8], refs[8:16]
        grads, hidden, target, normed, upstream, made, normed_sems, sems, out_sems = refs[16:]
        normed_copies = gather_into(s, normed_blocks, normed, normed_sems)
        copies = gather_into(s, blocks, upstream, sems)
        leaving = []
        grads.start()
        hidden.start()
        wait_all(normed_copies)
        for z in range(4):
            for xl in range(2):
                at = (z * 2 + xl) * step
                tile = dot_first(normed[:, at : at + step], grads[...]).astype(BF)
                for y in range(4):
                    for part in range(4):
                        line = (y * 4 + part) * s.row
                        for p in range(s.mlp_parts):
                            start = (xl * 4 + part) * s.mlp_rows + p * s.row
                            made[z * 4 + y, start : start + s.row] = tile[
                                line : line + s.row, p * s.cell : (p + 1) * s.cell
                            ]
            if z % 2:
                pair = z // 2
                if pair == 0:
                    wait_all(copies)
                wide = s.hidden // 2
                columns = hidden[:, pair * wide : (pair + 1) * wide]
                for p in range(s.out_parts):
                    tile = dot_first(columns, upstream[:, p * s.cell : (p + 1) * s.cell]).astype(BF)
                    for f in range(8):
                        start = SHARE * s.mlp_rows + p * s.down_row
                        made[pair * 8 + f, start : start + s.down_row] = tile[f * s.down_row : (f + 1) * s.down_row]
                half = pl.ds(pair * 8, 8)
                copy = pltpu.make_async_copy(made.at[half], target.at[half], out_sems.at[pair])
                copy.start()
                leaving.append(copy)
        for copy in leaving:
            copy.wait()

    return body


def mlp_out(s):
    step = 4 * HEAD_SIZE

    def body(hidden, down, near, far):
        for target, core in ((far, 1), (near, 0)):
            for group in range(2):
                rows = pl.ds(group * s.group + core * s.half, s.half)
                for n in range(s.width // step):
                    columns = slice(n * step, (n + 1) * step)
                    target[pl.ds(group * s.half, s.half), columns] = dot(hidden[rows], down[:, columns]).astype(BF)

    return body


def mlp_back_end(s):
    def body(own, first, second, third, cotangent, hidden_two, gain_two, grad_hidden_two, low, terms):
        grad = total_of(own, (first, second, third))
        back, gains = norm_back(hidden_two[...], gain_two[...], grad)
        value = cotangent[...].astype(F32) + back
        grad_hidden_two[...] = value
        low[...] = value.astype(BF)
        terms[...] = jnp.sum(gains, axis=0, keepdims=True)

    return body


def out_weight_grads(s):
    def body(*refs):
        mixed, out_grad, branch, sems = refs[8:]
        wait_all(gather_into(s, refs[:8], branch, sems))
        for p in range(s.out_parts):
            columns = slice(p * s.cell, (p + 1) * s.cell)
            out_grad[:, columns] = dot_first(mixed[...], branch[:, columns]).astype(BF)

    return body


def head_back(s):
    scale = HEAD_SIZE ** (-0.5)

    def body(*refs):
        blocks = refs[:8]
        out_weight, probs, linear, cosine, sine, query, key, value, normed, weight = refs[8:18]
        gain_query, gain_key, gain_one, gain_two_terms, owner, lane = refs[18:24]
        near, far, owned_rows, branch, grad_mixed, grads, gain_row, sems = refs[24:]
        copies = gather_into(s, blocks, branch, sems)
        for later in (out_weight, probs, linear, cosine, sine, query, key, value, normed, weight):
            later.start()
        q, h = s.query, HEAD_SIZE
        query_sum = jnp.zeros((1, h), F32)
        key_sum = jnp.zeros((1, h), F32)
        for group in range(2):
            rows = pl.ds(group * s.group, s.group)
            for at in range(group * 4, group * 4 + 4):
                copies[at].wait()
            grad_mixed[rows] = dot_last(branch[rows], out_weight[...]).astype(BF)
            cos, sin = cosine[rows], sine[rows]
            key_grad = jnp.zeros((s.group, h), F32)
            value_grad = jnp.zeros((s.group, h), F32)
            for r in range(s.heads):
                columns = slice(r * h, (r + 1) * h)
                prob = probs[group * s.heads + r]
                out = grad_mixed[rows, columns]
                grad_prob = dot_last(out, value[rows])
                inner = jnp.sum(prob * grad_prob, axis=-1, keepdims=True)
                grad_score = (prob * (grad_prob - inner)).astype(BF)
                value_grad = value_grad + dot_first(prob.astype(BF), out)
                key_grad = key_grad + dot_first(grad_score, query[rows, columns]) * scale
                turned = dot(grad_score, key[rows]) * scale
                back, terms = norm_back(
                    linear[rows, columns], gain_query[...], turned * cos - turn(turned) * sin
                )
                grads[rows, columns] = back.astype(BF)
                query_sum = query_sum + jnp.sum(terms, axis=0, keepdims=True)
            back, terms = norm_back(
                linear[rows, q : q + h], gain_key[...], key_grad * cos - turn(key_grad) * sin
            )
            grads[rows, q : q + h] = back.astype(BF)
            key_sum = key_sum + jnp.sum(terms, axis=0, keepdims=True)
            grads[rows, q + h :] = value_grad.astype(BF)
        wide = 4 * HEAD_SIZE
        for n in range(s.width // wide):
            columns = slice(n * wide, (n + 1) * wide)
            total = jnp.zeros((1, wide), F32)
            for target, core in ((far, 1), (near, 0)):
                for group in range(2):
                    rows = pl.ds(group * s.group + core * s.half, s.half)
                    part = dot_last(grads[rows], weight[columns])
                    target[pl.ds(group * s.half, s.half), columns] = part.astype(BF)
                    total = total + jnp.sum(part * normed[rows, columns].astype(F32), axis=0, keepdims=True)
            gain_row[:, columns] = total / gain_one[:, columns]
        far.send()
        near.send()
        gain_row[:, s.width : 2 * s.width] = gain_two_terms[...]
        gain_row[:, 2 * s.width : 2 * s.width + h] = query_sum
        gain_row[:, 2 * s.width + h :] = key_sum
        owned = dot((owner[...].astype(F32) * gain_row[...]).astype(BF), lane[...])
        for o in range(128):
            owned_rows[o, :, s.cell :] = jnp.broadcast_to(owned[o : o + 1], (s.row, h)).astype(BF)
        step = 16 * s.row
        for n in range(8):
            tile = dot_first(normed[:, n * step : (n + 1) * step], grads[...]).astype(BF)
            owned_rows[n * 16 : (n + 1) * 16, :, : s.cell] = tile.reshape(16, s.row, s.cell)

    return body


def plane_sum(s):
    def body(parts, total):
        value = parts[0].astype(F32)
        for f in range(1, 16):
            value = value + parts[f].astype(F32)
        total[...] = value.astype(BF)

    return body


def input_end(s):
    def body(own, first, second, third, tokens, grad_hidden_two, gain_one, input_grad):
        back, _ = norm_back(tokens[...].astype(F32), gain_one[...], total_of(own, (first, second, third)))
        input_grad[...] = grad_hidden_two[...] + back

    return body


def output_end(s):
    def body(own, first, second, third, hidden_two, block_output):
        block_output[...] = (hidden_two[...] + total_of(own, (first, second, third))).astype(BF)

    return body


def adam(weight, grad, first, second, rate, decay):
    first_new = BETA_ONE * first + (1.0 - BETA_ONE) * grad
    second_new = BETA_TWO * second + (1.0 - BETA_TWO) * grad * grad
    first_hat = first_new / (1.0 - BETA_ONE**STEP)
    second_hat = second_new / (1.0 - BETA_TWO**STEP)
    weight_new = weight - rate * (first_hat / (jnp.sqrt(second_hat) + ADAM_EPS) + decay * weight)
    return (weight_new, first_new, second_new)


def step_into(ins, outs, columns, grad, rate, decay):
    results = adam(ins[0][:, columns], grad.astype(F32), ins[1][:, columns], ins[2][:, columns], rate, decay)
    for out, value in zip(outs, results):
        out[:, columns] = value


def split_refs(refs, first, count):
    ins = [refs[first + 3 * i : first + 3 * i + 3] for i in range(count)]
    outs = [refs[first + 3 * (count + i) : first + 3 * (count + i) + 3] for i in range(count)]
    return ins, outs


def send_all(outs):
    for out in outs:
        out.send()


def head_update(s):
    def body(*refs):
        owned, lines = refs[:2]
        ins, outs = split_refs(refs, 2, 5)
        rate = MODEL_WIDTH ** (-0.5)
        out_rate = (TOK_DEV / (QUERY_HEADS * HEAD_SIZE)) ** 0.5
        gain_grad = jnp.zeros((s.row, HEAD_SIZE), F32)
        for j in range(SHARE):
            xl, part = divmod(j, 4)
            grad = jnp.zeros((s.row, s.cell), F32)
            for z in range(4):
                for y in range(4):
                    source = ((z * 2 + xl) * 4 + y) * 4 + part
                    grad = grad + owned[source, :, : s.cell].astype(F32)
                    gain_grad = gain_grad + owned[source, :, s.cell :].astype(F32)
            start = 0
            for i, size in enumerate((s.query, HEAD_SIZE, HEAD_SIZE)):
                columns = slice(j * size, (j + 1) * size)
                step_into(ins[i], outs[i], columns, grad[:, start : start + size], rate, DECAY)
                start += size
        for i in range(3):
            send_all(outs[i])
        for p in range(s.out_parts):
            columns = slice(p * s.cell, (p + 1) * s.cell)
            step_into(ins[3], outs[3], columns, lines[:, columns], out_rate, DECAY)
        send_all(outs[3])
        step_into(ins[4], outs[4], slice(0, s.gains), gain_grad[:1, : s.gains], 0.5, 0.0)

    return body


def mlp_update(s):
    def body(*refs):
        columns, lines = refs[:2]
        ins, outs = split_refs(refs, 2, 3)
        for i, start in ((0, 0), (1, s.hidden)):
            for j in range(SHARE):
                done = 0
                while done < s.hidden:
                    at = start + done
                    part, inside = at // s.cell, at % s.cell
                    size = min(s.cell - inside, s.hidden - done)
                    grad = columns[j, part * s.row : (part + 1) * s.row, inside : inside + size]
                    own = slice(j * s.hidden + done, j * s.hidden + done + size)
                    step_into(ins[i], outs[i], own, grad, MODEL_WIDTH ** (-0.5), DECAY)
                    done += size
            send_all(outs[i])
        for p in range(s.out_parts):
            grad = lines[p * s.down_row : (p + 1) * s.down_row]
            step_into(ins[2], outs[2], slice(p * s.cell, (p + 1) * s.cell), grad, FF ** (-0.5), DECAY)

    return body


def layout(table, other):
    span = TOK_DEV // 2
    both = jnp.stack([table, other])
    sizes, spans = both[:, :2], both[:, 2:]
    chip = lax.axis_index("xh") * 2 + lax.axis_index("xl")
    core = lax.axis_index("c")
    offset = jnp.arange(2)[:, None, None] + 2 * jnp.arange(2)[None, None, :]
    place = ((chip + offset) % 4) // 2 * 2 + (core + jnp.arange(2)[None, :, None]) % 2
    block = (2 * place[..., None] + jnp.arange(2)).reshape(2, 8)
    owner = jnp.sum(jnp.where(block[:, :, None] == jnp.arange(8), spans[:, None, :], 0), axis=-1)
    slots = (owner[:, :, None] * span + jnp.arange(span)).reshape(2, -1)
    ends = jnp.cumsum(sizes, axis=1)
    passed = slots[:, :, None] >= ends[:, None, :]
    sequence = jnp.sum(passed.astype(jnp.int32), axis=-1)
    position = slots - jnp.sum(jnp.where(passed, sizes[:, None, :], 0), axis=-1)
    return slots, sequence, position


def local(
    tokens,
    cotangent,
    lengths,
    span_ids,
    query_weight,
    key_matrix,
    value_matrix,
    out_weight,
    gate_weight,
    up_weight,
    down_weight,
    norm_gains,
    query_first,
    key_first_moment,
    value_first_moment,
    out_first,
    gate_first,
    up_first,
    down_first,
    gains_first,
    query_second,
    key_second_moment,
    value_second_moment,
    out_second,
    gate_second,
    up_second,
    down_second,
    gains_second,
):
    s = Sizes()
    block = (s.block, s.width)
    half_rows = (s.group, s.width)

    def ring_scatter(near, arrived, name, after=()):
        own, *others = call(
            ring_add(s), [shape(block, F32)] + [shape(block)] * 3, [near, arrived], after=after, name=name + "_add"
        )
        arrived = [from_chip(piece, -OFFSETS[i + 1]) for i, piece in enumerate(others)]
        return [own] + arrived, others

    columns, lines, mark = call(
        pack_weights(s),
        [shape((SHARE, 2 * s.row + s.mlp_rows, s.cell)), shape((s.out_rows + s.down_rows, s.cell))],
        [Far(query_weight), Far(key_matrix), Far(value_matrix), Far(out_weight), Far(gate_weight), Far(up_weight)]
        + [Far(down_weight), norm_gains[None]],
        large=54,
        mark=True,
        name="pack_weights",
    )
    (table,) = tie([jnp.concatenate([lengths[0], span_ids[0]])], [mark], "table_then")
    other_table = lax.ppermute(table, "xl", [(0, 1), (1, 0)])
    (tokens_then,) = tie([tokens], [mark], "tokens_then", HBM)
    input_near = from_chips(tokens_then)
    inputs = with_cores(input_near)
    columns = lax.all_to_all(columns, RING, 0, 0, tiled=True)
    lines = lax.ppermute(lines, AXES, row_route())

    count = 128 * s.gains
    owner = np.asarray(np.arange(count)[None] // s.gains == np.arange(128)[:, None], ml_dtypes.bfloat16)
    lane = np.asarray(np.arange(count)[:, None] % s.gains == np.arange(HEAD_SIZE)[None], ml_dtypes.bfloat16)

    early, late = call(
        place_weights(s),
        [shape((s.early, s.cell)), shape((s.late, s.cell))],
        [columns, lines],
        after=[other_table],
        scratch=[pltpu.VMEM((s.row, s.cell), F32)],
        name="place_weights",
    )
    early = lax.all_gather(early, PLANE, axis=0)
    (cotangent_then,) = tie([cotangent], [tokens_then], "cotangent_then", HBM)
    upstream_near = from_chips(cotangent_then)
    slots, sequence, position = layout(table, other_table)
    freq = THETA ** (-(2.0 * jnp.arange(HEAD_SIZE // 2, dtype=F32)) / HEAD_SIZE)
    angle = position.reshape(-1).astype(F32)[:, None] * freq
    cosine, sine = jnp.cos(angle), jnp.sin(angle)
    cosine = jnp.concatenate([cosine, cosine], axis=1)
    sine = jnp.concatenate([-sine, sine], axis=1)
    allowed = (sequence[:, :, None] == sequence[:, None, :]) & (slots[:, None, :] <= slots[:, :, None])
    bias = jnp.where(allowed, 0.0, -1e30).astype(F32)

    (late,) = tie(
        [late], [*inputs[1:], *upstream_near[1:], cosine, sine, bias], "late_then", HBM
    )
    late = lax.all_gather(late, PLANE, axis=0)
    upstream = with_cores(upstream_near)

    gain_at = s.ring_rows + s.out_rows
    gains = early[:, gain_at : gain_at + SHARE, : s.gains].astype(F32)
    gains = gains.reshape(4, 4, 2, -1).transpose(0, 2, 1, 3).reshape(1, -1)
    gain_one = gains[:, : s.width]
    gain_two = gains[:, s.width : 2 * s.width]
    gain_query = gains[:, 2 * s.width : 2 * s.width + HEAD_SIZE]
    gain_key = gains[:, 2 * s.width + HEAD_SIZE :]

    eight = pltpu.SemaphoreType.DMA((8,))
    head_weight, out_slice, normed_one, linear, probs, query, key, value, mixed, near, far = call(
        head_forward(s),
        [
            Far(shape((s.width, s.cell))),
            Far(shape((s.query, s.width))),
            Far(shape((s.rows, s.width))),
            Far(shape((s.rows, s.query + HEAD_SIZE), F32)),
            Far(shape((2 * s.heads, s.group, s.group), F32)),
            shape((s.rows, s.query)),
            shape((s.rows, HEAD_SIZE)),
            shape((s.rows, HEAD_SIZE)),
            shape((s.rows, s.query)),
            shape(half_rows),
            Far(shape(half_rows)),
        ],
        [*[Far(v) for v in inputs], Far(early), Far(cosine), Far(sine), Far(bias), gain_one, gain_query, gain_key],
        flops=2 * s.rows * s.width * (s.cell + s.query),
        large=54,
        name="head_forward",
    )
    parts, _ = ring_scatter(near, from_core(far), "branch")
    hidden_two, normed_two = call(
        branch_end(s), [shape(block, F32), shape(block)], [*parts, tokens, gain_two], name="branch_end"
    )
    normed_blocks = with_cores(from_chips(normed_two))
    down, hidden, grads, far, near = call(
        mlp_block(s),
        [
            Far(shape((s.hidden, s.width))),
            Far(shape((s.rows, s.hidden))),
            Far(shape((s.rows, 2 * s.hidden))),
            Far(shape(half_rows)),
            Far(shape(half_rows)),
        ],
        [*normed_blocks, *upstream, late],
        any_first=17,
        near=(0,),
        scratch=[
            pltpu.VMEM((s.rows, s.width), BF),
            pltpu.VMEM((s.rows, s.width), BF),
            pltpu.VMEM((s.width, 2 * s.hidden), BF),
            pltpu.VMEM((s.rows, s.hidden), F32),
            pltpu.VMEM((16, s.late, s.cell), BF),
            eight,
            eight,
            pltpu.SemaphoreType.DMA((2,)),
        ],
        flops=10 * s.rows * s.width * s.hidden,
        large=60,
        name="mlp_block",
    )
    parts, sent = ring_scatter(near, from_core(far), "mlp_back")
    late_grad, mark = call(
        mlp_weight_grads(s),
        [shape((16, s.late, s.cell))],
        [*normed_blocks, *upstream, Far(grads, later=True), Far(hidden, later=True)],
        any_first=16,
        near=(0,),
        any_out=True,
        after=sent,
        scratch=[
            pltpu.VMEM((s.rows, s.width), BF),
            pltpu.VMEM((s.rows, s.width), BF),
            pltpu.VMEM((16, s.late, s.cell), BF),
            eight,
            eight,
            pltpu.SemaphoreType.DMA((2,)),
        ],
        flops=6 * s.rows * s.width * s.hidden,
        large=54,
        mark=True,
        name="mlp_weight_grads",
    )
    grad_hidden_two, grad_branch, gain_two_terms = call(
        mlp_back_end(s),
        [shape(block, F32), shape(block), shape((1, s.width), F32)],
        [*parts, cotangent, hidden_two, gain_two],
        after=[mark],
        name="mlp_back_end",
    )
    (late_grad,) = tie([late_grad], [grad_branch], "late_grad_then", HBM)
    late_grad = lax.psum_scatter(late_grad.reshape(-1, s.cell), PLANE, scatter_dimension=0, tiled=True)
    branch_near = from_chips(grad_branch)
    out_near, out_far = call(
        mlp_out(s),
        [shape(half_rows)] * 2,
        [Far(hidden), Far(down)],
        after=[grad_branch],
        flops=2 * s.rows * s.width * s.hidden,
        large=54,
        name="mlp_out",
    )
    out_far, *branch_near[1:] = tie([out_far, *branch_near[1:]], [], "branch_then")
    branch_blocks = with_cores(branch_near)
    output_parts, out_sent = ring_scatter(out_near, from_core(out_far), "output")

    moved = (out_slice, probs, linear, cosine, sine, query, key, value, normed_one, head_weight)
    (out_grad,) = call(
        out_weight_grads(s),
        [Far(shape((s.query, s.width)))],
        [*branch_blocks, Far(mixed)],
        any_first=8,
        near=(0,),
        scratch=[pltpu.VMEM((s.rows, s.width), BF), eight],
        flops=2 * s.rows * s.width * s.query,
        large=54,
        name="out_weight_grads",
    )
    out_parts = lax.all_to_all(out_grad.reshape(16, s.row, s.width), PLANE, 0, 0, tiled=True)
    near, far, owned, mark = call(
        head_back(s),
        [
            Far(shape(half_rows)),
            Far(shape(half_rows)),
            Far(shape((128, s.row, s.cell + HEAD_SIZE))),
        ],
        [*branch_blocks, *[Far(v, later=True) for v in moved]]
        + [gain_query, gain_key, gain_one, gain_two_terms, owner, lane],
        any_first=8,
        near=(0,),
        after=out_sent,
        scratch=[
            pltpu.VMEM((s.rows, s.width), BF),
            pltpu.VMEM((s.rows, s.query), BF),
            pltpu.VMEM((s.rows, s.cell), BF),
            pltpu.VMEM((1, count), F32),
            eight,
        ],
        hidden=True,
        large=54,
        mark=True,
        name="head_back",
    )
    (block_output,) = call(output_end(s), [shape(block)], [*output_parts, hidden_two], name="output_end")
    (out_lines,) = call(plane_sum(s), [shape((s.row, s.width))], [out_parts], after=[mark], name="plane_sum")
    owned, far = tie([owned, far], [block_output, out_lines], "head_grads_then")
    owned = lax.all_to_all(owned, AXES, 0, 0, tiled=True)
    parts, sent = ring_scatter(near, from_core(far), "input")
    (late_grad,) = tie([late_grad], sent[:1], "late_grad_last")
    input_grad, input_mark = call(
        input_end(s), [shape(block, F32)], [*parts, tokens, grad_hidden_two, gain_one], mark=True, name="input_end"
    )

    home = [(to, own) for own, to in row_route()]
    mlp_end = SHARE * s.mlp_rows
    columns = lax.all_to_all(late_grad[:mlp_end].reshape(SHARE, s.mlp_rows, s.cell), RING, 0, 0, tiled=True)
    lines = lax.ppermute(late_grad[mlp_end:], AXES, home)
    out_lines = lax.ppermute(out_lines, AXES, home)

    def states(*groups):
        return [Far(a) for group in groups for a in group]

    mlp_states = states(
        (gate_weight, gate_first, gate_second),
        (up_weight, up_first, up_second),
        (down_weight, down_first, down_second),
    )
    mlp_new = call(
        mlp_update(s),
        [Far(shape(a.value.shape, F32)) for a in mlp_states],
        [columns, lines] + mlp_states,
        after=[Far(owned), input_mark],
        mark=True,
        large=62,
        name="mlp_update",
    )
    head_states = states(
        (query_weight, query_first, query_second),
        (key_matrix, key_first_moment, key_second_moment),
        (value_matrix, value_first_moment, value_second_moment),
        (out_weight, out_first, out_second),
    )
    gains_state = [a[None] for a in (norm_gains, gains_first, gains_second)]
    head_new = call(
        head_update(s),
        [Far(shape(a.value.shape, F32)) for a in head_states] + [shape(a.shape, F32) for a in gains_state],
        [owned, out_lines] + head_states + gains_state,
        after=[mlp_new[-1]],
        large=62,
        name="head_update",
    )
    return (block_output, input_grad, *head_new[:12], *mlp_new[:9], *[value[0] for value in head_new[12:]])


def solution(mesh):
    fine = Mesh(mesh.devices.reshape(SIZES), AXES)
    matrix, vector, grouped = P(AXES, None), P(AXES), P(("z", "xl", "y"), None)
    states = (matrix,) * 7 + (vector,)
    return jax.shard_map(
        local,
        mesh=fine,
        in_specs=(matrix, matrix, grouped, grouped) + states * 3,
        out_specs=(matrix, matrix) + (matrix,) * 21 + (vector,) * 3,
        check_vma=False,
    )
```
